32 devices in a mesh: dp: 16 (over z, x, core), tensor: 2 (over y).
Axes of the slice: x: 2, y: 2, z: 4, core: 2. Of those that a mesh axis runs over, the one named last changes fastest.
Arguments:
- tokens: bfloat16 [8192, 2048], P('dp'), may hold values from -6 to 6
- seq_lengths: int32 [16, 4], P('dp'), may hold values from 0 to 512, as said below
- first_gain: bfloat16 [2048], replicated, may hold values from 0.099609375 to 1.8984375
- query_weight: bfloat16 [2048, 2048], P('dp', 'tensor'), may hold values from -0.125 to 0.125
- key_matrix: bfloat16 [2048, 1024], P('dp', 'tensor'), may hold values from -0.125 to 0.125
- value_matrix: bfloat16 [2048, 1024], P('dp', 'tensor'), may hold values from -0.125 to 0.125
- query_norm_gain: bfloat16 [128], replicated, may hold values from 0.099609375 to 1.8984375
- key_gain: bfloat16 [128], replicated, may hold values from 0.099609375 to 1.8984375
- output_weight: bfloat16 [2048, 2048], P('tensor', 'dp'), may hold values from -1 to 1
- second_gain: bfloat16 [2048], replicated, may hold values from 0.099609375 to 1.8984375
- gate_weight: bfloat16 [2048, 6144], P('dp', 'tensor'), may hold values from -0.125 to 0.125
- up_weight: bfloat16 [2048, 6144], P('dp', 'tensor'), may hold values from -0.125 to 0.125
- down_weight: bfloat16 [6144, 2048], P('tensor', 'dp'), may hold values from -0.078125 to 0.078125
- cotangent: bfloat16 [8192, 2048], P('dp'), may hold values from -6 to 6
Outputs:
- block_output: bfloat16 [8192, 2048], P('dp')
- token_grad: float32 [8192, 2048], P('dp')
- first_gain_grad: float32 [2048], P('dp')
- query_weight_grad: float32 [2048, 2048], P('dp', 'tensor')
- key_weight_grad: float32 [2048, 1024], P('dp', 'tensor')
- value_weight_grad: float32 [2048, 1024], P('dp', 'tensor')
- query_gain_grad: float32 [128], P('dp')
- key_gain_grad: float32 [128], P('dp')
- output_weight_grad: float32 [2048, 2048], P('tensor', 'dp')
- second_gain_grad: float32 [2048], P('dp')
- gate_weight_grad: float32 [2048, 6144], P('dp', 'tensor')
- up_weight_grad: float32 [2048, 6144], P('dp', 'tensor')
- down_weight_grad: float32 [6144, 2048], P('tensor', 'dp')
The draws below stay inside these ranges and needn't reach their ends.
Inputs may be any that keep to these rules, and one draw needn't show every extreme that they name: `seq_lengths`: row g lists the lengths of the sequences of data group g in slot order; a zero is an empty slot. Padded to multiples of 64, the sequences of a group fit in 512 rows. In every draw some group holds a single sequence of 512 tokens.
All inputs are finite; a program needn't handle non-finite values.
Results may differ from the reference program's by a relative error of at most 0.014.
Values may be sent and summed in bfloat16 or wider, within the bound.
No kernel may reach another device: no remote copies, remote signals or barrier semaphores. Data moves between devices by JAX's collectives and lax.ppermute only.
A program may use at most 256 MiB of HBM per device.

```python
import jax
import jax.numpy as jnp
from jax import lax

MODEL_WIDTH = 2048
QUERY_HEADS_TOTAL = 16
KEY_VALUE_HEADS = 8
HEAD_SIZE = 128
FF = 6144
ROWS = 512
BLK = 64
SEQS = 4
GROUPS = 16
TOKENS = 8192


def draw_seq_lengths(key, part):
    key = jax.random.fold_in(key, 11)
    key_total, key_cuts, key_trim, key_full = jax.random.split(key, 4)
    blocks_all = ROWS // BLK
    blocks_used = jax.random.randint(key_total, (GROUPS, 1), blocks_all // 2, blocks_all + 1).astype(jnp.int32)
    cut_points = jax.random.randint(key_cuts, (GROUPS, SEQS - 1), 0, blocks_all + 1).astype(jnp.int32)
    cut_points = jnp.sort(jnp.minimum(cut_points, blocks_used), axis=1)
    bounds = jnp.concatenate([jnp.zeros((GROUPS, 1), jnp.int32), cut_points, blocks_used], axis=1)
    block_counts = bounds[:, 1:] - bounds[:, :-1]
    shortfall = jax.random.randint(key_trim, (GROUPS, SEQS), 0, BLK).astype(jnp.int32)
    lengths = jnp.where(block_counts > 0, block_counts * BLK - shortfall, 0)
    chosen = jax.random.randint(key_full, (), 0, GROUPS)
    single_row = jnp.where(jnp.arange(SEQS) == 0, ROWS, 0)
    lengths = jnp.where((jnp.arange(GROUPS) == chosen)[:, None], single_row[None, :], lengths)
    return lengths.astype(jnp.int32)


def block_scale(stream_key, extent, pieces, low, top_value):
    factor_of = 1.0
    for dim, parts in pieces:
        draws = jax.random.uniform(jax.random.fold_in(jax.random.fold_in(stream_key, 6), dim), (parts,), jnp.float32, low / len(pieces), top_value / len(pieces))
        factor_of = factor_of * jnp.repeat(jnp.exp(draws), extent[dim] // parts).reshape((-1,) + (1,) * (len(extent) - 1 - dim))
    return factor_of


def centred(rng, shape, spread, limit, pieces=(), kind=jnp.bfloat16):
    values = spread * jax.random.normal(rng, shape, jnp.float32)
    if pieces:
        values = values * block_scale(rng, shape, pieces, -0.22, 0.18)
    return jnp.clip(values, -limit, limit).astype(kind)


def setup_inputs(seed: int = 0) -> dict:
    arg_keys = jax.random.split(jax.random.key(seed), 15)
    return {
        "tokens": centred(arg_keys[0], (TOKENS, MODEL_WIDTH), 1.0, 6.0, ((0, 16),)),
        "seq_lengths": draw_seq_lengths(jax.random.fold_in(arg_keys[14], 71), 0),
        "first_gain": jnp.clip(1.0 + 0.18 * jax.random.normal(arg_keys[2], (MODEL_WIDTH,), jnp.float32), 0.099609375, 1.8984375).astype(jnp.bfloat16),
        "query_weight": centred(arg_keys[3], (MODEL_WIDTH, QUERY_HEADS_TOTAL * HEAD_SIZE), MODEL_WIDTH ** -0.5, 0.125, ((0, 16), (1, 2))),
        "key_matrix": centred(arg_keys[4], (MODEL_WIDTH, KEY_VALUE_HEADS * HEAD_SIZE), MODEL_WIDTH ** -0.5, 0.125, ((0, 16), (1, 2))),
        "value_matrix": centred(arg_keys[5], (MODEL_WIDTH, KEY_VALUE_HEADS * HEAD_SIZE), MODEL_WIDTH ** -0.5, 0.125, ((0, 16), (1, 2))),
        "query_norm_gain": jnp.clip(1.0 + 0.18 * jax.random.normal(arg_keys[6], (HEAD_SIZE,), jnp.float32), 0.099609375, 1.8984375).astype(jnp.bfloat16),
        "key_gain": jnp.clip(1.0 + 0.18 * jax.random.normal(arg_keys[7], (HEAD_SIZE,), jnp.float32), 0.099609375, 1.8984375).astype(jnp.bfloat16),
        "output_weight": centred(arg_keys[8], (QUERY_HEADS_TOTAL * HEAD_SIZE, MODEL_WIDTH), (QUERY_HEADS_TOTAL * HEAD_SIZE // 64) ** -0.5, 1.0, ((0, 2), (1, 16))),
        "second_gain": jnp.clip(1.0 + 0.18 * jax.random.normal(arg_keys[9], (MODEL_WIDTH,), jnp.float32), 0.099609375, 1.8984375).astype(jnp.bfloat16),
        "gate_weight": centred(arg_keys[10], (MODEL_WIDTH, FF), MODEL_WIDTH ** -0.5, 0.125, ((0, 16), (1, 2))),
        "up_weight": centred(arg_keys[11], (MODEL_WIDTH, FF), MODEL_WIDTH ** -0.5, 0.125, ((0, 16), (1, 2))),
        "down_weight": centred(arg_keys[12], (FF, MODEL_WIDTH), FF ** -0.5, 0.078125, ((0, 2), (1, 16))),
        "cotangent": centred(arg_keys[13], (TOKENS, MODEL_WIDTH), 1.0, 6.0, ((0, 16),)),
    }


@jax.custom_vjp
def reduced_precision(v):
    return lax.optimization_barrier(v.astype(jnp.bfloat16)).astype(jnp.float32)

@jax.custom_vjp
def reduced_precision_grad(v):
    return v

def low_keep(v):
    return (reduced_precision(v), None)

def low_pass(kept, grad):
    return (grad,)

def back_keep(v):
    return (v, None)

def back_low(kept, grad):
    return (reduced_precision(grad),)
reduced_precision.defvjp(low_keep, low_pass)
reduced_precision_grad.defvjp(back_keep, back_low)
epsilon = 1e-06
rope_base = 1000000.0
highest = lax.Precision.HIGHEST

def matrix_product(left, right):
    return jnp.dot(left, right, precision=highest)

def rownorm_apply(inputs, gain_vector):
    return inputs * lax.rsqrt(lax.optimization_barrier(jnp.mean(inputs * inputs, axis=-1, keepdims=True)) + epsilon) * gain_vector

def layout(lengths, count_of_rows):
    lengths = lengths.astype(jnp.int32)
    padded = ((lengths + BLK - 1) // BLK * BLK).astype(jnp.int32)
    starts = (jnp.cumsum(padded) - padded).astype(jnp.int32)
    row_index = jnp.arange(count_of_rows, dtype=jnp.int32)
    inside = (row_index[:, None] >= starts[None, :]) & (row_index[:, None] < (starts + lengths)[None, :])
    live_rows = jnp.any(inside, axis=1)
    slot_index = jnp.arange(lengths.shape[0], dtype=jnp.int32)
    owning = lax.optimization_barrier(jnp.sum(jnp.where(inside, slot_index[None, :], 0), axis=1)).astype(jnp.int32)
    position = lax.optimization_barrier(jnp.sum(jnp.where(inside, row_index[:, None] - starts[None, :], 0), axis=1)).astype(jnp.int32)
    segment = jnp.where(live_rows, owning, -1 - row_index).astype(jnp.int32)
    return (live_rows, segment, position)

def rotation(position, width):
    half_width = width // 2
    frequency = jnp.power(rope_base, -(jnp.arange(half_width, dtype=jnp.float32) * 2.0) / width)
    angles = position.astype(jnp.float32)[:, None] * frequency[None, :]
    return (jnp.cos(angles)[:, None, :], jnp.sin(angles)[:, None, :])

def rotary_apply(inputs, cosine_table, sinusoid_table):
    half_width = inputs.shape[-1] // 2
    leading = inputs[..., :half_width]
    trailing = inputs[..., half_width:]
    return jnp.concatenate([leading * cosine_table - trailing * sinusoid_table, trailing * cosine_table + leading * sinusoid_table], axis=-1)

def forward(tokens, first_gain, query_weight, key_matrix, value_matrix, query_norm_gain, key_gain, output_weight, second_gain, gate_weight, up_weight, down_weight, segment, cosine_table, sinusoid_table):
    count_of_rows = tokens.shape[0]
    heads_per_group = QUERY_HEADS_TOTAL // KEY_VALUE_HEADS
    normalized_rows = reduced_precision(rownorm_apply(tokens, first_gain))
    query_rows = reduced_precision_grad(matrix_product(normalized_rows, query_weight)).reshape(count_of_rows, QUERY_HEADS_TOTAL, HEAD_SIZE)
    key_tile_rows = reduced_precision_grad(matrix_product(normalized_rows, key_matrix)).reshape(count_of_rows, KEY_VALUE_HEADS, HEAD_SIZE)
    value_tile_rows = reduced_precision(reduced_precision_grad(matrix_product(normalized_rows, value_matrix))).reshape(count_of_rows, KEY_VALUE_HEADS, HEAD_SIZE)
    query_rows = reduced_precision(rotary_apply(rownorm_apply(query_rows, query_norm_gain), cosine_table, sinusoid_table)).reshape(count_of_rows, KEY_VALUE_HEADS, heads_per_group, HEAD_SIZE)
    key_tile_rows = reduced_precision(rotary_apply(rownorm_apply(key_tile_rows, key_gain), cosine_table, sinusoid_table))
    scores = reduced_precision_grad(jnp.einsum('qhgd,khd->hgqk', query_rows, key_tile_rows, precision=highest) * HEAD_SIZE ** (-0.5))
    row_index = jnp.arange(count_of_rows, dtype=jnp.int32)
    allowed = (segment[:, None] == segment[None, :]) & (row_index[None, :] <= row_index[:, None])
    scores = jnp.where(allowed, scores, -1e+30)
    weights = jax.nn.softmax(scores, axis=-1)
    mixture = jnp.einsum('hgqk,khd->qhgd', reduced_precision(weights), value_tile_rows, precision=highest).reshape(count_of_rows, QUERY_HEADS_TOTAL * HEAD_SIZE)
    mixture = reduced_precision(reduced_precision_grad(mixture))
    branch = reduced_precision_grad(matrix_product(mixture, output_weight))
    middle = tokens + branch
    normed_two = reduced_precision(rownorm_apply(middle, second_gain))
    gate_value = reduced_precision_grad(matrix_product(normed_two, gate_weight))
    up_value = reduced_precision_grad(matrix_product(normed_two, up_weight))
    hidden = reduced_precision(jax.nn.silu(gate_value) * up_value)
    return middle + reduced_precision_grad(matrix_product(hidden, down_weight))

def reference(tokens, seq_lengths, first_gain, query_weight, key_matrix, value_matrix, query_norm_gain, key_gain, output_weight, second_gain, gate_weight, up_weight, down_weight, cotangent):
    float_weights = tuple((weight.astype(jnp.float32) for weight in (first_gain, query_weight, key_matrix, value_matrix, query_norm_gain, key_gain, output_weight, second_gain, gate_weight, up_weight, down_weight)))
    token_blocks = tokens.astype(jnp.float32).reshape(GROUPS, ROWS, MODEL_WIDTH)
    back_blocks = cotangent.astype(jnp.float32).reshape(GROUPS, ROWS, MODEL_WIDTH)

    def advance(totals, packet):
        token_block, back_block, lengths = packet
        live_rows, segment, position = layout(lengths, ROWS)
        cosine_table, sinusoid_table = rotation(position, HEAD_SIZE)

        def apply_layer(inputs, *weights):
            return forward(inputs, *weights, segment, cosine_table, sinusoid_table)
        result, pullback = jax.vjp(apply_layer, token_block, *float_weights)
        gradients = pullback(back_block * live_rows[:, None].astype(jnp.float32))
        totals = tuple((running + fresh for running, fresh in zip(totals, gradients[1:])))
        return (totals, (result.astype(jnp.bfloat16), gradients[0]))
    zero_grads = tuple((jnp.zeros_like(weight) for weight in float_weights))
    totals, (outputs, token_grads) = lax.scan(advance, zero_grads, (token_blocks, back_blocks, seq_lengths))
    grad_first, grad_query, grad_key, grad_value, grad_qgain, grad_kgain, grad_output, grad_second, grad_gate, grad_up, grad_down = totals
    return (outputs.reshape(TOKENS, MODEL_WIDTH), token_grads.reshape(TOKENS, MODEL_WIDTH), grad_first, grad_query, grad_key, grad_value, grad_qgain, grad_kgain, grad_output, grad_second, grad_gate, grad_up, grad_down)
```

```python
import functools

import jax
import jax.numpy as jnp
from jax import lax
from jax.experimental import pallas as pl
from jax.experimental.pallas import tpu as pltpu
from jax.sharding import PartitionSpec as P

HEAD_SIZE = 128
BLK = 64


epsilon = 1e-06
rope_base = 1000000.0


def matrix_product(left, right):
    return jnp.dot(left, right, preferred_element_type=jnp.float32)


def inner_left(left, right):
    return lax.dot_general(
        left, right, (((0,), (0,)), ((), ())), preferred_element_type=jnp.float32
    )


def inner_right(left, right):
    return lax.dot_general(
        left, right, (((1,), (1,)), ((), ())), preferred_element_type=jnp.float32
    )


def layout(lengths, count_of_rows):
    padded = (lengths + BLK - 1) // BLK * BLK
    starts = jnp.cumsum(padded) - padded
    row_index = jnp.arange(count_of_rows, dtype=jnp.int32)
    inside = (row_index[:, None] >= starts[None, :]) & (
        row_index[:, None] < (starts + lengths)[None, :]
    )
    live_rows = jnp.any(inside, axis=1)
    slot_index = jnp.arange(lengths.shape[0], dtype=jnp.int32)
    owning = jnp.sum(jnp.where(inside, slot_index[None, :], 0), axis=1)
    position = jnp.sum(jnp.where(inside, row_index[:, None] - starts[None, :], 0), axis=1)
    segment = jnp.where(live_rows, owning, -1 - row_index)
    return (live_rows, segment, position)


def rotation(position, width):
    half_width = width // 2
    frequency = jnp.power(rope_base, -(jnp.arange(half_width, dtype=jnp.float32) * 2.0) / width)
    angles = position.astype(jnp.float32)[:, None] * frequency[None, :]
    return (jnp.cos(angles)[:, None, :], jnp.sin(angles)[:, None, :])


CHUNKS = 3
PARTS = 4
LANES = 128
VMEM_LIMIT = 56 * 1024 * 1024


def add_low(left, right):
    return (left.astype(jnp.float32) + right.astype(jnp.float32)).astype(jnp.bfloat16)


class Ring:
    def __init__(self, size):
        self.size = size
        self.steps = size // 4
        index = lax.axis_index("dp")
        self.place = index // 4
        self.side = (index // 2) % 2
        self.core = index % 2
        self.places = [(self.place - 1 - i) % self.steps for i in range(self.steps)]
        self.groups = [
            [place * 4 + side * 2 + core for place in range(self.steps) for core in range(2)]
            for side in range(2)
        ]

    def swap_core(self, value):
        return lax.ppermute(value, "dp", [(i, i ^ 1) for i in range(self.size)])

    def swap_side(self, value):
        return lax.ppermute(value, "dp", [(i, i ^ 2) for i in range(self.size)])

    def shift(self, value, places):
        return lax.ppermute(
            value, "dp", [(i, (i + 4 * places) % self.size) for i in range(self.size)]
        )

    def pick(self, value, axis):
        low, high = jnp.split(value, 2, axis=axis)
        return (
            jnp.where(self.side == 0, low, high),
            jnp.where(self.side == 0, high, low),
        )

    def ordered(self, mine, other, axis):
        return jnp.where(
            self.side == 0,
            jnp.concatenate([mine, other], axis=axis),
            jnp.concatenate([other, mine], axis=axis),
        )

    def block(self, back, core, side):
        return ((self.place - back) % self.steps) * 4 + core * 2 + side

    def place_in(self, whole, back, core, side, value):
        start = (self.block(back, core, side), 0, 0)
        return lax.dynamic_update_slice(whole, value[None], start)


class Gather:
    def __init__(self, ring, piece):
        self.ring = ring
        self.current, self.across, self.index = piece, None, 0
        self.whole = jnp.zeros((ring.size,) + piece.shape, piece.dtype)

    def put(self, back, core, side, value):
        self.whole = self.ring.place_in(self.whole, back, core, side, value)

    def start(self):
        ring, moves = self.ring, {}
        if self.index < ring.steps:
            moves["side"] = ring.swap_side(self.current)
            moves["core"] = ring.swap_core(self.current)
            if self.index < ring.steps - 1:
                moves["hop"] = ring.shift(self.current, 1)
        if self.across is not None:
            moves["both"] = ring.swap_core(self.across)
        return moves

    def finish(self, moves):
        ring, back = self.ring, self.index
        core, side = ring.core, ring.side
        if "both" in moves:
            self.put(back - 1, 1 - core, 1 - side, moves["both"])
        self.across = None
        if "side" in moves:
            self.put(back, core, side, self.current)
            self.put(back, core, 1 - side, moves["side"])
            self.put(back, 1 - core, side, moves["core"])
            self.across, self.current = moves["side"], moves.get("hop")
        self.index += 1

    def result(self):
        return self.whole.reshape(-1, self.whole.shape[2])


class Scatter:
    def __init__(self, ring, mine, other):
        self.ring = ring
        count = mine.shape[0] // ring.steps
        self.mine = [mine[i * count : (i + 1) * count] for i in range(ring.steps)]
        self.other = [other[i * count : (i + 1) * count] for i in range(ring.steps)]
        self.term, self.index, self.total = None, 0, None

    def start(self):
        moves = {}
        if self.index < self.ring.steps:
            moves["side"] = self.ring.swap_side(self.other[self.index])
        if self.term is not None:
            moves["hop"] = self.ring.shift(self.term, 1)
        return moves

    def finish(self, moves):
        value = self.mine[self.index].astype(jnp.float32) + moves["side"].astype(jnp.float32)
        if "hop" in moves:
            value = value + moves["hop"].astype(jnp.float32)
        self.index += 1
        self.total = value
        self.term = value.astype(jnp.bfloat16) if self.index < self.ring.steps else None


def settle(*values):
    return lax.optimization_barrier(values)


def swap_tensor(value):
    return lax.ppermute(value, "tensor", [(0, 1), (1, 0)])


def arrange(value, steps, width):
    blocks = [value[:, i * width : (i + 1) * width] for i in range(4 * steps)]
    order = [4 * place + k for place in range(steps) for k in (0, 2, 1, 3)]
    return jnp.concatenate([blocks[i] for i in order], axis=1)


def arrange_vector(vector, steps):
    return vector.reshape(steps, 2, 2, -1).swapaxes(1, 2).reshape(-1)


def row_call(kernel, rows, block, ins, outs, sums=(), ties=()):
    in_specs = [
        pl.BlockSpec((block, a.shape[1]), lambda i: (i, 0))
        if kind == "rows"
        else pl.BlockSpec(a.shape, lambda i: (0, 0))
        for a, kind in ins
    ]
    out_specs = [pl.BlockSpec((block, c), lambda i: (i, 0)) for c, _ in outs]
    out_specs += [pl.BlockSpec((1, c), lambda i: (0, 0)) for c in sums]
    out_shape = [jax.ShapeDtypeStruct((rows, c), d) for c, d in outs]
    out_shape += [jax.ShapeDtypeStruct((1, c), jnp.float32) for c in sums]
    moved = sum(a.size * a.dtype.itemsize for a, _ in ins)
    moved += sum(rows * c * jnp.dtype(d).itemsize for c, d in outs)
    count = len(ins)

    def body(*refs):
        kernel(*refs[:count], *refs[count + len(ties) :])

    return pl.pallas_call(
        body,
        grid=(rows // block,),
        in_specs=in_specs + [pl.BlockSpec(memory_space=pl.ANY) for _ in ties],
        out_specs=out_specs,
        out_shape=out_shape,
        compiler_params=pltpu.CompilerParams(vmem_limit_bytes=VMEM_LIMIT),
        cost_estimate=pl.CostEstimate(flops=0, bytes_accessed=moved, transcendentals=0),
    )(*[a for a, _ in ins], *ties)


def inverse_rms(value):
    return lax.rsqrt(jnp.mean(value * value, axis=-1, keepdims=True) + epsilon)


def first_kernel(turn, tokens, cotangent, live, gain, tokens_out, upstream_out, normed_out):
    value = turn(tokens[...])
    tokens_out[...] = value
    value = value.astype(jnp.float32)
    normed_out[...] = (value * inverse_rms(value) * gain[...]).astype(jnp.bfloat16)
    back = turn(cotangent[...]).astype(jnp.float32)
    upstream_out[...] = (back * live[...]).astype(jnp.bfloat16)


def middle_kernel(tokens, mine, other, gain, middle_out, normed_out):
    branch = mine[...].astype(jnp.float32) + other[...].astype(jnp.float32)
    value = tokens[...].astype(jnp.float32) + branch
    middle_out[...] = value
    normed_out[...] = (value * inverse_rms(value) * gain[...]).astype(jnp.bfloat16)


def back_rms(value, gain, back):
    scale = inverse_rms(value)
    normed = value * scale
    pulled = back * gain
    center = jnp.mean(pulled * normed, axis=-1, keepdims=True)
    return scale * (pulled - normed * center), back * normed


def add_sum(out_ref, value):
    @pl.when(pl.program_id(0) == 0)
    def _():
        out_ref[...] = jnp.zeros_like(out_ref)

    out_ref[...] += jnp.sum(value, axis=0, keepdims=True)


def back_middle_kernel(mine, other, middle, upstream, gain, back_out, low_out, gain_out):
    back = mine[...].astype(jnp.float32) + other[...].astype(jnp.float32)
    value, gain_term = back_rms(middle[...], gain[...], back)
    value = value + upstream[...].astype(jnp.float32)
    back_out[...] = value
    low_out[...] = value.astype(jnp.bfloat16)
    add_sum(gain_out, gain_term)


def output_kernel(turn, middle, mine, other, out):
    value = middle[...] + mine[...].astype(jnp.float32) + other[...].astype(jnp.float32)
    out[...] = turn(value).astype(jnp.bfloat16)


def token_kernel(turn, mine, other, tokens, back_middle, gain, out):
    back = mine[...].astype(jnp.float32) + other[...].astype(jnp.float32)
    value, _ = back_rms(tokens[...].astype(jnp.float32), gain[...], back)
    out[...] = turn(value + back_middle[...])


def feed_kernel(chunk, normed, upstream, full, out):
    gate = matrix_product(normed[...], full[:, :chunk])
    up = matrix_product(normed[...], full[:, chunk : 2 * chunk])
    back = matrix_product(upstream[...], full[:, 2 * chunk :])
    share = jax.nn.sigmoid(gate)
    active = gate * share
    out[:, :chunk] = (back * up * (share * (1.0 + gate * (1.0 - share)))).astype(jnp.bfloat16)
    out[:, chunk : 2 * chunk] = (back * active).astype(jnp.bfloat16)
    out[:, 2 * chunk :] = (active * up).astype(jnp.bfloat16)


def feed_call(normed, upstream, full, ties=()):
    rows, model_width = normed.shape
    columns = full.shape[1]
    block = 256
    return pl.pallas_call(
        lambda a, b, c, *rest: feed_kernel(columns // 3, a, b, c, rest[-1]),
        grid=(rows // block,),
        in_specs=[
            pl.BlockSpec((block, model_width), lambda i: (i, 0)),
            pl.BlockSpec((block, model_width), lambda i: (i, 0)),
            pl.BlockSpec(full.shape, lambda i: (0, 0)),
        ]
        + [pl.BlockSpec(memory_space=pl.ANY) for _ in ties],
        out_specs=pl.BlockSpec((block, columns), lambda i: (i, 0)),
        out_shape=jax.ShapeDtypeStruct((rows, columns), jnp.bfloat16),
        compiler_params=pltpu.CompilerParams(vmem_limit_bytes=VMEM_LIMIT),
        cost_estimate=pl.CostEstimate(
            flops=2 * rows * model_width * columns,
            bytes_accessed=2 * (2 * normed.size + full.size + rows * columns),
            transcendentals=rows * columns // 3,
        ),
    )(normed, upstream, full, *ties)


def wide_kernel(count, started, *refs):
    out, total = refs[-1], None
    for act, full in zip(refs[:count], refs[count : 2 * count]):
        term = inner_right(act[...], full[...])
        total = term if total is None else total + term
    if started:
        total = total + refs[2 * count][...]
    out[...] = total.astype(out.dtype)


def wide_call(acts, fulls, span, out_dtype, start=None, ties=()):
    lo, hi = span
    size, index = hi - lo, lo // (hi - lo)
    rows, model_width, count = acts[0].shape[0], fulls[0].shape[0], len(acts)
    tile = 512
    ins = list(acts) + list(fulls)
    specs = [pl.BlockSpec((rows, size), lambda i: (0, index))] * count
    specs += [pl.BlockSpec((tile, size), lambda i: (i, index))] * count
    if start is not None:
        ins.append(start)
        specs.append(pl.BlockSpec((rows, tile), lambda i: (0, i)))
    ins += list(ties)
    specs += [pl.BlockSpec(memory_space=pl.ANY) for _ in ties]
    return pl.pallas_call(
        functools.partial(wide_kernel, count, start is not None),
        grid=(model_width // tile,),
        in_specs=specs,
        out_specs=pl.BlockSpec((rows, tile), lambda i: (0, i)),
        out_shape=jax.ShapeDtypeStruct((rows, model_width), out_dtype),
        compiler_params=pltpu.CompilerParams(vmem_limit_bytes=VMEM_LIMIT),
        cost_estimate=pl.CostEstimate(
            flops=2 * rows * model_width * size * count,
            bytes_accessed=2 * (rows + model_width) * size * count + rows * model_width * 6,
            transcendentals=0,
        ),
    )(*ins)


def grad_kernel(split, *refs):
    out = refs[-1]
    for columns, lefts in ((slice(0, split), refs[0:2]), (slice(split, None), refs[2:4])):
        total = 0.0
        for left, act in zip(lefts, refs[4:6]):
            total = total + inner_left(left[...], act[:, columns])
        out[:, columns] = total.astype(jnp.bfloat16)


def grad_call(normed, upstream, acts, ties=()):
    rows, model_width = normed[0].shape
    columns = acts[0].shape[1]
    tall = 512
    return pl.pallas_call(
        functools.partial(grad_kernel, columns // 3 * 2),
        grid=(model_width // tall,),
        in_specs=[pl.BlockSpec((rows, tall), lambda i: (0, i))] * 4
        + [pl.BlockSpec((rows, columns), lambda i: (0, 0))] * 2
        + [pl.BlockSpec(memory_space=pl.ANY) for _ in ties],
        out_specs=pl.BlockSpec((tall, columns), lambda i: (i, 0)),
        out_shape=jax.ShapeDtypeStruct((model_width, columns), jnp.bfloat16),
        compiler_params=pltpu.CompilerParams(vmem_limit_bytes=VMEM_LIMIT),
        cost_estimate=pl.CostEstimate(
            flops=4 * rows * model_width * columns,
            bytes_accessed=2 * (8 * rows * model_width + 4 * rows * columns + model_width * columns),
            transcendentals=0,
        ),
    )(*normed, *upstream, *acts, *ties)


def norm_rope(raw, gain, cosine, sine):
    scale = inverse_rms(raw)
    normed = raw * scale
    scaled = normed * gain
    return scaled * cosine + pltpu.roll(scaled, HEAD_SIZE // 2, 1) * sine, normed, scale


def back_norm_rope(back, normed, scale, gain, cosine, sine):
    back = back * cosine - pltpu.roll(back, HEAD_SIZE // 2, 1) * sine
    pulled = back * gain
    center = jnp.mean(pulled * normed, axis=-1, keepdims=True)
    return scale * (pulled - normed * center), back * normed


def softmax_rows(query, key, allowed):
    scores = jnp.where(allowed, inner_right(query, key) * HEAD_SIZE ** (-0.5), -1e30)
    raised = jnp.exp(scores - jnp.max(scores, axis=-1, keepdims=True))
    return raised / jnp.sum(raised, axis=-1, keepdims=True)


def allowed_pairs(segment_column, segment_row):
    count = segment_column.shape[0]
    row = lax.broadcasted_iota(jnp.int32, (count, count), 0)
    column = lax.broadcasted_iota(jnp.int32, (count, count), 1)
    return (segment_column[...] == segment_row[...]) & (column <= row)


def attend_kernel(
    queries, keys, values, query_gain, key_gain, cosine, sine, seg_column, seg_row, out
):
    allowed = allowed_pairs(seg_column, seg_row)
    cosine, sine = cosine[...], sine[...]
    key = norm_rope(keys[...], key_gain[...], cosine, sine)[0].astype(jnp.bfloat16)
    value = values[...].astype(jnp.bfloat16)
    for lo in range(0, queries.shape[1], HEAD_SIZE):
        span = slice(lo, lo + HEAD_SIZE)
        query = norm_rope(queries[:, span], query_gain[...], cosine, sine)[0]
        weights = softmax_rows(query.astype(jnp.bfloat16), key, allowed)
        out[:, span] = matrix_product(weights.astype(jnp.bfloat16), value).astype(jnp.bfloat16)


def attend_back_kernel(
    first,
    query_columns,
    key_columns,
    queries,
    keys,
    values,
    query_gain,
    key_gain,
    cosine,
    sine,
    seg_column,
    seg_row,
    back_mixture,
    *rest,
):
    out, query_gain_out, key_gain_out = rest[-3:]
    head = first + pl.program_id(0)
    wide = queries.shape[1]
    scaling = HEAD_SIZE ** (-0.5)
    allowed = allowed_pairs(seg_column, seg_row)
    cosine, sine = cosine[...], sine[...]
    key, key_normed, key_scale = norm_rope(keys[...], key_gain[...], cosine, sine)
    key = key.astype(jnp.bfloat16)
    value = values[...].astype(jnp.bfloat16)
    back_key, back_value, query_term = 0.0, 0.0, 0.0
    for lo in range(0, wide, HEAD_SIZE):
        span = slice(lo, lo + HEAD_SIZE)
        query, normed, scale = norm_rope(queries[:, span], query_gain[...], cosine, sine)
        query = query.astype(jnp.bfloat16)
        weights = softmax_rows(query, key, allowed)
        back = back_mixture[:, span]
        back_weights = inner_right(back, value)
        back_value = back_value + inner_left(weights.astype(jnp.bfloat16), back)
        center = jnp.sum(back_weights * weights, axis=-1, keepdims=True)
        back_scores = (weights * (back_weights - center)).astype(jnp.bfloat16)
        back_query = matrix_product(back_scores, key) * scaling
        back_key = back_key + inner_left(back_scores, query) * scaling
        back_query, term = back_norm_rope(
            back_query, normed, scale, query_gain[...], cosine, sine
        )
        query_term = query_term + term
        start = pl.multiple_of(head * wide + lo, HEAD_SIZE)
        out[:, pl.ds(start, HEAD_SIZE)] = back_query.astype(jnp.bfloat16)
    back_key, key_term = back_norm_rope(
        back_key, key_normed, key_scale, key_gain[...], cosine, sine
    )
    start = pl.multiple_of(query_columns + head * HEAD_SIZE, HEAD_SIZE)
    out[:, pl.ds(start, HEAD_SIZE)] = back_key.astype(jnp.bfloat16)
    start = pl.multiple_of(query_columns + key_columns + head * HEAD_SIZE, HEAD_SIZE)
    out[:, pl.ds(start, HEAD_SIZE)] = back_value.astype(jnp.bfloat16)
    add_sum(query_gain_out, query_term)
    add_sum(key_gain_out, key_term)


def attention_call(raw, query_columns, key_columns, gains, tables, segment, heads, back=None):
    rows, columns = raw.shape
    first, count = heads
    wide = query_columns * HEAD_SIZE // key_columns
    first_key = query_columns // HEAD_SIZE + first
    first_value = first_key + key_columns // HEAD_SIZE
    ins = [raw, raw, raw, *gains, *tables, segment[:, None], segment[None, :]]
    specs = [
        pl.BlockSpec((rows, wide), lambda h: (0, first + h)),
        pl.BlockSpec((rows, HEAD_SIZE), lambda h: (0, first_key + h)),
        pl.BlockSpec((rows, HEAD_SIZE), lambda h: (0, first_value + h)),
    ] + [pl.BlockSpec(a.shape, lambda h: (0, 0)) for a in ins[3:]]
    params = dict(
        grid=(count,),
        compiler_params=pltpu.CompilerParams(vmem_limit_bytes=VMEM_LIMIT),
    )
    pairs = count * wide // HEAD_SIZE * rows * rows
    if back is None:
        return pl.pallas_call(
            attend_kernel,
            in_specs=specs,
            out_specs=pl.BlockSpec((rows, wide), lambda h: (0, h)),
            out_shape=jax.ShapeDtypeStruct((rows, count * wide), jnp.bfloat16),
            cost_estimate=pl.CostEstimate(
                flops=4 * pairs * HEAD_SIZE, bytes_accessed=5 * raw.size, transcendentals=pairs
            ),
            **params,
        )(*ins)
    gain_spec = pl.BlockSpec((1, HEAD_SIZE), lambda h: (0, 0))
    gain_shape = jax.ShapeDtypeStruct((1, HEAD_SIZE), jnp.float32)
    return pl.pallas_call(
        functools.partial(attend_back_kernel, first, query_columns, key_columns),
        in_specs=specs + [pl.BlockSpec((rows, wide), lambda h: (0, first + h))],
        out_specs=[pl.BlockSpec((rows, columns), lambda h: (0, 0)), gain_spec, gain_spec],
        out_shape=[jax.ShapeDtypeStruct((rows, columns), jnp.bfloat16), gain_shape, gain_shape],
        cost_estimate=pl.CostEstimate(
            flops=12 * pairs * HEAD_SIZE, bytes_accessed=8 * raw.size, transcendentals=pairs
        ),
        **params,
    )(*ins, back)


def back_first_kernel(raw_grad, full, tokens, out, gain_out):
    value = tokens[...].astype(jnp.float32)
    tile = out.shape[1]
    column = pl.program_id(0) * tile
    back = inner_right(raw_grad[...], full[...])
    out[...] = back.astype(jnp.bfloat16)
    part = tokens[:, pl.ds(pl.multiple_of(column, tile), tile)].astype(jnp.float32)
    gain_out[...] = jnp.sum(back * (part * inverse_rms(value)), axis=0, keepdims=True)


def back_first_call(raw_grad, full, tokens):
    rows, model_width = tokens.shape
    tile = 512
    return pl.pallas_call(
        back_first_kernel,
        grid=(model_width // tile,),
        in_specs=[
            pl.BlockSpec(raw_grad.shape, lambda i: (0, 0)),
            pl.BlockSpec((tile, full.shape[1]), lambda i: (i, 0)),
            pl.BlockSpec(tokens.shape, lambda i: (0, 0)),
        ],
        out_specs=[
            pl.BlockSpec((rows, tile), lambda i: (0, i)),
            pl.BlockSpec((1, tile), lambda i: (0, i)),
        ],
        out_shape=[
            jax.ShapeDtypeStruct((rows, model_width), jnp.bfloat16),
            jax.ShapeDtypeStruct((1, model_width), jnp.float32),
        ],
        compiler_params=pltpu.CompilerParams(vmem_limit_bytes=VMEM_LIMIT),
        cost_estimate=pl.CostEstimate(
            flops=2 * rows * full.size, bytes_accessed=2 * full.size + 8 * tokens.size, transcendentals=0
        ),
    )(raw_grad, full, tokens)


def scatter_kernel(width, info, left, right, *rest):
    mine_out, other_out, whole = rest[-3:]
    whole[...] = inner_left(left[...], right[...])
    mine = whole[pl.ds(pl.multiple_of(info[1] * width, width), width), :]
    other = whole[pl.ds(pl.multiple_of((1 - info[1]) * width, width), width), :]
    if len(rest) > 3:
        mine = mine + rest[0][...].astype(jnp.float32)
        other = other + rest[1][...].astype(jnp.float32)
    mine_out[...] = mine.astype(jnp.bfloat16)
    other_out[...] = other.astype(jnp.bfloat16)


def scatter_call(ring, width, left, right, core, got=()):
    rows, columns = right.shape
    steps = ring.steps
    if 2 * width % LANES:
        blocks = left.reshape(rows, steps, 2, 2, width)
        outs = []
        for k, side in enumerate((ring.side, 1 - ring.side)):
            parts = [
                lax.dynamic_slice(blocks, (0, place, core, side, 0), (rows, 1, 1, 1, width))
                for place in ring.places
            ]
            picked = jnp.concatenate([p.reshape(rows, width) for p in parts], axis=1)
            total = inner_left(picked, right)
            if got:
                total = total + got[k].astype(jnp.float32)
            outs.append(total.astype(jnp.bfloat16))
        return outs
    info = jnp.stack([core, ring.side] + ring.places).astype(jnp.int32)
    half = pl.BlockSpec((width, columns), lambda i, info: (i, 0))
    shape = jax.ShapeDtypeStruct((steps * width, columns), jnp.bfloat16)
    return pl.pallas_call(
        functools.partial(scatter_kernel, width),
        grid_spec=pltpu.PrefetchScalarGridSpec(
            num_scalar_prefetch=1,
            grid=(steps,),
            in_specs=[
                pl.BlockSpec((rows, 2 * width), lambda i, info: (0, info[2 + i] * 2 + info[0])),
                pl.BlockSpec((rows, columns), lambda i, info: (0, 0)),
            ]
            + [half for _ in got],
            out_specs=[half, half],
            scratch_shapes=[pltpu.VMEM((2 * width, columns), jnp.float32)],
        ),
        out_shape=[shape, shape],
        compiler_params=pltpu.CompilerParams(vmem_limit_bytes=VMEM_LIMIT),
        cost_estimate=pl.CostEstimate(
            flops=4 * rows * steps * width * columns,
            bytes_accessed=2 * (right.size + left.size) + 4 * steps * width * columns,
            transcendentals=0,
        ),
    )(info, left, right, *got)


def shards(
    dp_size,
    tokens,
    seq_lengths,
    first_gain,
    query_weight,
    key_matrix,
    value_matrix,
    query_norm_gain,
    key_gain,
    output_weight,
    second_gain,
    gate_weight,
    up_weight,
    down_weight,
    cotangent,
):
    ring = Ring(dp_size)
    steps = ring.steps
    rows, model_width = tokens.shape
    width = query_weight.shape[0]
    key_heads = key_matrix.shape[1] // HEAD_SIZE
    query_columns, key_columns = query_weight.shape[1], key_matrix.shape[1]
    part = rows // PARTS
    tiled = width % LANES == 0
    turned = functools.partial(arrange, steps=steps, width=width)
    turn = turned if tiled else (lambda value: value)
    if not tiled:
        tokens, cotangent = turned(tokens), turned(cotangent)

    def parts_of(value):
        return [value[i * part : (i + 1) * part] for i in range(PARTS)]

    hidden_width = gate_weight.shape[1] // 2
    chunk = hidden_width // CHUNKS
    pieces = [ring.pick(w, 1) for w in (gate_weight, up_weight, down_weight.T)]
    feed_mine, feed_other = (
        [
            jnp.concatenate([p[k][:, j * chunk : (j + 1) * chunk] for p in pieces], axis=1)
            for j in range(CHUNKS)
        ]
        for k in range(2)
    )
    feed_full = [None] * CHUNKS

    def feed_gather(j, got):
        block = ring.ordered(feed_mine[j], got, 0)
        feed_full[j] = lax.all_gather(
            block, "dp", axis=0, tiled=True, axis_index_groups=ring.groups
        )

    attention = Gather(ring, jnp.concatenate([query_weight, key_matrix, value_matrix], axis=1))
    output = Gather(ring, output_weight.T)

    def step(movers, *others):
        moves = [mover.start() for mover in movers]
        moves, others = lax.optimization_barrier((moves, others))
        for mover, move in zip(movers, moves):
            mover.finish(move)
        return others

    live_rows, segment, position = layout(seq_lengths[0], rows)
    cosine_table, sinusoid_table = rotation(position, HEAD_SIZE)
    gain_one = arrange_vector(first_gain.astype(jnp.float32), steps)[None]
    gain_two = arrange_vector(second_gain.astype(jnp.float32), steps)[None]
    tables = (
        jnp.concatenate([cosine_table[:, 0], cosine_table[:, 0]], axis=1),
        jnp.concatenate([-sinusoid_table[:, 0], sinusoid_table[:, 0]], axis=1),
    )
    head_gains = (
        query_norm_gain.astype(jnp.float32)[None],
        key_gain.astype(jnp.float32)[None],
    )
    token_rows, upstream, input_one = row_call(
        functools.partial(first_kernel, turn),
        rows,
        128,
        [
            (tokens, "rows"),
            (cotangent, "rows"),
            (live_rows[:, None].astype(jnp.float32), "rows"),
            (gain_one, "all"),
        ],
        [(model_width, jnp.bfloat16)] * 3,
    )
    for i in range(steps):
        if i == 0:
            token_rows, upstream, input_one, tables = step(
                [attention], token_rows, upstream, input_one, tables
            )
        elif i == steps - 2:
            (got,) = step([attention], ring.swap_side(feed_other[0]))
            feed_gather(0, got)
        elif i == steps - 1:
            step([attention, output])
        else:
            step([attention])
    step([attention])
    attention_full = attention.result()
    upstream_parts = parts_of(upstream)
    upstream_other = []

    raw = matrix_product(input_one, attention_full)
    raw, got, back = step(
        [output], raw, ring.swap_side(feed_other[1]), ring.swap_side(upstream_parts[0])
    )
    upstream_other.append(back)
    feed_gather(1, got)
    half = key_heads // 2
    attend_args = (raw, query_columns, key_columns, head_gains, tables, segment)
    mixture_low = []
    for i in range(2):
        (mixed,) = step([output], attention_call(*attend_args, (i * half, half)))
        mixture_low.append(mixed)
    while output.index <= steps:
        step([output])
    mixture_low = jnp.concatenate(mixture_low, axis=1)
    branch = inner_right(mixture_low, output.result()).astype(jnp.bfloat16)
    extra = [ring.swap_side(w) for w in feed_other[2:]]
    branch, extra = settle(branch, extra)
    for j, got in enumerate(extra):
        feed_gather(2 + j, got)

    branch_parts, token_parts = parts_of(branch), parts_of(token_rows)
    middle_parts, normed_parts = [], []
    got = None
    for i in range(PARTS + 1):
        work = []
        if i:
            work = row_call(
                middle_kernel,
                part,
                part,
                [
                    (token_parts[i - 1], "rows"),
                    (branch_parts[i - 1], "rows"),
                    (got, "rows"),
                    (gain_two, "all"),
                ],
                [(model_width, jnp.float32), (model_width, jnp.bfloat16)],
            )
        if i < PARTS:
            moves = [swap_tensor(branch_parts[i])]
            if i + 1 < PARTS:
                moves.append(ring.swap_side(upstream_parts[i + 1]))
            moves, work, branch_parts = settle(moves, work, branch_parts)
            got = moves[0]
            upstream_other += moves[1:]
        if i:
            middle_parts.append(work[0])
            normed_parts.append(work[1])
    normed_other = [ring.swap_side(p) for p in normed_parts]
    middle = jnp.concatenate(middle_parts, axis=0)
    normed = jnp.concatenate(normed_parts, axis=0)

    span, out_span = (0, 2 * chunk), (2 * chunk, 3 * chunk)
    acts = [feed_call(normed, upstream, feed_full[0])]
    for j in range(1, CHUNKS - 1):
        acts.append(feed_call(normed, upstream, feed_full[j], acts[-1:]))
    normed_other = jnp.concatenate(normed_other, axis=0)
    upstream_other = jnp.concatenate(upstream_other, axis=0)
    sides = (normed, normed_other), (upstream, upstream_other)
    acts_other, feed_grads = [], []
    for j in range(CHUNKS - 1):
        acts_other.append(
            feed_call(normed_other, upstream_other, feed_full[j], (acts[-1:] + feed_grads)[-1:])
        )
        feed_grads.append(grad_call(*sides, (acts[j], acts_other[j])))
    early_other = wide_call(acts_other, feed_full[:-1], span, jnp.float32, ties=feed_grads[-1:])
    early_mine = wide_call(acts, feed_full[:-1], span, jnp.float32, ties=(early_other,))
    acts_other.append(feed_call(normed_other, upstream_other, feed_full[-1], (early_mine,)))
    back_other = wide_call(acts_other[-1:], feed_full[-1:], span, jnp.bfloat16, early_other)
    acts.append(feed_call(normed, upstream, feed_full[-1], (back_other,)))

    back_other = parts_of(back_other)
    back_mine = wide_call(acts[-1:], feed_full[-1:], span, jnp.float32, early_mine)
    got, back_mine = settle(ring.swap_side(back_other[0]), back_mine)
    back_mine = parts_of(back_mine)
    mine = add_low(back_mine[0], got)
    back_parts, low_parts, mixed_parts, grad_second = [], [], [], 0.0
    out_other, out_mine, out_sums, out_got = None, None, [], []

    def back_middle_call(i, mine, other):
        return row_call(
            back_middle_kernel,
            part,
            part,
            [
                (mine, "rows"),
                (other, "rows"),
                (middle_parts[i], "rows"),
                (upstream_parts[i], "rows"),
                (gain_two, "all"),
            ],
            [(model_width, jnp.float32), (model_width, jnp.bfloat16)],
            [model_width],
        )

    output_full = output.result()
    for i in range(PARTS):
        work = []
        if i == 0:
            work = [grad_call(*sides, (acts[-1], acts_other[-1]), (mine,))]
        if i == 1:
            work = [wide_call(acts_other, feed_full, out_span, jnp.bfloat16, ties=(mine,))]
        if i == 2:
            work = [wide_call(acts, feed_full, out_span, jnp.float32, ties=(mine,))]
        done = []
        if i:
            back, low, term = back_middle_call(i - 1, last[0], last[1])
            done = [back, low, term, matrix_product(low, output_full).astype(jnp.bfloat16)]
        moves = [swap_tensor(mine)]
        moves.append(ring.swap_side(back_other[i + 1] if i + 1 < PARTS else out_other[0]))
        moves, work, done = settle(moves, work, done)
        last = (mine, moves[0])
        if i + 1 < PARTS:
            mine = add_low(back_mine[i + 1], moves[1])
        else:
            out_got.append(moves[1])
        if i == 0:
            feed_grads.append(work[0])
        if i == 1:
            out_other = parts_of(work[0])
        if i == 2:
            out_mine = parts_of(work[0])
        if done:
            back_parts.append(done[0])
            low_parts.append(done[1])
            grad_second = grad_second + done[2]
            mixed_parts.append(done[3])
    back, low, term = back_middle_call(PARTS - 1, last[0], last[1])
    back_parts.append(back)
    low_parts.append(low)
    grad_second = grad_second + term
    mixed_parts.append(matrix_product(low, output_full).astype(jnp.bfloat16))
    back_middle = jnp.concatenate(back_parts, axis=0)
    branch_low = jnp.concatenate(low_parts, axis=0)
    back_mixture = jnp.concatenate(mixed_parts, axis=0)

    scattered = [
        lax.psum_scatter(
            grad, "dp", scatter_dimension=0, tiled=True, axis_index_groups=ring.groups
        )
        for grad in feed_grads
    ]

    core = ring.core
    far = scatter_call(ring, width, branch_low, mixture_low, 1 - core)
    out_sums.append(add_low(out_mine[0], out_got[0]))
    raw_grads, head_terms, far_got, out_done = [], [], None, []
    for i in range(2):
        moves = [ring.swap_side(out_other[1 + i]), swap_tensor(out_sums[i])]
        if i == 0:
            moves += [ring.swap_core(f) for f in far]
        work = attention_call(*attend_args, (i * half, half), back_mixture)
        moves, work = settle(moves, work)
        out_sums.append(add_low(out_mine[1 + i], moves[0]))
        out_done.append(moves[1])
        if i == 0:
            near = scatter_call(ring, width, branch_low, mixture_low, core, moves[2:])
        raw_grads.append(work[0])
        head_terms.append(work[1:])
    heads_done = half * HEAD_SIZE
    queries_done = query_columns // 2

    def join(first, second, start, size, cut):
        return [first[:, start : start + cut], second[:, start + cut : start + size]]

    raw_grad = jnp.concatenate(
        join(*raw_grads, 0, query_columns, queries_done)
        + join(*raw_grads, query_columns, key_columns, heads_done)
        + join(*raw_grads, query_columns + key_columns, key_columns, heads_done),
        axis=1,
    )
    grad_qgain = head_terms[0][0] + head_terms[1][0]
    grad_kgain = head_terms[0][1] + head_terms[1][1]

    output_sum = Scatter(ring, *near)
    far = scatter_call(ring, width, input_one, raw_grad, 1 - core)
    moves = [ring.swap_core(f) for f in far] + [
        ring.swap_side(out_other[3]),
        swap_tensor(out_sums[2]),
    ]
    back_one, grad_first, moves = settle(
        *back_first_call(raw_grad, attention_full, token_rows), moves
    )
    out_sums.append(add_low(out_mine[3], moves[2]))
    out_done.append(moves[3])
    attention_sum = Scatter(
        ring, *scatter_call(ring, width, input_one, raw_grad, core, moves[:2])
    )
    back_one = parts_of(back_one)
    back_one_other = []
    gains = jnp.concatenate(
        [
            arrange_vector(grad_first[0], steps),
            arrange_vector(grad_second[0], steps) * 0.5,
            grad_qgain[0],
            grad_kgain[0],
        ]
    )
    (out_last,) = step([output_sum], swap_tensor(out_sums[3]))
    out_done.append(out_last)
    pairs = [ring.pick(total, 0) for total in scattered]
    pairs_got = []
    gains = gains + swap_tensor(gains)
    distance = 1
    for i in range(steps):
        movers = [attention_sum] + ([output_sum] if output_sum.index < steps else [])
        others = []
        if i < PARTS:
            others.append(swap_tensor(back_one[i]))
        if distance < dp_size:
            others.append(
                lax.ppermute(gains, "dp", [(k, k ^ distance) for k in range(dp_size)])
            )
        final = i - (steps - 1 - CHUNKS)
        if 0 < final < CHUNKS:
            others.insert(0, ring.swap_side(pairs[final - 1][1]))
        others = list(step(movers, *others))
        if 0 < final < CHUNKS:
            pairs_got.append(others.pop(0))
        if distance < dp_size:
            gains = gains + others.pop()
            distance *= 2
        back_one_other += others
    (token_grad,) = row_call(
        functools.partial(token_kernel, turn),
        rows,
        128,
        [
            (jnp.concatenate(back_one, axis=0), "rows"),
            (jnp.concatenate(back_one_other, axis=0), "rows"),
            (token_rows, "rows"),
            (back_middle, "rows"),
            (gain_one, "all"),
        ],
        [(model_width, jnp.float32)],
    )
    (block_output,) = row_call(
        functools.partial(output_kernel, turn),
        rows,
        128,
        [
            (middle, "rows"),
            (jnp.concatenate(out_sums, axis=0), "rows"),
            (jnp.concatenate(out_done, axis=0), "rows"),
        ],
        [(model_width, jnp.bfloat16)],
    )
    if not tiled:
        token_grad, block_output = turned(token_grad), turned(block_output)
    grad_output = output_sum.total
    grad_attention = attention_sum.total
    grad_query = grad_attention[:, :query_columns]
    grad_key = grad_attention[:, query_columns : query_columns + key_columns]
    grad_value = grad_attention[:, query_columns + key_columns :]

    chunk_grads = []
    pairs_got.append(ring.swap_side(pairs[-1][1]))
    for (mine, _), other in zip(pairs, pairs_got):
        both = (
            jnp.where(ring.side == 0, mine, other),
            jnp.where(ring.side == 0, other, mine),
        )
        chunk_grads.append([b.astype(jnp.float32) for b in both])
    grad_gate, grad_up, grad_down = (
        jnp.concatenate(
            [
                chunk_grads[j][side][:, k * chunk : (k + 1) * chunk]
                for side in range(2)
                for j in range(CHUNKS)
            ],
            axis=1,
        )
        for k in range(3)
    )

    while distance < dp_size:
        gains = gains + lax.ppermute(gains, "dp", [(k, k ^ distance) for k in range(dp_size)])
        distance *= 2
    index = lax.axis_index("dp")

    def own_part(start, size):
        return lax.dynamic_slice_in_dim(gains, start + index * (size // dp_size), size // dp_size)

    return (
        block_output,
        token_grad,
        own_part(0, model_width),
        grad_query,
        grad_key,
        grad_value,
        own_part(2 * model_width, HEAD_SIZE),
        own_part(2 * model_width + HEAD_SIZE, HEAD_SIZE),
        grad_output.T,
        own_part(model_width, model_width),
        grad_gate,
        grad_up,
        grad_down.T,
    )


def solution(mesh):
    return jax.shard_map(
        functools.partial(shards, mesh.shape["dp"]),
        mesh=mesh,
        in_specs=(
            P("dp", None),
            P("dp", None),
            P(),
            P("dp", "tensor"),
            P("dp", "tensor"),
            P("dp", "tensor"),
            P(),
            P(),
            P("tensor", "dp"),
            P(),
            P("dp", "tensor"),
            P("dp", "tensor"),
            P("tensor", "dp"),
            P("dp", None),
        ),
        out_specs=(
            P("dp", None),
            P("dp", None),
            P("dp"),
            P("dp", "tensor"),
            P("dp", "tensor"),
            P("dp", "tensor"),
            P("dp"),
            P("dp"),
            P("tensor", "dp"),
            P("dp"),
            P("dp", "tensor"),
            P("dp", "tensor"),
            P("tensor", "dp"),
        ),
        check_vma=False,
    )
```

```python
import functools

import jax
import jax.numpy as jnp
from jax import lax
from jax.experimental import pallas as pl
from jax.experimental.pallas import tpu as pltpu
from jax.sharding import PartitionSpec as P

HEAD_SIZE = 128
BLK = 64


epsilon = 1e-06
rope_base = 1000000.0


def matrix_product(left, right):
    return jnp.dot(left, right, preferred_element_type=jnp.float32)


def inner_left(left, right):
    return lax.dot_general(
        left, right, (((0,), (0,)), ((), ())), preferred_element_type=jnp.float32
    )


def inner_right(left, right):
    return lax.dot_general(
        left, right, (((1,), (1,)), ((), ())), preferred_element_type=jnp.float32
    )


def layout(lengths, count_of_rows):
    padded = (lengths + BLK - 1) // BLK * BLK
    starts = jnp.cumsum(padded) - padded
    row_index = jnp.arange(count_of_rows, dtype=jnp.int32)
    inside = (row_index[:, None] >= starts[None, :]) & (
        row_index[:, None] < (starts + lengths)[None, :]
    )
    live_rows = jnp.any(inside, axis=1)
    slot_index = jnp.arange(lengths.shape[0], dtype=jnp.int32)
    owning = jnp.sum(jnp.where(inside, slot_index[None, :], 0), axis=1)
    position = jnp.sum(jnp.where(inside, row_index[:, None] - starts[None, :], 0), axis=1)
    segment = jnp.where(live_rows, owning, -1 - row_index)
    return (live_rows, segment, position)


def rotation(position, width):
    half_width = width // 2
    frequency = jnp.power(rope_base, -(jnp.arange(half_width, dtype=jnp.float32) * 2.0) / width)
    angles = position.astype(jnp.float32)[:, None] * frequency[None, :]
    return (jnp.cos(angles)[:, None, :], jnp.sin(angles)[:, None, :])


CHUNKS = 3
PARTS = 4
LANES = 128
VMEM_LIMIT = 56 * 1024 * 1024


def add_low(left, right):
    return (left.astype(jnp.float32) + right.astype(jnp.float32)).astype(jnp.bfloat16)


class Ring:
    def __init__(self, size):
        self.size = size
        self.steps = size // 4
        index = lax.axis_index("dp")
        self.place = index // 4
        self.side = (index // 2) % 2
        self.core = index % 2
        self.places = [(self.place - 1 - i) % self.steps for i in range(self.steps)]
        self.groups = [
            [place * 4 + side * 2 + core for place in range(self.steps) for core in range(2)]
            for side in range(2)
        ]

    def swap_core(self, value):
        return lax.ppermute(value, "dp", [(i, i ^ 1) for i in range(self.size)])

    def swap_side(self, value):
        return lax.ppermute(value, "dp", [(i, i ^ 2) for i in range(self.size)])

    def shift(self, value, places):
        return lax.ppermute(
            value, "dp", [(i, (i + 4 * places) % self.size) for i in range(self.size)]
        )

    def pick(self, value, axis):
        low, high = jnp.split(value, 2, axis=axis)
        return (
            jnp.where(self.side == 0, low, high),
            jnp.where(self.side == 0, high, low),
        )

    def ordered(self, mine, other, axis):
        return jnp.where(
            self.side == 0,
            jnp.concatenate([mine, other], axis=axis),
            jnp.concatenate([other, mine], axis=axis),
        )

    def block(self, back, core, side):
        return ((self.place - back) % self.steps) * 4 + core * 2 + side


class Gather:
    def __init__(self, ring, piece):
        self.ring = ring
        self.hops, self.across, self.index = [piece], None, 0
        self.pieces, self.order = [], []

    def put(self, back, core, side, value):
        self.pieces.append(value)
        self.order.append(self.ring.block(back, core, side))

    def start(self, stages, hop=True, swap=True):
        ring, moves = self.ring, {}
        self.hops = list(stages.hold(*self.hops))
        if hop and len(self.hops) < ring.steps:
            moves["hop"] = ring.shift(self.hops[-1], 1)
        if swap and self.index < ring.steps:
            moves["side"] = ring.swap_side(self.hops[self.index])
            moves["core"] = ring.swap_core(self.hops[self.index])
        if swap and self.across is not None:
            moves["both"] = ring.swap_core(self.across)
        return moves

    def finish(self, moves):
        ring, back = self.ring, self.index
        core, side = ring.core, ring.side
        if "hop" in moves:
            self.hops.append(moves["hop"])
        if "both" in moves:
            self.put(back - 1, 1 - core, 1 - side, moves["both"])
            self.across = None
        if "side" in moves:
            self.put(back, core, side, self.hops[back])
            self.put(back, core, 1 - side, moves["side"])
            self.put(back, 1 - core, side, moves["core"])
            self.across = moves["side"]
            self.index += 1

    @property
    def done(self):
        return len(self.pieces) == self.ring.size


class Scatter:
    def __init__(self, ring, mine, other, crossed=None):
        self.ring = ring
        self.mine, self.other, self.crossed = mine, other, crossed
        self.term, self.index, self.total = None, 0, None
        if crossed is not None:
            self.add({"side": crossed[0]})

    def start(self, stages):
        moves = {}
        if self.index < self.ring.steps and self.crossed is None:
            (other,) = stages.hold(self.other[self.index])
            moves["side"] = self.ring.swap_side(other)
        if self.term is not None:
            moves["hop"] = self.ring.shift(self.term, 1)
        return moves

    def finish(self, moves):
        if self.crossed is not None:
            moves = dict(moves, side=self.crossed[self.index])
        self.add(moves)

    def add(self, moves):
        value = self.mine[self.index].astype(jnp.float32) + moves["side"].astype(jnp.float32)
        if "hop" in moves:
            value = value + moves["hop"].astype(jnp.float32)
        self.index += 1
        self.total = value
        self.term = value.astype(jnp.bfloat16) if self.index < self.ring.steps else None


class Stages:
    def __init__(self, mark):
        self.mark = mark

    def settle(self, *values):
        values, self.mark = lax.optimization_barrier((values, self.mark))
        return values

    def step(self, movers, *others):
        movers = [mover if isinstance(mover, tuple) else (mover, {}) for mover in movers]
        moves = [mover.start(self, **kind) for mover, kind in movers]
        moves, others = self.settle(moves, others)
        for (mover, _), move in zip(movers, moves):
            mover.finish(move)
        return others

    def hold(self, *values):
        return lax.optimization_barrier((values, self.mark))[0]

    @property
    def ties(self):
        return (self.mark,)


def swap_tensor(value):
    return lax.ppermute(value, "tensor", [(0, 1), (1, 0)])


def arrange(value, steps, width):
    blocks = [value[:, i * width : (i + 1) * width] for i in range(4 * steps)]
    order = [4 * place + k for place in range(steps) for k in (0, 2, 1, 3)]
    return jnp.concatenate([blocks[i] for i in order], axis=1)


def arrange_vector(vector, steps):
    return vector.reshape(steps, 2, 2, -1).swapaxes(1, 2).reshape(-1)


def loose(ties):
    return [pl.BlockSpec(memory_space=pl.ANY) for _ in ties]


def row_call(kernel, rows, block, ins, outs, sums=(), ties=(), into=None):
    arrays, specs, places, cuts = [], [], [], 1
    for value, kind in ins:
        places.append(len(arrays))
        if kind == "parts":
            cuts = len(value)
            span = rows // cuts // block
            for k, piece in enumerate(value):
                arrays.append(piece)
                specs.append(
                    pl.BlockSpec(
                        (block, piece.shape[1]),
                        lambda i, k=k, span=span: (jnp.clip(i - k * span, 0, span - 1), 0),
                    )
                )
            continue
        arrays.append(value)
        if kind == "all":
            specs.append(pl.BlockSpec(value.shape, lambda i: (0, 0)))
        else:
            first = 0 if kind == "rows" else kind
            specs.append(
                pl.BlockSpec((block, value.shape[1]), lambda i, first=first: (first + i, 0))
            )
    base, all_rows, aliases = 0, rows, {}
    count = len(arrays)
    if into is not None:
        given, base, all_rows = into
        if given is not None:
            ties = (given, *ties)
            aliases = {count: 0}
    out_specs = [pl.BlockSpec((block, c), lambda i: (base + i, 0)) for c, _ in outs]
    out_specs += [pl.BlockSpec((1, c), lambda i: (0, 0)) for c in sums]
    out_shape = [jax.ShapeDtypeStruct((all_rows, c), d) for c, d in outs]
    out_shape += [jax.ShapeDtypeStruct((1, c), jnp.float32) for c in sums]
    moved = sum(a.size * a.dtype.itemsize for a in arrays)
    moved += sum(rows * c * jnp.dtype(d).itemsize for c, d in outs)

    def body(*refs):
        given = refs[count + len(ties) :]
        if cuts == 1:
            kernel(*refs[:count], *given)
            return
        turn = pl.program_id(0) // (rows // cuts // block)
        for k in range(cuts):
            chosen = [
                refs[place + k] if kind == "parts" else refs[place]
                for place, (_, kind) in zip(places, ins)
            ]
            pl.when(turn == k)(functools.partial(kernel, *chosen, *given))

    return pl.pallas_call(
        body,
        grid=(rows // block,),
        in_specs=specs + loose(ties),
        out_specs=out_specs,
        out_shape=out_shape,
        input_output_aliases=aliases,
        compiler_params=pltpu.CompilerParams(vmem_limit_bytes=VMEM_LIMIT),
        cost_estimate=pl.CostEstimate(flops=0, bytes_accessed=moved, transcendentals=0),
    )(*arrays, *ties)


def inverse_rms(value):
    return lax.rsqrt(jnp.mean(value * value, axis=-1, keepdims=True) + epsilon)


def first_kernel(turn, tokens, cotangent, live, gain, tokens_out, upstream_out, normed_out):
    value = turn(tokens[...])
    tokens_out[...] = value
    value = value.astype(jnp.float32)
    normed_out[...] = (value * inverse_rms(value) * gain[...]).astype(jnp.bfloat16)
    back = turn(cotangent[...]).astype(jnp.float32)
    upstream_out[...] = (back * live[...]).astype(jnp.bfloat16)


def middle_kernel(tokens, mine, other, gain, middle_out, normed_out):
    branch = mine[...].astype(jnp.float32) + other[...].astype(jnp.float32)
    value = tokens[...].astype(jnp.float32) + branch
    middle_out[...] = value
    normed_out[...] = (value * inverse_rms(value) * gain[...]).astype(jnp.bfloat16)


def back_rms(value, gain, back):
    scale = inverse_rms(value)
    normed = value * scale
    pulled = back * gain
    center = jnp.mean(pulled * normed, axis=-1, keepdims=True)
    return scale * (pulled - normed * center), back * normed


def add_sum(out_ref, value):
    @pl.when(pl.program_id(0) == 0)
    def _():
        out_ref[...] = jnp.zeros_like(out_ref)

    out_ref[...] += jnp.sum(value, axis=0, keepdims=True)


def back_middle_kernel(
    mine, other, middle, upstream, gain, full, back_out, low_out, mixed_out, gain_out
):
    back = mine[...].astype(jnp.float32) + other[...].astype(jnp.float32)
    value, gain_term = back_rms(middle[...], gain[...], back)
    value = value + upstream[...].astype(jnp.float32)
    back_out[...] = value
    low = value.astype(jnp.bfloat16)
    low_out[...] = low
    mixed_out[...] = matrix_product(low, full[...]).astype(jnp.bfloat16)
    add_sum(gain_out, gain_term)


def output_kernel(turn, middle, mine, other, out):
    value = middle[...] + mine[...].astype(jnp.float32) + other[...].astype(jnp.float32)
    out[...] = turn(value).astype(jnp.bfloat16)


def token_kernel(turn, mine, other, tokens, back_middle, gain, out):
    back = mine[...].astype(jnp.float32) + other[...].astype(jnp.float32)
    value, _ = back_rms(tokens[...].astype(jnp.float32), gain[...], back)
    out[...] = turn(value + back_middle[...])


def feed_kernel(chunk, count, many, *refs):
    full, out = refs[count], refs[-1]
    block = out.shape[0]

    def picked(group, step):
        refs_of = refs[group[0] : group[1]]
        if len(refs_of) == 1:
            return refs_of[0][...]
        each = block // refs_of[0].shape[0]
        return jnp.concatenate([r[...] for r in refs_of[step * each : (step + 1) * each]], axis=0)

    def run(step):
        normed, upstream = picked((0, many), step), picked((many, count), step)
        gate = matrix_product(normed, full[:, :chunk])
        up = matrix_product(normed, full[:, chunk : 2 * chunk])
        back = matrix_product(upstream, full[:, 2 * chunk :])
        share = jax.nn.sigmoid(gate)
        active = gate * share
        out[:, :chunk] = (back * up * (share * (1.0 + gate * (1.0 - share)))).astype(jnp.bfloat16)
        out[:, chunk : 2 * chunk] = (back * active).astype(jnp.bfloat16)
        out[:, 2 * chunk :] = (active * up).astype(jnp.bfloat16)

    for step in range(2):
        pl.when(pl.program_id(0) == step)(functools.partial(run, step))


def feed_call(normed, upstream, full, ties=()):
    groups = [g if isinstance(g, list) else [g] for g in (normed, upstream)]
    rows, model_width = sum(a.shape[0] for a in groups[0]), full.shape[0]
    columns = full.shape[1]
    block = rows // 2
    specs = []
    for group in groups:
        if len(group) == 1:
            specs.append(pl.BlockSpec((block, model_width), lambda i: (i, 0)))
        else:
            specs += [pl.BlockSpec(a.shape, lambda i: (0, 0)) for a in group]
    return pl.pallas_call(
        functools.partial(feed_kernel, columns // 3, len(specs), len(groups[0])),
        grid=(2,),
        in_specs=specs + [pl.BlockSpec(full.shape, lambda i: (0, 0))] + loose(ties),
        out_specs=pl.BlockSpec((block, columns), lambda i: (i, 0)),
        out_shape=jax.ShapeDtypeStruct((rows, columns), jnp.bfloat16),
        compiler_params=pltpu.CompilerParams(vmem_limit_bytes=VMEM_LIMIT),
        cost_estimate=pl.CostEstimate(
            flops=2 * rows * model_width * columns,
            bytes_accessed=2 * (2 * rows * model_width + full.size + rows * columns),
            transcendentals=rows * columns // 3,
        ),
    )(*groups[0], *groups[1], full, *ties)


def wide_kernel(count, started, parts, *refs):
    outs, total = refs[-parts:], None
    for act, full in zip(refs[:count], refs[count : 2 * count]):
        term = inner_right(act[...], full[...])
        total = term if total is None else total + term
    if started:
        total = total + refs[2 * count][...]
    part = outs[0].shape[0]
    for i, out in enumerate(outs):
        out[...] = total[i * part : (i + 1) * part].astype(out.dtype)


def wide_call(acts, fulls, span, out_dtype, start=None, ties=(), parts=PARTS):
    lo, hi = span
    size, index = hi - lo, lo // (hi - lo)
    rows, model_width, count = acts[0].shape[0], fulls[0].shape[0], len(acts)
    tile = 512
    ins = list(acts) + list(fulls)
    specs = [pl.BlockSpec((rows, size), lambda i: (0, index))] * count
    specs += [pl.BlockSpec((tile, size), lambda i: (i, index))] * count
    if start is not None:
        ins.append(start)
        specs.append(pl.BlockSpec((rows, tile), lambda i: (0, i)))
    ins += list(ties)
    specs += [pl.BlockSpec(memory_space=pl.ANY) for _ in ties]
    return pl.pallas_call(
        functools.partial(wide_kernel, count, start is not None, parts),
        grid=(model_width // tile,),
        in_specs=specs,
        out_specs=[pl.BlockSpec((rows // parts, tile), lambda i: (0, i))] * parts,
        out_shape=[jax.ShapeDtypeStruct((rows // parts, model_width), out_dtype)] * parts,
        compiler_params=pltpu.CompilerParams(vmem_limit_bytes=VMEM_LIMIT),
        cost_estimate=pl.CostEstimate(
            flops=2 * rows * model_width * size * count,
            bytes_accessed=2 * (rows + model_width) * size * count + rows * model_width * 6,
            transcendentals=0,
        ),
    )(*ins)


def grad_kernel(split, counts, *refs):
    out = refs[-1]
    acts = refs[sum(counts) : sum(counts) + 2]
    first = 0
    total = [0.0, 0.0]
    for group, count in enumerate(counts):
        rows, act = 0, acts[group % 2]
        columns = slice(0, split) if group < 2 else slice(split, None)
        parts = [r[...] for r in refs[first : first + count]]
        left = parts[0] if count == 1 else jnp.concatenate(parts, axis=0)
        total[group // 2] = total[group // 2] + inner_left(left, act[:, columns])
        first += count
    out[:, :split] = total[0].astype(jnp.bfloat16)
    out[:, split:] = total[1].astype(jnp.bfloat16)


def grad_call(normed, upstream, acts, ties=(), place=0, places=1, into=None):
    groups = [g if isinstance(g, list) else [g] for g in (*normed, *upstream)]
    lefts = [a for group in groups for a in group]
    rows, model_width = acts[0].shape[0], lefts[0].shape[1]
    columns = acts[0].shape[1]
    tall = 512
    ins = lefts + list(acts)
    specs = [pl.BlockSpec((a.shape[0], tall), lambda i: (0, i)) for a in lefts]
    specs += [pl.BlockSpec((rows, columns), lambda i: (0, 0))] * 2
    aliases = {}
    if into is not None:
        aliases = {len(ins): 0}
        ins.append(into)
        specs.append(pl.BlockSpec(memory_space=pl.ANY))
    return pl.pallas_call(
        functools.partial(grad_kernel, columns // 3 * 2, [len(g) for g in groups]),
        grid=(model_width // tall,),
        in_specs=specs + loose(ties),
        out_specs=pl.BlockSpec((tall, columns), lambda i: (i, place)),
        out_shape=jax.ShapeDtypeStruct((model_width, places * columns), jnp.bfloat16),
        input_output_aliases=aliases,
        compiler_params=pltpu.CompilerParams(vmem_limit_bytes=VMEM_LIMIT),
        cost_estimate=pl.CostEstimate(
            flops=4 * rows * model_width * columns,
            bytes_accessed=2 * (4 * rows * model_width + 2 * rows * columns + model_width * columns),
            transcendentals=0,
        ),
    )(*ins, *ties)


def norm_rope(raw, gain, cosine, sine):
    scale = inverse_rms(raw)
    normed = raw * scale
    scaled = normed * gain
    return scaled * cosine + pltpu.roll(scaled, HEAD_SIZE // 2, 1) * sine, normed, scale


def back_norm_rope(back, normed, scale, gain, cosine, sine):
    back = back * cosine - pltpu.roll(back, HEAD_SIZE // 2, 1) * sine
    pulled = back * gain
    center = jnp.mean(pulled * normed, axis=-1, keepdims=True)
    return scale * (pulled - normed * center), back * normed


def softmax_rows(query, key, allowed):
    scores = jnp.where(allowed, inner_right(query, key) * HEAD_SIZE ** (-0.5), -1e30)
    raised = jnp.exp(scores - jnp.max(scores, axis=-1, keepdims=True))
    return raised / jnp.sum(raised, axis=-1, keepdims=True)


def allowed_pairs(segment_column, segment_row):
    count = segment_column.shape[0]
    row = lax.broadcasted_iota(jnp.int32, (count, count), 0)
    column = lax.broadcasted_iota(jnp.int32, (count, count), 1)
    return (segment_column[...] == segment_row[...]) & (column <= row)


def attend_kernel(
    queries, keys, values, query_gain, key_gain, cosine, sine, seg_column, seg_row, *rest
):
    out = rest[-1]
    allowed = allowed_pairs(seg_column, seg_row)
    cosine, sine = cosine[...], sine[...]
    key = norm_rope(keys[...], key_gain[...], cosine, sine)[0].astype(jnp.bfloat16)
    value = values[...].astype(jnp.bfloat16)
    for lo in range(0, queries.shape[1], HEAD_SIZE):
        span = slice(lo, lo + HEAD_SIZE)
        query = norm_rope(queries[:, span], query_gain[...], cosine, sine)[0]
        weights = softmax_rows(query.astype(jnp.bfloat16), key, allowed)
        out[:, span] = matrix_product(weights.astype(jnp.bfloat16), value).astype(jnp.bfloat16)


def attend_back_kernel(
    first,
    query_columns,
    key_columns,
    queries,
    keys,
    values,
    query_gain,
    key_gain,
    cosine,
    sine,
    seg_column,
    seg_row,
    *rest,
):
    out, query_gain_out, key_gain_out = rest[-3:]
    back_parts = rest[:PARTS]
    head = first + pl.program_id(0)
    wide = queries.shape[1]
    scaling = HEAD_SIZE ** (-0.5)
    allowed = allowed_pairs(seg_column, seg_row)
    cosine, sine = cosine[...], sine[...]
    key, key_normed, key_scale = norm_rope(keys[...], key_gain[...], cosine, sine)
    key = key.astype(jnp.bfloat16)
    value = values[...].astype(jnp.bfloat16)
    back_key, back_value, query_term = 0.0, 0.0, 0.0
    for lo in range(0, wide, HEAD_SIZE):
        span = slice(lo, lo + HEAD_SIZE)
        query, normed, scale = norm_rope(queries[:, span], query_gain[...], cosine, sine)
        query = query.astype(jnp.bfloat16)
        weights = softmax_rows(query, key, allowed)
        back = jnp.concatenate([b[:, span] for b in back_parts], axis=0)
        back_weights = inner_right(back, value)
        back_value = back_value + inner_left(weights.astype(jnp.bfloat16), back)
        center = jnp.sum(back_weights * weights, axis=-1, keepdims=True)
        back_scores = (weights * (back_weights - center)).astype(jnp.bfloat16)
        back_query = matrix_product(back_scores, key) * scaling
        back_key = back_key + inner_left(back_scores, query) * scaling
        back_query, term = back_norm_rope(
            back_query, normed, scale, query_gain[...], cosine, sine
        )
        query_term = query_term + term
        start = pl.multiple_of(head * wide + lo, HEAD_SIZE)
        out[:, pl.ds(start, HEAD_SIZE)] = back_query.astype(jnp.bfloat16)
    back_key, key_term = back_norm_rope(
        back_key, key_normed, key_scale, key_gain[...], cosine, sine
    )
    start = pl.multiple_of(query_columns + head * HEAD_SIZE, HEAD_SIZE)
    out[:, pl.ds(start, HEAD_SIZE)] = back_key.astype(jnp.bfloat16)
    start = pl.multiple_of(query_columns + key_columns + head * HEAD_SIZE, HEAD_SIZE)
    out[:, pl.ds(start, HEAD_SIZE)] = back_value.astype(jnp.bfloat16)
    add_sum(query_gain_out, query_term)
    add_sum(key_gain_out, key_term)


def attention_call(raw, query_columns, key_columns, gains, tables, segment, heads, back=None, ties=()):
    rows, columns = raw.shape
    first, count = heads
    wide = query_columns * HEAD_SIZE // key_columns
    first_key = query_columns // HEAD_SIZE + first
    first_value = first_key + key_columns // HEAD_SIZE
    ins = [raw, raw, raw, *gains, *tables, segment[:, None], segment[None, :]]
    specs = [
        pl.BlockSpec((rows, wide), lambda h: (0, first + h)),
        pl.BlockSpec((rows, HEAD_SIZE), lambda h: (0, first_key + h)),
        pl.BlockSpec((rows, HEAD_SIZE), lambda h: (0, first_value + h)),
    ] + [pl.BlockSpec(a.shape, lambda h: (0, 0)) for a in ins[3:]]
    params = dict(
        grid=(count,),
        compiler_params=pltpu.CompilerParams(vmem_limit_bytes=VMEM_LIMIT),
    )
    pairs = count * wide // HEAD_SIZE * rows * rows
    if back is None:
        return pl.pallas_call(
            attend_kernel,
            in_specs=specs + loose(ties),
            out_specs=pl.BlockSpec((rows, wide), lambda h: (0, h)),
            out_shape=jax.ShapeDtypeStruct((rows, count * wide), jnp.bfloat16),
            cost_estimate=pl.CostEstimate(
                flops=4 * pairs * HEAD_SIZE, bytes_accessed=5 * raw.size, transcendentals=pairs
            ),
            **params,
        )(*ins, *ties)
    gain_spec = pl.BlockSpec((1, HEAD_SIZE), lambda h: (0, 0))
    gain_shape = jax.ShapeDtypeStruct((1, HEAD_SIZE), jnp.float32)
    return pl.pallas_call(
        functools.partial(attend_back_kernel, first, query_columns, key_columns),
        in_specs=specs
        + [pl.BlockSpec((b.shape[0], wide), lambda h: (0, first + h)) for b in back]
        + loose(ties),
        out_specs=[pl.BlockSpec((rows, columns), lambda h: (0, 0)), gain_spec, gain_spec],
        out_shape=[jax.ShapeDtypeStruct((rows, columns), jnp.bfloat16), gain_shape, gain_shape],
        cost_estimate=pl.CostEstimate(
            flops=12 * pairs * HEAD_SIZE, bytes_accessed=8 * raw.size, transcendentals=pairs
        ),
        **params,
    )(*ins, *back, *ties)


def back_first_kernel(raw_grad, full, tokens, *rest):
    outs, gain_out, scale = rest[-2 - PARTS : -2], rest[-2], rest[-1]
    part, tile = outs[0].shape

    @pl.when(pl.program_id(0) == 0)
    def _():
        scale[...] = inverse_rms(tokens[...].astype(jnp.float32))

    back = inner_right(raw_grad[...], full[...])
    for i, out in enumerate(outs):
        out[...] = back[i * part : (i + 1) * part].astype(jnp.bfloat16)
    start = pl.multiple_of(pl.program_id(0) * tile, tile)
    normed = tokens[:, pl.ds(start, tile)].astype(jnp.float32) * scale[...]
    gain_out[...] = jnp.sum(back * normed, axis=0, keepdims=True)


def back_first_call(raw_grad, full, tokens, ties=()):
    rows, model_width = tokens.shape
    tile, part = 512, rows // PARTS
    return pl.pallas_call(
        back_first_kernel,
        grid=(model_width // tile,),
        in_specs=[
            pl.BlockSpec(raw_grad.shape, lambda i: (0, 0)),
            pl.BlockSpec((tile, full.shape[1]), lambda i: (i, 0)),
            pl.BlockSpec(tokens.shape, lambda i: (0, 0)),
        ]
        + [pl.BlockSpec(memory_space=pl.ANY) for _ in ties],
        out_specs=[pl.BlockSpec((part, tile), lambda i: (0, i))] * PARTS
        + [pl.BlockSpec((1, tile), lambda i: (0, i))],
        out_shape=[jax.ShapeDtypeStruct((part, model_width), jnp.bfloat16)] * PARTS
        + [jax.ShapeDtypeStruct((1, model_width), jnp.float32)],
        scratch_shapes=[pltpu.VMEM((rows, 1), jnp.float32)],
        compiler_params=pltpu.CompilerParams(vmem_limit_bytes=VMEM_LIMIT),
        cost_estimate=pl.CostEstimate(
            flops=2 * rows * full.size,
            bytes_accessed=2 * full.size + 8 * tokens.size,
            transcendentals=0,
        ),
    )(raw_grad, full, tokens, *ties)


def scatter_kernel(width, steps, lefts, gots, ties, info, *refs):
    turned, outs = refs[-1], refs[lefts + 1 + gots + ties : -1]
    left, right, got = refs[:lefts], refs[lefts], refs[lefts + 1 : lefts + 1 + gots]
    size = steps * width

    @pl.when(pl.program_id(0) == 0)
    def _():
        for k in range(2):
            side = info[1] if k == 0 else 1 - info[1]
            for i in range(steps):
                start = pl.multiple_of((info[2 + i] * 4 + info[0] * 2 + side) * width, width)
                first = 0
                for part in left:
                    block = part[:, pl.ds(start, width)].T
                    row = k * size + i * width
                    turned[row : row + width, first : first + part.shape[0]] = block
                    first += part.shape[0]

    total = matrix_product(turned[...], right[...])
    for k in range(2):
        value = total[k * size : (k + 1) * size]
        if gots:
            value = value + got[k][...].astype(jnp.float32)
        value = value.astype(jnp.bfloat16)
        each = len(outs) // 2
        rows = size // each
        for i in range(each):
            outs[k * each + i][...] = value[i * rows : (i + 1) * rows]


def scatter_call(ring, width, left, right, core, got=(), ties=(), apart=True):
    rows, columns = right.shape
    steps = ring.steps
    each = steps if apart else 1
    if 2 * width % LANES:
        blocks = jnp.concatenate(left, axis=0).reshape(rows, steps, 2, 2, width)
        outs = []
        for k, side in enumerate((ring.side, 1 - ring.side)):
            for i, place in enumerate(ring.places):
                picked = lax.dynamic_slice(
                    blocks, (0, place, core, side, 0), (rows, 1, 1, 1, width)
                )
                total = inner_left(picked.reshape(rows, width), right)
                if got:
                    total = total + got[k][i * width : (i + 1) * width].astype(jnp.float32)
                outs.append(total.astype(jnp.bfloat16))
        if apart:
            return outs[:steps], outs[steps:]
        return [jnp.concatenate(outs[:steps])], [jnp.concatenate(outs[steps:])]
    info = jnp.stack([core, ring.side] + ring.places).astype(jnp.int32)
    tile, tall = 512, steps * width // each
    outs = pl.pallas_call(
        functools.partial(scatter_kernel, width, steps, len(left), len(got), len(ties)),
        grid_spec=pltpu.PrefetchScalarGridSpec(
            num_scalar_prefetch=1,
            grid=(columns // tile,),
            in_specs=[pl.BlockSpec(a.shape, lambda i, info: (0, 0)) for a in left]
            + [pl.BlockSpec((rows, tile), lambda i, info: (0, i))]
            + [pl.BlockSpec((steps * width, tile), lambda i, info: (0, i)) for _ in got]
            + loose(ties),
            out_specs=[pl.BlockSpec((tall, tile), lambda i, info: (0, i))] * (2 * each),
            scratch_shapes=[pltpu.VMEM((2 * steps * width, rows), jnp.bfloat16)],
        ),
        out_shape=[jax.ShapeDtypeStruct((tall, columns), jnp.bfloat16)] * (2 * each),
        compiler_params=pltpu.CompilerParams(vmem_limit_bytes=VMEM_LIMIT),
        cost_estimate=pl.CostEstimate(
            flops=4 * rows * steps * width * columns,
            bytes_accessed=2 * (right.size + rows * 16 * width) + 4 * steps * width * columns,
            transcendentals=0,
        ),
    )(info, *left, right, *got, *ties)
    return outs[:each], outs[each:]


def finish_kernel(chunk, counts, info, *refs):
    count = len(counts)
    totals, others, (gate, up, down) = refs[:count], refs[count:-3], refs[-3:]
    side, width = info[0], gate.shape[0]
    half = gate.shape[1] // 2
    values = []
    for total, chunks in zip(totals, counts):
        mine = total[pl.ds(pl.multiple_of(side * width, width), width), :]
        values += [(mine[:, 3 * j * chunk : 3 * (j + 1) * chunk], side) for j in range(chunks)]
    values += [(other[...], 1 - side) for other in others]
    for j, (value, at) in enumerate(values):
        value = value.astype(jnp.float32)
        start = pl.multiple_of(at * half + j % CHUNKS * chunk, chunk)
        gate[:, pl.ds(start, chunk)] = value[:, :chunk]
        up[:, pl.ds(start, chunk)] = value[:, chunk : 2 * chunk]
        down[pl.ds(start, chunk), :] = value[:, 2 * chunk :].T


def finish_call(ring, chunk, totals, others):
    width, hidden = others[0].shape[0], 2 * CHUNKS * chunk
    counts = [a.shape[1] // (3 * chunk) for a in totals]
    shapes = [(width, hidden), (width, hidden), (hidden, width)]
    whole = [pl.BlockSpec(a.shape, lambda i, info: (0, 0)) for a in (*totals, *others)]
    return pl.pallas_call(
        functools.partial(finish_kernel, chunk, counts),
        grid_spec=pltpu.PrefetchScalarGridSpec(
            num_scalar_prefetch=1,
            grid=(1,),
            in_specs=whole,
            out_specs=[pl.BlockSpec(shape, lambda i, info: (0, 0)) for shape in shapes],
        ),
        out_shape=[jax.ShapeDtypeStruct(shape, jnp.float32) for shape in shapes],
        compiler_params=pltpu.CompilerParams(vmem_limit_bytes=VMEM_LIMIT),
        cost_estimate=pl.CostEstimate(
            flops=0, bytes_accessed=18 * hidden * width, transcendentals=0
        ),
    )(jnp.stack([ring.side]).astype(jnp.int32), *totals, *others)


def join_kernel(width, count, order, left, *rest):
    pieces, (product, whole) = rest[:count], rest[count:]
    for i, piece in enumerate(pieces):
        whole[pl.ds(pl.multiple_of(order[i] * width, width), width), :] = piece[...]
    product[...] = matrix_product(left[...], whole[...])


def join_call(gather, left):
    width, columns = gather.pieces[0].shape
    rows, model_width = left.shape
    tile = columns // 4
    count = len(gather.pieces)
    return pl.pallas_call(
        functools.partial(join_kernel, width, count),
        grid_spec=pltpu.PrefetchScalarGridSpec(
            num_scalar_prefetch=1,
            grid=(columns // tile,),
            in_specs=[pl.BlockSpec((rows, model_width), lambda i, order: (0, 0))]
            + [pl.BlockSpec((width, tile), lambda i, order: (0, i))] * count,
            out_specs=[
                pl.BlockSpec((rows, tile), lambda i, order: (0, i)),
                pl.BlockSpec((model_width, tile), lambda i, order: (0, i)),
            ],
        ),
        out_shape=[
            jax.ShapeDtypeStruct((rows, columns), jnp.float32),
            jax.ShapeDtypeStruct((model_width, columns), jnp.bfloat16),
        ],
        compiler_params=pltpu.CompilerParams(vmem_limit_bytes=VMEM_LIMIT),
        cost_estimate=pl.CostEstimate(
            flops=2 * rows * model_width * columns,
            bytes_accessed=4 * model_width * columns + 4 * rows * columns,
            transcendentals=0,
        ),
    )(jnp.stack(gather.order).astype(jnp.int32), left, *gather.pieces)


def join_wide_kernel(width, count, order, first, second, *rest):
    pieces, mixture, whole = rest[:count], rest[count], rest[count + 1]
    total, outs = rest[-1], rest[count + 2 : -1]
    for i, piece in enumerate(pieces):
        whole[pl.ds(pl.multiple_of(order[i] * width, width), width), :] = piece[...]

    @pl.when(pl.program_id(0) == 0)
    def _():
        mixture[...] = first[...]
        total[...] = inner_right(first[...], whole[...])

    @pl.when(pl.program_id(0) == 1)
    def _():
        mixture[...] = second[...]
        total[...] += inner_right(second[...], whole[...])
        part = outs[0].shape[0]
        for i, out in enumerate(outs):
            out[...] = total[i * part : (i + 1) * part, :].astype(jnp.bfloat16)


def join_wide_call(gather, left):
    width, columns = gather.pieces[0].shape
    rows, model_width = left[0].shape[0], width * len(gather.pieces)
    tile, part = columns // 2, rows // PARTS
    count = len(gather.pieces)
    return pl.pallas_call(
        functools.partial(join_wide_kernel, width, count),
        grid_spec=pltpu.PrefetchScalarGridSpec(
            num_scalar_prefetch=1,
            grid=(2,),
            in_specs=[pl.BlockSpec((rows, tile), lambda i, order: (0, 0))] * 2
            + [pl.BlockSpec((width, tile), lambda i, order: (0, i))] * count,
            out_specs=[
                pl.BlockSpec((rows, tile), lambda i, order: (0, i)),
                pl.BlockSpec((model_width, tile), lambda i, order: (0, i)),
            ]
            + [pl.BlockSpec((part, model_width), lambda i, order: (0, 0))] * PARTS,
            scratch_shapes=[pltpu.VMEM((rows, model_width), jnp.float32)],
        ),
        out_shape=[
            jax.ShapeDtypeStruct((rows, columns), jnp.bfloat16),
            jax.ShapeDtypeStruct((model_width, columns), jnp.bfloat16),
        ]
        + [jax.ShapeDtypeStruct((part, model_width), jnp.bfloat16)] * PARTS,
        compiler_params=pltpu.CompilerParams(vmem_limit_bytes=VMEM_LIMIT),
        cost_estimate=pl.CostEstimate(
            flops=2 * rows * model_width * columns,
            bytes_accessed=4 * model_width * columns + 4 * rows * model_width,
            transcendentals=0,
        ),
    )(jnp.stack(gather.order).astype(jnp.int32), *left, *gather.pieces)


def shards(
    dp_size,
    tokens,
    seq_lengths,
    first_gain,
    query_weight,
    key_matrix,
    value_matrix,
    query_norm_gain,
    key_gain,
    output_weight,
    second_gain,
    gate_weight,
    up_weight,
    down_weight,
    cotangent,
):
    ring = Ring(dp_size)
    steps = ring.steps
    rows, model_width = tokens.shape
    width = query_weight.shape[0]
    key_heads = key_matrix.shape[1] // HEAD_SIZE
    query_columns, key_columns = query_weight.shape[1], key_matrix.shape[1]
    part = rows // PARTS
    tiled = width % LANES == 0
    turned = functools.partial(arrange, steps=steps, width=width)
    turn = turned if tiled else (lambda value: value)
    if not tiled:
        tokens, cotangent = turned(tokens), turned(cotangent)

    hidden_width = gate_weight.shape[1] // 2
    chunk = hidden_width // CHUNKS
    pieces = [ring.pick(w, 1) for w in (gate_weight, up_weight, down_weight.T)]
    feed_mine, feed_other = (
        [
            jnp.concatenate([p[k][:, j * chunk : (j + 1) * chunk] for p in pieces], axis=1)
            for j in range(CHUNKS)
        ]
        for k in range(2)
    )
    feed_full = [None] * CHUNKS

    def feed_gather(j, got):
        block = ring.ordered(feed_mine[j], got, 0)
        feed_full[j] = lax.all_gather(
            block, "dp", axis=0, tiled=True, axis_index_groups=ring.groups
        )

    attention = Gather(ring, jnp.concatenate([query_weight, key_matrix, value_matrix], axis=1))
    output = Gather(ring, output_weight.T)

    live_rows, segment, position = layout(seq_lengths[0], rows)
    cosine_table, sinusoid_table = rotation(position, HEAD_SIZE)
    gain_one = arrange_vector(first_gain.astype(jnp.float32), steps)[None]
    gain_two = arrange_vector(second_gain.astype(jnp.float32), steps)[None]
    tables = (
        jnp.concatenate([cosine_table[:, 0], cosine_table[:, 0]], axis=1),
        jnp.concatenate([-sinusoid_table[:, 0], sinusoid_table[:, 0]], axis=1),
    )
    head_gains = (
        query_norm_gain.astype(jnp.float32)[None],
        key_gain.astype(jnp.float32)[None],
    )
    stages = Stages(jnp.broadcast_to(gain_one[:, :LANES], (8, LANES)) + 0.0)
    settle, step = stages.settle, stages.step
    token_rows, upstream, input_one = row_call(
        functools.partial(first_kernel, turn),
        rows,
        128,
        [
            (tokens, "rows"),
            (cotangent, "rows"),
            (live_rows[:, None].astype(jnp.float32), "rows"),
            (gain_one, "all"),
        ],
        [(model_width, jnp.bfloat16)] * 3,
    )
    for i in range(steps):
        ahead = (output, dict(hop=i != 2, swap=i == 2))
        movers = [attention, ahead]
        if i == 0:
            token_rows, upstream, input_one, tables = step(
                movers, token_rows, upstream, input_one, tables
            )
        elif i == 1:
            (got,) = step(movers, ring.swap_side(feed_other[0]))
            feed_gather(0, got)
        else:
            step(movers)
    step([attention])
    place = lax.axis_index("tensor")
    sent = [
        lax.dynamic_slice_in_dim(upstream, place * (rows // 2) + k * part, part) for k in range(2)
    ]

    late = stages.hold(*feed_other[1:])
    raw, attention_full = step([output], *join_call(attention, input_one))
    half = key_heads // 2
    attend_args = (raw, query_columns, key_columns, head_gains, tables, segment)
    mixture_low = []
    for i in range(2):
        mixed = attention_call(*attend_args, (i * half, half), ties=stages.ties)
        mixed, got = step([output], mixed, [ring.swap_side(late[0])] if i == 0 else [])
        mixture_low.append(mixed)
        if i == 0:
            feed_gather(1, got[0])
    late = stages.hold(*late)
    while not output.done:
        step([output])
    joined, got = settle(
        join_wide_call(output, mixture_low), [ring.swap_side(w) for w in late[1:]]
    )
    mixture_low, output_full, *branch_parts = joined
    for j, value in enumerate(got):
        feed_gather(2 + j, value)

    middle_parts, normed_parts, normed_other = [], [], []
    got = None
    for i in range(PARTS + 1):
        work = []
        if i:
            work = row_call(
                middle_kernel,
                part,
                part,
                [
                    (token_rows, i - 1),
                    (branch_parts[i - 1], "rows"),
                    (got, "rows"),
                    (gain_two, "all"),
                ],
                [(model_width, jnp.float32), (model_width, jnp.bfloat16)],
            )
        if i < PARTS:
            moves = [swap_tensor(branch_parts[i])]
            if i < 2:
                moves.append(ring.swap_side(stages.hold(sent[i])[0]))
            else:
                moves.append(ring.swap_side(normed_parts[i - 2]))
            moves, work, branch_parts = settle(moves, work, branch_parts)
            got = moves[0]
            if i < 2:
                sent[i] = moves[1]
            else:
                normed_other.append(moves[1])
        if i:
            middle_parts.append(work[0])
            normed_parts.append(work[1])
    got = [swap_tensor(v) for v in stages.hold(*sent)]

    span, out_span = (0, 2 * chunk), (2 * chunk, 3 * chunk)
    rest = [ring.swap_side(p) for p in normed_parts[len(normed_other) :]]
    acts = []
    for j in range(CHUNKS - 1):
        act, got, rest[j : j + 1] = settle(
            feed_call(normed_parts, upstream, feed_full[j], stages.ties), got, rest[j : j + 1]
        )
        acts.append(act)
    rest, upstream_other = settle(
        rest, [jnp.where(place == 0, a, b) for a, b in zip(sent + got, got + sent)]
    )
    normed_other += rest
    sides = (normed_parts, normed_other), (upstream, upstream_other)
    acts_other = [feed_call(normed_other, upstream_other, feed_full[0], stages.ties)]
    feed_grads = [grad_call(*sides, (acts[0], acts_other[0]))]
    for j in range(1, CHUNKS):
        acts_other.append(
            feed_call(normed_other, upstream_other, feed_full[j], (feed_grads + acts_other[1:])[-1:])
        )
    back_other = wide_call(acts_other, feed_full, span, jnp.bfloat16)
    last_grads = None
    (acts_last,) = settle(
        feed_call(normed_parts, upstream, feed_full[-1], tuple(back_other[:1]))
    )
    acts.append(acts_last)
    back_other = [back_other[0], *stages.hold(*back_other[1:])]

    back_mine = wide_call(acts, feed_full, span, jnp.float32, ties=stages.ties)
    got, back_mine = settle(ring.swap_side(back_other[0]), back_mine)
    mine = add_low(back_mine[0], got)
    back_parts, low_parts, mixed_parts, grad_second = [], [], [], 0.0
    out_other, out_mine, out_sums, out_got = None, None, [], []

    def back_middle_call(i, mine, other):
        return row_call(
            back_middle_kernel,
            part,
            part,
            [
                (mine, "rows"),
                (other, "rows"),
                (middle_parts[i], "rows"),
                (upstream, i),
                (gain_two, "all"),
                (output_full, "all"),
            ],
            [
                (model_width, jnp.float32),
                (model_width, jnp.bfloat16),
                (query_columns, jnp.bfloat16),
            ],
            [model_width],
            stages.ties,
        )

    for i in range(PARTS):
        work = []
        if i + 1 < CHUNKS:
            last_grads = grad_call(
                *sides,
                (acts[i + 1], acts_other[i + 1]),
                (mine,) + stages.ties,
                i,
                CHUNKS - 1,
                last_grads,
            )
            work = [last_grads]
        if i == PARTS - 2:
            work = [wide_call(acts_other, feed_full, out_span, jnp.bfloat16, ties=(mine,))]
        if i == PARTS - 1:
            work = [wide_call(acts, feed_full, out_span, jnp.float32, ties=(mine,))]
        done = back_middle_call(i - 1, *last) if i else []
        moves = [swap_tensor(mine)]
        if i + 1 < PARTS:
            moves.append(ring.swap_side(back_other[i + 1]))
        if i == PARTS - 1:
            moves.append(ring.swap_side(out_other[0]))
            out_other[2:] = stages.hold(*out_other[2:])
        moves, work, done = settle(moves, work, done)
        back_other[i + 2 :] = stages.hold(*back_other[i + 2 :])
        last = (mine, moves[0])
        if i + 1 < PARTS:
            mine = add_low(back_mine[i + 1], moves[1])
        if i == PARTS - 1:
            out_got.append(moves[-1])
        if i + 1 < CHUNKS:
            last_grads = work[0]
        if i == PARTS - 2:
            out_other = list(work[0])
        if i == PARTS - 1:
            out_mine = work[0]
        if i:
            back_parts.append(done[0])
            low_parts.append(done[1])
            mixed_parts.append(done[2])
            grad_second = grad_second + done[3]
    done = back_middle_call(PARTS - 1, *last)
    back_parts.append(done[0])
    low_parts.append(done[1])
    mixed_parts.append(done[2])
    grad_second = grad_second + done[3]
    feed_grads.append(last_grads)

    scattered = [
        lax.psum_scatter(
            grad, "dp", scatter_dimension=0, tiled=True, axis_index_groups=ring.groups
        )
        for grad in feed_grads
    ]

    core = ring.core
    out_other[2:] = stages.hold(*out_other[2:])
    out_sums = [add_low(out_mine[0], out_got[0])]
    far = scatter_call(
        ring, width, low_parts, mixture_low, 1 - core, ties=stages.ties, apart=False
    )
    (far,) = settle([ring.swap_core(f[0]) for f in far])
    out_other[3:] = stages.hold(*out_other[3:])
    near, across = scatter_call(
        ring, width, low_parts, mixture_low, core, far, stages.ties, apart=False
    )
    def picked(total):
        return lax.dynamic_slice_in_dim(total, (1 - ring.side) * width, width)

    work, scattered[0], got, out_next, pair = settle(
        attention_call(
            *attend_args, (0, key_heads), mixed_parts, stages.ties + tuple(near)
        ),
        scattered[0],
        [ring.swap_side(w) for w in out_other[1:]],
        swap_tensor(out_sums[0]),
        ring.swap_side(picked(*stages.hold(scattered[0]))),
    )
    raw_grad, grad_qgain, grad_kgain = work
    out_sums += [add_low(m, g) for m, g in zip(out_mine[1:], got)]
    out_done = [out_next]
    pairs_got = [pair]
    across = stages.hold(*across)

    far = scatter_call(
        ring, width, [input_one], raw_grad, 1 - core, ties=stages.ties, apart=False
    )
    far, work, out_next = settle(
        [ring.swap_core(f[0]) for f in far],
        back_first_call(
            raw_grad, attention_full, token_rows, stages.ties + (far[0][0],)
        ),
        swap_tensor(out_sums[1]),
    )
    out_done.append(out_next)
    *back_one, grad_first = work
    gains = jnp.concatenate(
        [
            arrange_vector(grad_first[0], steps),
            arrange_vector(grad_second[0], steps) * 0.5,
            grad_qgain[0],
            grad_kgain[0],
        ]
    )
    back_one_other = []
    near_one, across, gains_got = settle(
        scatter_call(ring, width, [input_one], raw_grad, core, far, stages.ties),
        ring.swap_side(across[0]),
        swap_tensor(gains),
    )
    gains = gains + gains_got
    attention_sum = Scatter(ring, *near_one)

    def places_of(value):
        return [value[i * width : (i + 1) * width] for i in range(steps)]

    output_sum = Scatter(ring, places_of(near[0]), None, places_of(across))
    def token_call(first, last, into, ties):
        ins = [
            (back_one[first:last], "parts"),
            (back_one_other[first:last], "parts"),
            (token_rows, first),
            (back_parts[first:last], "parts"),
            (gain_one, "all"),
        ]
        return row_call(
            functools.partial(token_kernel, turn),
            (last - first) * part,
            part,
            ins,
            [(model_width, jnp.float32)],
            ties=ties,
            into=(into, first, rows),
        )[0]

    distance = 1
    token_grad = block_output = None
    for i in range(steps):
        movers = [attention_sum] + ([output_sum] if output_sum.index < steps else [])
        others = []
        if i < PARTS:
            others.append(swap_tensor(*stages.hold(back_one[i])))
        if i < 2:
            others.append(swap_tensor(out_sums[2 + i]))
        if 0 < i < CHUNKS:
            pair = picked(scattered[1])[:, (i - 1) * 3 * chunk : i * 3 * chunk]
            others.append(ring.swap_side(*stages.hold(pair)))
        if i == 2:
            (block_output,) = row_call(
                functools.partial(output_kernel, turn),
                rows,
                128,
                [(middle_parts, "parts"), (out_sums, "parts"), (out_done, "parts")],
                [(model_width, jnp.bfloat16)],
                ties=stages.ties,
            )
            others.append(block_output)
        if i == steps - 1:
            early = len(back_one_other)
            token_grad = token_call(0, early, None, stages.ties)
            grads = finish_call(ring, chunk, scattered, pairs_got)
            others += [token_grad, grads]
        if distance < dp_size:
            others.append(
                lax.ppermute(gains, "dp", [(k, k ^ distance) for k in range(dp_size)])
            )
        others = list(step(movers, *others))
        if distance < dp_size:
            gains = gains + others.pop()
            distance *= 2
        if i == steps - 1:
            grads = others.pop()
            token_grad = others.pop()
        if i == 2:
            block_output = others.pop()
        if 0 < i < CHUNKS:
            pairs_got.append(others.pop())
        if i < 2:
            out_done.append(others.pop())
        if i < PARTS:
            back_one_other.append(others.pop())
    if early < PARTS:
        token_grad = token_call(early, PARTS, token_grad, stages.ties)
    if not tiled:
        token_grad, block_output = turned(token_grad), turned(block_output)
    grad_output = output_sum.total
    grad_attention = attention_sum.total
    grad_query = grad_attention[:, :query_columns]
    grad_key = grad_attention[:, query_columns : query_columns + key_columns]
    grad_value = grad_attention[:, query_columns + key_columns :]

    grad_gate, grad_up, grad_down = grads

    while distance < dp_size:
        gains = gains + lax.ppermute(gains, "dp", [(k, k ^ distance) for k in range(dp_size)])
        distance *= 2
    index = lax.axis_index("dp")

    def own_part(start, size):
        return lax.dynamic_slice_in_dim(gains, start + index * (size // dp_size), size // dp_size)

    return (
        block_output,
        token_grad,
        own_part(0, model_width),
        grad_query,
        grad_key,
        grad_value,
        own_part(2 * model_width, HEAD_SIZE),
        own_part(2 * model_width + HEAD_SIZE, HEAD_SIZE),
        grad_output.T,
        own_part(model_width, model_width),
        grad_gate,
        grad_up,
        grad_down,
    )


def solution(mesh):
    return jax.shard_map(
        functools.partial(shards, mesh.shape["dp"]),
        mesh=mesh,
        in_specs=(
            P("dp", None),
            P("dp", None),
            P(),
            P("dp", "tensor"),
            P("dp", "tensor"),
            P("dp", "tensor"),
            P(),
            P(),
            P("tensor", "dp"),
            P(),
            P("dp", "tensor"),
            P("dp", "tensor"),
            P("tensor", "dp"),
            P("dp", None),
        ),
        out_specs=(
            P("dp", None),
            P("dp", None),
            P("dp"),
            P("dp", "tensor"),
            P("dp", "tensor"),
            P("dp", "tensor"),
            P("dp"),
            P("dp"),
            P("tensor", "dp"),
            P("dp"),
            P("dp", "tensor"),
            P("dp", "tensor"),
            P("tensor", "dp"),
        ),
        check_vma=False,
    )
```

```python
import functools

import jax
import jax.numpy as jnp
from jax import lax
from jax.experimental import pallas as pl
from jax.experimental.pallas import tpu as pltpu
from jax.sharding import PartitionSpec as P

HEAD_SIZE = 128
BLK = 64


epsilon = 1e-06
rope_base = 1000000.0


def matrix_product(left, right):
    return jnp.dot(left, right, preferred_element_type=jnp.float32)


def inner_left(left, right):
    return lax.dot_general(
        left, right, (((0,), (0,)), ((), ())), preferred_element_type=jnp.float32
    )


def inner_right(left, right):
    return lax.dot_general(
        left, right, (((1,), (1,)), ((), ())), preferred_element_type=jnp.float32
    )


def layout(lengths, count_of_rows):
    padded = (lengths + BLK - 1) // BLK * BLK
    starts = jnp.cumsum(padded) - padded
    row_index = jnp.arange(count_of_rows, dtype=jnp.int32)
    inside = (row_index[:, None] >= starts[None, :]) & (
        row_index[:, None] < (starts + lengths)[None, :]
    )
    live_rows = jnp.any(inside, axis=1)
    slot_index = jnp.arange(lengths.shape[0], dtype=jnp.int32)
    owning = jnp.sum(jnp.where(inside, slot_index[None, :], 0), axis=1)
    position = jnp.sum(jnp.where(inside, row_index[:, None] - starts[None, :], 0), axis=1)
    segment = jnp.where(live_rows, owning, -1 - row_index)
    return (live_rows, segment, position)


def rotation(position, width):
    half_width = width // 2
    frequency = jnp.power(rope_base, -(jnp.arange(half_width, dtype=jnp.float32) * 2.0) / width)
    angles = position.astype(jnp.float32)[:, None] * frequency[None, :]
    return (jnp.cos(angles)[:, None, :], jnp.sin(angles)[:, None, :])


CHUNKS = 3
PARTS = 4
LANES = 128
ROW_BLOCK = 256
VMEM_LIMIT = 56 * 1024 * 1024


def add_low(left, right):
    return (left.astype(jnp.float32) + right.astype(jnp.float32)).astype(jnp.bfloat16)


class Ring:
    def __init__(self, size):
        self.size = size
        self.steps = size // 4
        index = lax.axis_index("dp")
        self.place = index // 4
        self.side = (index // 2) % 2
        self.core = index % 2
        self.places = [(self.place - 1 - i) % self.steps for i in range(self.steps)]
        self.groups = [
            [place * 4 + side * 2 + core for place in range(self.steps) for core in range(2)]
            for side in range(2)
        ]

    def swap_core(self, value):
        return lax.ppermute(value, "dp", [(i, i ^ 1) for i in range(self.size)])

    def swap_side(self, value):
        return lax.ppermute(value, "dp", [(i, i ^ 2) for i in range(self.size)])

    def shift(self, value, places):
        return lax.ppermute(
            value, "dp", [(i, (i + 4 * places) % self.size) for i in range(self.size)]
        )

    def pick(self, value, axis):
        low, high = jnp.split(value, 2, axis=axis)
        return (
            jnp.where(self.side == 0, low, high),
            jnp.where(self.side == 0, high, low),
        )

    def ordered(self, mine, other, axis):
        return jnp.where(
            self.side == 0,
            jnp.concatenate([mine, other], axis=axis),
            jnp.concatenate([other, mine], axis=axis),
        )

    def block(self, back, core, side):
        return ((self.place - back) % self.steps) * 4 + core * 2 + side


class Gather:
    def __init__(self, ring, piece):
        self.ring = ring
        self.hops, self.across, self.index = [piece], None, 0
        self.pieces, self.order = [], []

    def put(self, back, core, side, value):
        self.pieces.append(value)
        self.order.append(self.ring.block(back, core, side))

    def start(self, stages, hop=True, swap=True):
        ring, moves = self.ring, {}
        self.hops = list(stages.hold(*self.hops))
        if hop and len(self.hops) < ring.steps:
            moves["hop"] = ring.shift(self.hops[-1], 1)
        if swap and self.index < ring.steps:
            moves["side"] = ring.swap_side(self.hops[self.index])
            moves["core"] = ring.swap_core(self.hops[self.index])
        if swap and self.across is not None:
            moves["both"] = ring.swap_core(self.across)
        return moves

    def finish(self, moves):
        ring, back = self.ring, self.index
        core, side = ring.core, ring.side
        if "hop" in moves:
            self.hops.append(moves["hop"])
        if "both" in moves:
            self.put(back - 1, 1 - core, 1 - side, moves["both"])
            self.across = None
        if "side" in moves:
            self.put(back, core, side, self.hops[back])
            self.put(back, core, 1 - side, moves["side"])
            self.put(back, 1 - core, side, moves["core"])
            self.across = moves["side"]
            self.index += 1

    @property
    def done(self):
        return len(self.pieces) == self.ring.size


class Stages:
    def __init__(self, mark):
        self.mark = mark

    def settle(self, *values):
        values, self.mark = lax.optimization_barrier((values, self.mark))
        return values

    def step(self, movers, *others):
        movers = [mover if isinstance(mover, tuple) else (mover, {}) for mover in movers]
        moves = [mover.start(self, **kind) for mover, kind in movers]
        moves, others = self.settle(moves, others)
        for (mover, _), move in zip(movers, moves):
            mover.finish(move)
        return others

    def hold(self, *values):
        return lax.optimization_barrier((values, self.mark))[0]

    @property
    def ties(self):
        return (self.mark,)


def swap_tensor(value):
    return lax.ppermute(value, "tensor", [(0, 1), (1, 0)])


def arrange(value, steps, width):
    blocks = [value[:, i * width : (i + 1) * width] for i in range(4 * steps)]
    order = [4 * place + k for place in range(steps) for k in (0, 2, 1, 3)]
    return jnp.concatenate([blocks[i] for i in order], axis=1)


def arrange_vector(vector, steps):
    return vector.reshape(steps, 2, 2, -1).swapaxes(1, 2).reshape(-1)


def sums_kernel(kinds, counts, *refs):
    ins, outs = refs[: sum(counts)], list(refs[sum(counts) :])
    for kind, count in zip(kinds, counts):
        group, ins = ins[:count], ins[count:]
        total = group[0][...].astype(jnp.float32)
        for ref in group[1:]:
            total = total + ref[...].astype(jnp.float32)
        if kind == "low":
            outs.pop(0)[...] = total.astype(jnp.bfloat16)
        elif kind == "turned":
            outs.pop(0)[...] = total.T
        elif kind[0] == "open":
            joined = outs.pop(0)
            joined[:, : total.shape[1]] = total.astype(jnp.bfloat16)
        elif kind[0] == "close":
            joined[:, kind[1] : kind[1] + total.shape[1]] = total.astype(jnp.bfloat16)
        else:
            first = 0
            for width in kind:
                outs.pop(0)[...] = total[:, first : first + width]
                first += width


def sums_call(*groups):
    shapes = []
    for kind, arrays in groups:
        rows, columns = arrays[-1][-1] if isinstance(arrays[-1], tuple) else arrays[-1].shape
        if kind[0] == "open":
            shapes.append(jax.ShapeDtypeStruct((rows, kind[1]), jnp.bfloat16))
        elif kind[0] == "close":
            continue
        elif kind == "low":
            shapes.append(jax.ShapeDtypeStruct((rows, columns), jnp.bfloat16))
        elif kind == "turned":
            shapes.append(jax.ShapeDtypeStruct((columns, rows), jnp.float32))
        else:
            shapes += [jax.ShapeDtypeStruct((rows, w), jnp.float32) for w in kind]
    ins, specs = [], []
    for _, arrays in groups:
        shape = arrays[-1][-1] if isinstance(arrays[-1], tuple) else arrays[-1].shape
        for a in arrays:
            a, *block = a if isinstance(a, tuple) else (a, (0, 0))
            ins.append(a)
            specs.append(pl.BlockSpec(shape, lambda i, block=block[0]: block))
    return pl.pallas_call(
        functools.partial(sums_kernel, [k for k, _ in groups], [len(a) for _, a in groups]),
        grid=(1,),
        in_specs=specs,
        out_specs=[pl.BlockSpec(shape.shape, lambda i: (0, 0)) for shape in shapes],
        out_shape=shapes,
        compiler_params=pltpu.CompilerParams(vmem_limit_bytes=VMEM_LIMIT),
        cost_estimate=pl.CostEstimate(
            flops=0, bytes_accessed=4 * sum(a.size for a in ins), transcendentals=0
        ),
    )(*ins)


def loose(ties):
    return [pl.BlockSpec(memory_space=pl.ANY) for _ in ties]


def row_call(kernel, rows, block, ins, outs, sums=(), ties=(), into=None):
    arrays, specs, places, cuts = [], [], [], 1
    for value, kind in ins:
        places.append(len(arrays))
        if kind in ("parts", "halves"):
            if kind == "parts":
                cuts = len(value)
            span = rows // len(value) // block
            for k, piece in enumerate(value):
                arrays.append(piece)
                specs.append(
                    pl.BlockSpec(
                        (block, piece.shape[1]),
                        lambda i, k=k, span=span: (jnp.clip(i - k * span, 0, span - 1), 0),
                    )
                )
            continue
        arrays.append(value)
        if kind == "all":
            specs.append(pl.BlockSpec(value.shape, lambda i: (0, 0)))
        else:
            first = 0 if kind == "rows" else kind
            specs.append(
                pl.BlockSpec((block, value.shape[1]), lambda i, first=first: (first + i, 0))
            )
    base, all_rows, aliases = 0, rows, {}
    count = len(arrays)
    if into is not None:
        given, base, all_rows = into
        if given is not None:
            ties = (given, *ties)
            aliases = {count: 0}
    out_specs = [pl.BlockSpec((block, c), lambda i: (base + i, 0)) for c, _ in outs]
    out_specs += [pl.BlockSpec((1, c), lambda i: (0, 0)) for c in sums]
    out_shape = [jax.ShapeDtypeStruct((all_rows, c), d) for c, d in outs]
    out_shape += [jax.ShapeDtypeStruct((1, c), jnp.float32) for c in sums]
    moved = sum(a.size * a.dtype.itemsize for a in arrays)
    moved += sum(rows * c * jnp.dtype(d).itemsize for c, d in outs)

    def body(*refs):
        given = refs[count + len(ties) :]
        if cuts == 1:
            kernel(*refs[:count], *given)
            return
        turn = pl.program_id(0) // (rows // cuts // block)
        for k in range(cuts):
            chosen = [
                refs[place + k * len(value) // cuts]
                if kind in ("parts", "halves")
                else refs[place]
                for place, (value, kind) in zip(places, ins)
            ]
            pl.when(turn == k)(functools.partial(kernel, *chosen, *given))

    return pl.pallas_call(
        body,
        grid=(rows // block,),
        in_specs=specs + loose(ties),
        out_specs=out_specs,
        out_shape=out_shape,
        input_output_aliases=aliases,
        compiler_params=pltpu.CompilerParams(vmem_limit_bytes=VMEM_LIMIT),
        cost_estimate=pl.CostEstimate(flops=0, bytes_accessed=moved, transcendentals=0),
    )(*arrays, *ties)


def inverse_rms(value):
    return lax.rsqrt(jnp.mean(value * value, axis=-1, keepdims=True) + epsilon)


def first_kernel(turn, tokens, cotangent, live, gain, tokens_out, upstream_out, normed_out):
    value = turn(tokens[...])
    tokens_out[...] = value
    value = value.astype(jnp.float32)
    normed_out[...] = (value * inverse_rms(value) * gain[...]).astype(jnp.bfloat16)
    back = turn(cotangent[...]).astype(jnp.float32)
    upstream_out[...] = (back * live[...]).astype(jnp.bfloat16)


def middle_kernel(tokens, mine, other, gain, middle_out, normed_out):
    branch = mine[...].astype(jnp.float32) + other[...].astype(jnp.float32)
    value = tokens[...].astype(jnp.float32) + branch
    middle_out[...] = value
    normed_out[...] = (value * inverse_rms(value) * gain[...]).astype(jnp.bfloat16)


def back_rms(value, gain, back):
    scale = inverse_rms(value)
    normed = value * scale
    pulled = back * gain
    center = jnp.mean(pulled * normed, axis=-1, keepdims=True)
    return scale * (pulled - normed * center), back * normed


def add_sum(out_ref, value):
    @pl.when(pl.program_id(0) == 0)
    def _():
        out_ref[...] = jnp.zeros_like(out_ref)

    out_ref[...] += jnp.sum(value, axis=0, keepdims=True)


def back_middle_kernel(
    mine, other, middle, upstream, gain, full, back_out, low_out, mixed_out, gain_out
):
    back = mine[...].astype(jnp.float32) + other[...].astype(jnp.float32)
    value, gain_term = back_rms(middle[...], gain[...], back)
    value = value + upstream[...].astype(jnp.float32)
    back_out[...] = value
    low = value.astype(jnp.bfloat16)
    low_out[...] = low
    mixed_out[...] = matrix_product(low, full[...]).astype(jnp.bfloat16)
    add_sum(gain_out, gain_term)


def output_kernel(turn, middle, mine, other, out):
    value = middle[...] + mine[...].astype(jnp.float32) + other[...].astype(jnp.float32)
    out[...] = turn(value).astype(jnp.bfloat16)


def token_kernel(turn, mine, other, tokens, back_middle, gain, out):
    back = mine[...].astype(jnp.float32) + other[...].astype(jnp.float32)
    value, _ = back_rms(tokens[...].astype(jnp.float32), gain[...], back)
    out[...] = turn(value + back_middle[...])


def feed_kernel(chunk, count, many, *refs):
    full, out = refs[count], refs[-1]
    block = out.shape[0]

    def picked(group, step):
        refs_of = refs[group[0] : group[1]]
        if len(refs_of) == 1:
            return refs_of[0][...]
        each = block // refs_of[0].shape[0]
        return jnp.concatenate([r[...] for r in refs_of[step * each : (step + 1) * each]], axis=0)

    def run(step):
        normed, upstream = picked((0, many), step), picked((many, count), step)
        gate = matrix_product(normed, full[:, :chunk])
        up = matrix_product(normed, full[:, chunk : 2 * chunk])
        back = matrix_product(upstream, full[:, 2 * chunk :])
        share = jax.nn.sigmoid(gate)
        active = gate * share
        out[:, :chunk] = (back * up * (share * (1.0 + gate * (1.0 - share)))).astype(jnp.bfloat16)
        out[:, chunk : 2 * chunk] = (back * active).astype(jnp.bfloat16)
        out[:, 2 * chunk :] = (active * up).astype(jnp.bfloat16)

    for step in range(2):
        pl.when(pl.program_id(0) == step)(functools.partial(run, step))


def feed_call(normed, upstream, full, ties=()):
    groups = [g if isinstance(g, list) else [g] for g in (normed, upstream)]
    rows, model_width = sum(a.shape[0] for a in groups[0]), full.shape[0]
    columns = full.shape[1]
    block = rows // 2
    specs = []
    for group in groups:
        if len(group) == 1:
            specs.append(pl.BlockSpec((block, model_width), lambda i: (i, 0)))
        else:
            specs += [pl.BlockSpec(a.shape, lambda i: (0, 0)) for a in group]
    return pl.pallas_call(
        functools.partial(feed_kernel, columns // 3, len(specs), len(groups[0])),
        grid=(2,),
        in_specs=specs + [pl.BlockSpec(full.shape, lambda i: (0, 0))] + loose(ties),
        out_specs=pl.BlockSpec((block, columns), lambda i: (i, 0)),
        out_shape=jax.ShapeDtypeStruct((rows, columns), jnp.bfloat16),
        compiler_params=pltpu.CompilerParams(vmem_limit_bytes=VMEM_LIMIT),
        cost_estimate=pl.CostEstimate(
            flops=2 * rows * model_width * columns,
            bytes_accessed=2 * (2 * rows * model_width + full.size + rows * columns),
            transcendentals=rows * columns // 3,
        ),
    )(*groups[0], *groups[1], full, *ties)


def wide_kernel(count, started, parts, *refs):
    outs, total = refs[-parts:], None
    for act, full in zip(refs[:count], refs[count : 2 * count]):
        term = inner_right(act[...], full[...])
        total = term if total is None else total + term
    if started:
        total = total + refs[2 * count][...]
    part = outs[0].shape[0]
    for i, out in enumerate(outs):
        out[...] = total[i * part : (i + 1) * part].astype(out.dtype)


def wide_call(acts, fulls, span, out_dtype, start=None, ties=(), parts=PARTS):
    lo, hi = span
    size, index = hi - lo, lo // (hi - lo)
    rows, model_width, count = acts[0].shape[0], fulls[0].shape[0], len(acts)
    tile = 512
    ins = list(acts) + list(fulls)
    specs = [pl.BlockSpec((rows, size), lambda i: (0, index))] * count
    specs += [pl.BlockSpec((tile, size), lambda i: (i, index))] * count
    if start is not None:
        ins.append(start)
        specs.append(pl.BlockSpec((rows, tile), lambda i: (0, i)))
    ins += list(ties)
    specs += [pl.BlockSpec(memory_space=pl.ANY) for _ in ties]
    return pl.pallas_call(
        functools.partial(wide_kernel, count, start is not None, parts),
        grid=(model_width // tile,),
        in_specs=specs,
        out_specs=[pl.BlockSpec((rows // parts, tile), lambda i: (0, i))] * parts,
        out_shape=[jax.ShapeDtypeStruct((rows // parts, model_width), out_dtype)] * parts,
        compiler_params=pltpu.CompilerParams(vmem_limit_bytes=VMEM_LIMIT),
        cost_estimate=pl.CostEstimate(
            flops=2 * rows * model_width * size * count,
            bytes_accessed=2 * (rows + model_width) * size * count + rows * model_width * 6,
            transcendentals=0,
        ),
    )(*ins)


def grad_kernel(split, counts, *refs):
    out = refs[-1]
    acts = refs[sum(counts) : sum(counts) + 2]
    first = 0
    total = [0.0, 0.0]
    for group, count in enumerate(counts):
        rows, act = 0, acts[group % 2]
        columns = slice(0, split) if group < 2 else slice(split, None)
        parts = [r[...] for r in refs[first : first + count]]
        left = parts[0] if count == 1 else jnp.concatenate(parts, axis=0)
        total[group // 2] = total[group // 2] + inner_left(left, act[:, columns])
        first += count
    out[:, :split] = total[0].astype(jnp.bfloat16)
    out[:, split:] = total[1].astype(jnp.bfloat16)


def grad_call(normed, upstream, acts, ties=(), place=0, places=1, into=None):
    groups = [g if isinstance(g, list) else [g] for g in (*normed, *upstream)]
    lefts = [a for group in groups for a in group]
    rows, model_width = acts[0].shape[0], lefts[0].shape[1]
    columns = acts[0].shape[1]
    tall = 512
    ins = lefts + list(acts)
    specs = [pl.BlockSpec((a.shape[0], tall), lambda i: (0, i)) for a in lefts]
    specs += [pl.BlockSpec((rows, columns), lambda i: (0, 0))] * 2
    aliases = {}
    if into is not None:
        aliases = {len(ins): 0}
        ins.append(into)
        specs.append(pl.BlockSpec(memory_space=pl.ANY))
    return pl.pallas_call(
        functools.partial(grad_kernel, columns // 3 * 2, [len(g) for g in groups]),
        grid=(model_width // tall,),
        in_specs=specs + loose(ties),
        out_specs=pl.BlockSpec((tall, columns), lambda i: (i, place)),
        out_shape=jax.ShapeDtypeStruct((model_width, places * columns), jnp.bfloat16),
        input_output_aliases=aliases,
        compiler_params=pltpu.CompilerParams(vmem_limit_bytes=VMEM_LIMIT),
        cost_estimate=pl.CostEstimate(
            flops=4 * rows * model_width * columns,
            bytes_accessed=2 * (4 * rows * model_width + 2 * rows * columns + model_width * columns),
            transcendentals=0,
        ),
    )(*ins, *ties)


def norm_rope(raw, gain, cosine, sine):
    scale = inverse_rms(raw)
    normed = raw * scale
    scaled = normed * gain
    return scaled * cosine + pltpu.roll(scaled, HEAD_SIZE // 2, 1) * sine, normed, scale


def back_norm_rope(back, normed, scale, gain, cosine, sine):
    back = back * cosine - pltpu.roll(back, HEAD_SIZE // 2, 1) * sine
    pulled = back * gain
    center = jnp.mean(pulled * normed, axis=-1, keepdims=True)
    return scale * (pulled - normed * center), back * normed


def allowed_pairs(segment_column, segment_row, first, count):
    height = first + count
    key = lax.broadcasted_iota(jnp.int32, (height, count), 0)
    query = lax.broadcasted_iota(jnp.int32, (height, count), 1) + first
    same = segment_column[:height, :] == segment_row[:, first:height]
    return same & (key <= query)


def attend_kernel(
    queries, keys, values, query_gain, key_gain, cosine, sine, seg_column, seg_row, *rest
):
    out, total_out = rest[-2:]
    rows = queries.shape[0]
    cosine, sine = cosine[...], sine[...]
    key = norm_rope(keys[...], key_gain[...], cosine, sine)[0].astype(jnp.bfloat16)
    value = values[...].T.astype(jnp.bfloat16)
    spans = [slice(lo, lo + HEAD_SIZE) for lo in range(0, queries.shape[1], HEAD_SIZE)]
    heads = [
        norm_rope(queries[:, span], query_gain[...], cosine, sine)[0].astype(jnp.bfloat16)
        for span in spans
    ]
    for first in range(0, rows, ROW_BLOCK):
        end = first + ROW_BLOCK
        allowed = allowed_pairs(seg_column, seg_row, first, ROW_BLOCK)
        for k, (span, query) in enumerate(zip(spans, heads)):
            scores = inner_right(key[:end], query[first:end]) * HEAD_SIZE ** (-0.5)
            scores = jnp.where(allowed, scores, -1e30)
            largest = jnp.max(scores, axis=0, keepdims=True)
            raised = jnp.exp(scores - largest)
            total = jnp.sum(raised, axis=0, keepdims=True)
            weights = (raised * (1.0 / total)).astype(jnp.bfloat16)
            mixed = matrix_product(value[:, :end], weights)
            out[first:end, span] = mixed.T.astype(jnp.bfloat16)
            total_out[k : k + 1, first:end] = largest + jnp.log(total)


def attend_back_kernel(
    first_head,
    query_columns,
    key_columns,
    queries,
    keys,
    values,
    query_gain,
    key_gain,
    cosine,
    sine,
    seg_column,
    seg_row,
    totals,
    *rest,
):
    out, query_gain_out, key_gain_out = rest[-3:]
    back_parts = rest[:PARTS]
    head = first_head + pl.program_id(0)
    rows, wide = queries.shape
    scaling = HEAD_SIZE ** (-0.5)
    cosine, sine = cosine[...], sine[...]
    key, key_normed, key_scale = norm_rope(keys[...], key_gain[...], cosine, sine)
    turned = key.T.astype(jnp.bfloat16)
    key = key.astype(jnp.bfloat16)
    value = values[...].astype(jnp.bfloat16)
    back_mixture = jnp.concatenate([b[...] for b in back_parts], axis=0)
    spans = [slice(lo, lo + HEAD_SIZE) for lo in range(0, wide, HEAD_SIZE)]
    heads = [norm_rope(queries[:, span], query_gain[...], cosine, sine) for span in spans]
    back_queries = [[] for _ in spans]
    back_key, back_value = None, None
    for first in range(0, rows, ROW_BLOCK):
        end = first + ROW_BLOCK
        allowed = allowed_pairs(seg_column, seg_row, first, ROW_BLOCK)
        key_term, value_term = 0.0, 0.0
        for k, span in enumerate(spans):
            query = heads[k][0][first:end].astype(jnp.bfloat16)
            back = back_mixture[first:end, span]
            scores = inner_right(key[:end], query) * scaling
            weights = jnp.where(allowed, jnp.exp(scores - totals[k : k + 1, first:end]), 0.0)
            terms = inner_right(value[:end], back) * weights
            value_term = value_term + matrix_product(weights.astype(jnp.bfloat16), back)
            center = jnp.sum(terms, axis=0, keepdims=True)
            back_scores = (terms - weights * center).astype(jnp.bfloat16)
            back_queries[k].append(matrix_product(turned[:, :end], back_scores).T * scaling)
            key_term = key_term + matrix_product(back_scores, query) * scaling
        if back_key is None:
            back_key, back_value = key_term, value_term
        else:
            back_key = jnp.concatenate([back_key + key_term[:first], key_term[first:]], axis=0)
            back_value = jnp.concatenate(
                [back_value + value_term[:first], value_term[first:]], axis=0
            )
    query_term = 0.0
    for k, (lo, (_, normed, scale)) in enumerate(zip(range(0, wide, HEAD_SIZE), heads)):
        back_query, term = back_norm_rope(
            jnp.concatenate(back_queries[k], axis=0), normed, scale, query_gain[...], cosine, sine
        )
        query_term = query_term + term
        start = pl.multiple_of(head * wide + lo, HEAD_SIZE)
        out[:, pl.ds(start, HEAD_SIZE)] = back_query.astype(jnp.bfloat16)
    back_key, key_sum = back_norm_rope(
        back_key, key_normed, key_scale, key_gain[...], cosine, sine
    )
    start = pl.multiple_of(query_columns + head * HEAD_SIZE, HEAD_SIZE)
    out[:, pl.ds(start, HEAD_SIZE)] = back_key.astype(jnp.bfloat16)
    start = pl.multiple_of(query_columns + key_columns + head * HEAD_SIZE, HEAD_SIZE)
    out[:, pl.ds(start, HEAD_SIZE)] = back_value.astype(jnp.bfloat16)
    add_sum(query_gain_out, query_term)
    add_sum(key_gain_out, key_sum)


def attention_call(raw, query_columns, key_columns, gains, tables, segment, heads, back=None, totals=None, ties=()):
    rows, columns = raw.shape
    first, count = heads
    wide = query_columns * HEAD_SIZE // key_columns
    first_key = query_columns // HEAD_SIZE + first
    first_value = first_key + key_columns // HEAD_SIZE
    ins = [raw, raw, raw, *gains, *tables, segment[:, None], segment[None, :]]
    specs = [
        pl.BlockSpec((rows, wide), lambda h: (0, first + h)),
        pl.BlockSpec((rows, HEAD_SIZE), lambda h: (0, first_key + h)),
        pl.BlockSpec((rows, HEAD_SIZE), lambda h: (0, first_value + h)),
    ] + [pl.BlockSpec(a.shape, lambda h: (0, 0)) for a in ins[3:]]
    params = dict(
        grid=(count,),
        compiler_params=pltpu.CompilerParams(vmem_limit_bytes=VMEM_LIMIT),
    )
    pairs = count * wide // HEAD_SIZE * rows * rows
    if back is None:
        return pl.pallas_call(
            attend_kernel,
            in_specs=specs + loose(ties),
            out_specs=[
                pl.BlockSpec((rows, wide), lambda h: (0, h)),
                pl.BlockSpec((8, rows), lambda h: (h, 0)),
            ],
            out_shape=[
                jax.ShapeDtypeStruct((rows, count * wide), jnp.bfloat16),
                jax.ShapeDtypeStruct((count * 8, rows), jnp.float32),
            ],
            cost_estimate=pl.CostEstimate(
                flops=4 * pairs * HEAD_SIZE, bytes_accessed=5 * raw.size, transcendentals=pairs
            ),
            **params,
        )(*ins, *ties)
    gain_spec = pl.BlockSpec((1, HEAD_SIZE), lambda h: (0, 0))
    gain_shape = jax.ShapeDtypeStruct((1, HEAD_SIZE), jnp.float32)
    return pl.pallas_call(
        functools.partial(attend_back_kernel, first, query_columns, key_columns),
        in_specs=specs
        + [pl.BlockSpec((8, rows), lambda h: (h, 0))]
        + [pl.BlockSpec((b.shape[0], wide), lambda h: (0, first + h)) for b in back]
        + loose(ties),
        out_specs=[pl.BlockSpec((rows, columns), lambda h: (0, 0)), gain_spec, gain_spec],
        out_shape=[jax.ShapeDtypeStruct((rows, columns), jnp.bfloat16), gain_shape, gain_shape],
        cost_estimate=pl.CostEstimate(
            flops=12 * pairs * HEAD_SIZE, bytes_accessed=8 * raw.size, transcendentals=pairs
        ),
        **params,
    )(*ins, totals, *back, *ties)


def back_first_kernel(raw_grad, full, tokens, *rest):
    outs, gain_out, scale = rest[-2 - PARTS : -2], rest[-2], rest[-1]
    part, tile = outs[0].shape

    @pl.when(pl.program_id(0) == 0)
    def _():
        scale[...] = inverse_rms(tokens[...].astype(jnp.float32))

    back = inner_right(raw_grad[...], full[...])
    for i, out in enumerate(outs):
        out[...] = back[i * part : (i + 1) * part].astype(jnp.bfloat16)
    start = pl.multiple_of(pl.program_id(0) * tile, tile)
    normed = tokens[:, pl.ds(start, tile)].astype(jnp.float32) * scale[...]
    gain_out[...] = jnp.sum(back * normed, axis=0, keepdims=True)


def back_first_call(raw_grad, full, tokens, ties=()):
    rows, model_width = tokens.shape
    tile, part = 512, rows // PARTS
    return pl.pallas_call(
        back_first_kernel,
        grid=(model_width // tile,),
        in_specs=[
            pl.BlockSpec(raw_grad.shape, lambda i: (0, 0)),
            pl.BlockSpec((tile, full.shape[1]), lambda i: (i, 0)),
            pl.BlockSpec(tokens.shape, lambda i: (0, 0)),
        ]
        + [pl.BlockSpec(memory_space=pl.ANY) for _ in ties],
        out_specs=[pl.BlockSpec((part, tile), lambda i: (0, i))] * PARTS
        + [pl.BlockSpec((1, tile), lambda i: (0, i))],
        out_shape=[jax.ShapeDtypeStruct((part, model_width), jnp.bfloat16)] * PARTS
        + [jax.ShapeDtypeStruct((1, model_width), jnp.float32)],
        scratch_shapes=[pltpu.VMEM((rows, 1), jnp.float32)],
        compiler_params=pltpu.CompilerParams(vmem_limit_bytes=VMEM_LIMIT),
        cost_estimate=pl.CostEstimate(
            flops=2 * rows * full.size,
            bytes_accessed=2 * full.size + 8 * tokens.size,
            transcendentals=0,
        ),
    )(raw_grad, full, tokens, *ties)


def scatter_kernel(width, steps, lefts, gots, ties, info, *refs):
    turned, outs = refs[-1], refs[lefts + 1 + gots + ties : -1]
    left, right, got = refs[:lefts], refs[lefts], refs[lefts + 1 : lefts + 1 + gots]
    size = steps * width

    @pl.when(pl.program_id(0) == 0)
    def _():
        for k in range(2):
            side = info[1] if k == 0 else 1 - info[1]
            for i in range(steps):
                start = pl.multiple_of((info[2 + i] * 4 + info[0] * 2 + side) * width, width)
                first = 0
                for part in left:
                    block = part[:, pl.ds(start, width)].T
                    row = k * size + i * width
                    turned[row : row + width, first : first + part.shape[0]] = block
                    first += part.shape[0]

    total = matrix_product(turned[...], right[...])
    for k in range(2):
        value = total[k * size : (k + 1) * size]
        if gots:
            value = value + got[k][...].astype(jnp.float32)
        value = value.astype(jnp.bfloat16)
        each = len(outs) // 2
        rows = size // each
        for i in range(each):
            outs[k * each + i][...] = value[i * rows : (i + 1) * rows]


def scatter_call(ring, width, left, right, core, got=(), ties=(), apart=True):
    rows, columns = right.shape
    steps = ring.steps
    each = steps if apart else 1
    if 2 * width % LANES:
        blocks = jnp.concatenate(left, axis=0).reshape(rows, steps, 2, 2, width)
        outs = []
        for k, side in enumerate((ring.side, 1 - ring.side)):
            for i, place in enumerate(ring.places):
                picked = lax.dynamic_slice(
                    blocks, (0, place, core, side, 0), (rows, 1, 1, 1, width)
                )
                total = inner_left(picked.reshape(rows, width), right)
                if got:
                    total = total + got[k][i * width : (i + 1) * width].astype(jnp.float32)
                outs.append(total.astype(jnp.bfloat16))
        if apart:
            return outs[:steps], outs[steps:]
        return [jnp.concatenate(outs[:steps])], [jnp.concatenate(outs[steps:])]
    info = jnp.stack([core, ring.side] + ring.places).astype(jnp.int32)
    tile, tall = 512, steps * width // each
    outs = pl.pallas_call(
        functools.partial(scatter_kernel, width, steps, len(left), len(got), len(ties)),
        grid_spec=pltpu.PrefetchScalarGridSpec(
            num_scalar_prefetch=1,
            grid=(columns // tile,),
            in_specs=[pl.BlockSpec(a.shape, lambda i, info: (0, 0)) for a in left]
            + [pl.BlockSpec((rows, tile), lambda i, info: (0, i))]
            + [pl.BlockSpec((steps * width, tile), lambda i, info: (0, i)) for _ in got]
            + loose(ties),
            out_specs=[pl.BlockSpec((tall, tile), lambda i, info: (0, i))] * (2 * each),
            scratch_shapes=[pltpu.VMEM((2 * steps * width, rows), jnp.bfloat16)],
        ),
        out_shape=[jax.ShapeDtypeStruct((tall, columns), jnp.bfloat16)] * (2 * each),
        compiler_params=pltpu.CompilerParams(vmem_limit_bytes=VMEM_LIMIT),
        cost_estimate=pl.CostEstimate(
            flops=4 * rows * steps * width * columns,
            bytes_accessed=2 * (right.size + rows * 16 * width) + 4 * steps * width * columns,
            transcendentals=0,
        ),
    )(info, *left, right, *got, *ties)
    return outs[:each], outs[each:]


def finish_kernel(chunk, counts, info, *refs):
    count = len(counts)
    totals, others, (gate, up, down) = refs[:count], refs[count:-3], refs[-3:]
    side, width = info[0], gate.shape[0]
    half = gate.shape[1] // 2
    values = []
    for total, chunks in zip(totals, counts):
        mine = total[pl.ds(pl.multiple_of(side * width, width), width), :]
        values += [(mine[:, 3 * j * chunk : 3 * (j + 1) * chunk], side) for j in range(chunks)]
    values += [(other[...], 1 - side) for other in others]
    for j, (value, at) in enumerate(values):
        value = value.astype(jnp.float32)
        start = pl.multiple_of(at * half + j % CHUNKS * chunk, chunk)
        gate[:, pl.ds(start, chunk)] = value[:, :chunk]
        up[:, pl.ds(start, chunk)] = value[:, chunk : 2 * chunk]
        down[pl.ds(start, chunk), :] = value[:, 2 * chunk :].T


def finish_last_kernel(chunk, info, other, _gate, _up, _down, gate, up, down):
    value = other[...].astype(jnp.float32)
    gate[...] = value[:, :chunk]
    up[...] = value[:, chunk : 2 * chunk]
    down[...] = value[:, 2 * chunk :].T


def finish_call(ring, chunk, totals, others, into=None):
    width, hidden = others[0].shape[0], 2 * CHUNKS * chunk
    shapes = [(width, hidden), (width, hidden), (hidden, width)]
    if into is None:
        counts = [a.shape[1] // (3 * chunk) for a in totals]
        kernel = functools.partial(finish_kernel, chunk, counts)
        ins = [*totals, *others]
        specs = [pl.BlockSpec(a.shape, lambda i, info: (0, 0)) for a in ins]
        out_specs = [pl.BlockSpec(shape, lambda i, info: (0, 0)) for shape in shapes]
        aliases = {}
    else:
        kernel = functools.partial(finish_last_kernel, chunk)
        ins = [*others, *into]
        specs = [pl.BlockSpec(others[0].shape, lambda i, info: (0, 0))] + loose(into)
        last = lambda info: (1 - info[0]) * CHUNKS + CHUNKS - 1
        out_specs = [pl.BlockSpec((width, chunk), lambda i, info: (0, last(info)))] * 2
        out_specs.append(pl.BlockSpec((chunk, width), lambda i, info: (last(info), 0)))
        aliases = {2: 0, 3: 1, 4: 2}
    return pl.pallas_call(
        kernel,
        grid_spec=pltpu.PrefetchScalarGridSpec(
            num_scalar_prefetch=1, grid=(1,), in_specs=specs, out_specs=out_specs
        ),
        out_shape=[jax.ShapeDtypeStruct(shape, jnp.float32) for shape in shapes],
        input_output_aliases=aliases,
        compiler_params=pltpu.CompilerParams(vmem_limit_bytes=VMEM_LIMIT),
        cost_estimate=pl.CostEstimate(
            flops=0, bytes_accessed=18 * hidden * width, transcendentals=0
        ),
    )(jnp.stack([ring.side]).astype(jnp.int32), *ins)


def join_kernel(width, count, order, left, *rest):
    pieces, (product, whole) = rest[:count], rest[count:]
    for i, piece in enumerate(pieces):
        whole[pl.ds(pl.multiple_of(order[i] * width, width), width), :] = piece[...]
    product[...] = matrix_product(left[...], whole[...])


def join_call(gather, left):
    width, columns = gather.pieces[0].shape
    rows, model_width = left.shape
    tile = columns // 4
    count = len(gather.pieces)
    return pl.pallas_call(
        functools.partial(join_kernel, width, count),
        grid_spec=pltpu.PrefetchScalarGridSpec(
            num_scalar_prefetch=1,
            grid=(columns // tile,),
            in_specs=[pl.BlockSpec((rows, model_width), lambda i, order: (0, 0))]
            + [pl.BlockSpec((width, tile), lambda i, order: (0, i))] * count,
            out_specs=[
                pl.BlockSpec((rows, tile), lambda i, order: (0, i)),
                pl.BlockSpec((model_width, tile), lambda i, order: (0, i)),
            ],
        ),
        out_shape=[
            jax.ShapeDtypeStruct((rows, columns), jnp.float32),
            jax.ShapeDtypeStruct((model_width, columns), jnp.bfloat16),
        ],
        compiler_params=pltpu.CompilerParams(vmem_limit_bytes=VMEM_LIMIT),
        cost_estimate=pl.CostEstimate(
            flops=2 * rows * model_width * columns,
            bytes_accessed=4 * model_width * columns + 4 * rows * columns,
            transcendentals=0,
        ),
    )(jnp.stack(gather.order).astype(jnp.int32), left, *gather.pieces)


def join_wide_kernel(width, count, order, first, second, *rest):
    pieces, mixture, whole = rest[:count], rest[count], rest[count + 1]
    total, outs = rest[-1], rest[count + 2 : -1]
    for i, piece in enumerate(pieces):
        whole[pl.ds(pl.multiple_of(order[i] * width, width), width), :] = piece[...]

    @pl.when(pl.program_id(0) == 0)
    def _():
        mixture[...] = first[...]
        total[...] = inner_right(first[...], whole[...])

    @pl.when(pl.program_id(0) == 1)
    def _():
        mixture[...] = second[...]
        total[...] += inner_right(second[...], whole[...])
        part = outs[0].shape[0]
        for i, out in enumerate(outs):
            out[...] = total[i * part : (i + 1) * part, :].astype(jnp.bfloat16)


def join_wide_call(gather, left):
    width, columns = gather.pieces[0].shape
    rows, model_width = left[0].shape[0], width * len(gather.pieces)
    tile, part = columns // 2, rows // PARTS
    count = len(gather.pieces)
    return pl.pallas_call(
        functools.partial(join_wide_kernel, width, count),
        grid_spec=pltpu.PrefetchScalarGridSpec(
            num_scalar_prefetch=1,
            grid=(2,),
            in_specs=[pl.BlockSpec((rows, tile), lambda i, order: (0, 0))] * 2
            + [pl.BlockSpec((width, tile), lambda i, order: (0, i))] * count,
            out_specs=[
                pl.BlockSpec((rows, tile), lambda i, order: (0, i)),
                pl.BlockSpec((model_width, tile), lambda i, order: (0, i)),
            ]
            + [pl.BlockSpec((part, model_width), lambda i, order: (0, 0))] * PARTS,
            scratch_shapes=[pltpu.VMEM((rows, model_width), jnp.float32)],
        ),
        out_shape=[
            jax.ShapeDtypeStruct((rows, columns), jnp.bfloat16),
            jax.ShapeDtypeStruct((model_width, columns), jnp.bfloat16),
        ]
        + [jax.ShapeDtypeStruct((part, model_width), jnp.bfloat16)] * PARTS,
        compiler_params=pltpu.CompilerParams(vmem_limit_bytes=VMEM_LIMIT),
        cost_estimate=pl.CostEstimate(
            flops=2 * rows * model_width * columns,
            bytes_accessed=4 * model_width * columns + 4 * rows * model_width,
            transcendentals=0,
        ),
    )(jnp.stack(gather.order).astype(jnp.int32), *left, *gather.pieces)


def shards(
    dp_size,
    tokens,
    seq_lengths,
    first_gain,
    query_weight,
    key_matrix,
    value_matrix,
    query_norm_gain,
    key_gain,
    output_weight,
    second_gain,
    gate_weight,
    up_weight,
    down_weight,
    cotangent,
):
    ring = Ring(dp_size)
    steps = ring.steps
    rows, model_width = tokens.shape
    width = query_weight.shape[0]
    key_heads = key_matrix.shape[1] // HEAD_SIZE
    query_columns, key_columns = query_weight.shape[1], key_matrix.shape[1]
    part = rows // PARTS
    tiled = width % LANES == 0
    turned = functools.partial(arrange, steps=steps, width=width)
    turn = turned if tiled else (lambda value: value)
    if not tiled:
        tokens, cotangent = turned(tokens), turned(cotangent)

    hidden_width = gate_weight.shape[1] // 2
    chunk = hidden_width // CHUNKS
    pieces = [ring.pick(w, 1) for w in (gate_weight, up_weight, down_weight.T)]
    feed_mine, feed_other = (
        [
            jnp.concatenate([p[k][:, j * chunk : (j + 1) * chunk] for p in pieces], axis=1)
            for j in range(CHUNKS)
        ]
        for k in range(2)
    )
    feed_full = [None] * CHUNKS

    def feed_gather(j, got):
        block = ring.ordered(feed_mine[j], got, 0)
        feed_full[j] = lax.all_gather(
            block, "dp", axis=0, tiled=True, axis_index_groups=ring.groups
        )

    attention = Gather(ring, jnp.concatenate([query_weight, key_matrix, value_matrix], axis=1))
    output = Gather(ring, output_weight.T)

    live_rows, segment, position = layout(seq_lengths[0], rows)
    cosine_table, sinusoid_table = rotation(position, HEAD_SIZE)
    gain_one = arrange_vector(first_gain.astype(jnp.float32), steps)[None]
    gain_two = arrange_vector(second_gain.astype(jnp.float32), steps)[None]
    tables = (
        jnp.concatenate([cosine_table[:, 0], cosine_table[:, 0]], axis=1),
        jnp.concatenate([-sinusoid_table[:, 0], sinusoid_table[:, 0]], axis=1),
    )
    head_gains = (
        query_norm_gain.astype(jnp.float32)[None],
        key_gain.astype(jnp.float32)[None],
    )
    stages = Stages(jnp.broadcast_to(gain_one[:, :LANES], (8, LANES)) + 0.0)
    settle, step = stages.settle, stages.step
    token_rows, upstream, input_one = row_call(
        functools.partial(first_kernel, turn),
        rows,
        128,
        [
            (tokens, "rows"),
            (cotangent, "rows"),
            (live_rows[:, None].astype(jnp.float32), "rows"),
            (gain_one, "all"),
        ],
        [(model_width, jnp.bfloat16)] * 3,
    )
    for i in range(steps):
        movers = [attention]
        if i != 2:
            movers.append((output, dict(swap=i > 2)))
        others = []
        if i in (1, 2):
            others.append(ring.swap_side(*stages.hold(feed_other[i - 1])))
        if i == 0:
            others = [token_rows, upstream, input_one, tables]
        others = step(movers, *others)
        if i == 0:
            token_rows, upstream, input_one, tables = others
        if i in (1, 2):
            feed_gather(i - 1, others[0])
    step([attention])
    place = lax.axis_index("tensor")
    sent = [
        lax.dynamic_slice_in_dim(upstream, place * (rows // 2) + k * part, part) for k in range(2)
    ]

    late = stages.hold(*feed_other[2:])
    raw, attention_full = step([output], *join_call(attention, input_one))
    half = key_heads // 2
    attend_args = (raw, query_columns, key_columns, head_gains, tables, segment)
    mixture_low, row_totals = [], []
    for i in range(2):
        mixed = attention_call(*attend_args, (i * half, half), ties=stages.ties)
        mixed, got = step([output], mixed, [ring.swap_side(w) for w in late] if i == 0 else [])
        mixture_low.append(mixed[0])
        row_totals.append(mixed[1])
        for j, value in enumerate(got):
            feed_gather(2 + j, value)
    while not output.done:
        step([output])
    mixture_low, output_full, *branch_parts = join_wide_call(output, mixture_low)

    middle_parts, normed_parts, normed_other = [], [], []
    got = None
    for i in range(PARTS + 1):
        work = []
        if i:
            work = row_call(
                middle_kernel,
                part,
                part,
                [
                    (token_rows, i - 1),
                    (branch_parts[i - 1], "rows"),
                    (got, "rows"),
                    (gain_two, "all"),
                ],
                [(model_width, jnp.float32), (model_width, jnp.bfloat16)],
            )
        if i < PARTS:
            moves = [swap_tensor(branch_parts[i])]
            if i < 2:
                moves.append(ring.swap_side(stages.hold(sent[i])[0]))
            else:
                moves.append(ring.swap_side(normed_parts[i - 2]))
            moves, work, branch_parts = settle(moves, work, branch_parts)
            got = moves[0]
            if i < 2:
                sent[i] = moves[1]
            else:
                normed_other.append(moves[1])
        if i:
            middle_parts.append(work[0])
            normed_parts.append(work[1])
    got = [swap_tensor(v) for v in stages.hold(*sent)]

    span, out_span = (0, 2 * chunk), (2 * chunk, 3 * chunk)
    rest = [ring.swap_side(p) for p in normed_parts[len(normed_other) :]]
    acts = []
    for j in range(CHUNKS - 1):
        act, rest[j : j + 1], there = settle(
            feed_call(normed_parts, upstream, feed_full[j], stages.ties),
            rest[j : j + 1],
            got if j == CHUNKS - 2 else [],
        )
        acts.append(act)
    got = there
    rest, upstream_other = settle(
        rest, [jnp.where(place == 0, a, b) for a, b in zip(sent + got, got + sent)]
    )
    normed_other += rest
    sides = (normed_parts, normed_other), (upstream, upstream_other)
    acts_other = [feed_call(normed_other, upstream_other, feed_full[0], stages.ties)]
    feed_grads = [grad_call(*sides, (acts[0], acts_other[0]))]
    for j in range(1, CHUNKS):
        acts_other.append(
            feed_call(normed_other, upstream_other, feed_full[j], (feed_grads + acts_other[1:])[-1:])
        )
    back_other = wide_call(acts_other, feed_full, span, jnp.bfloat16)
    last_grads = None
    (acts_last,) = settle(
        feed_call(normed_parts, upstream, feed_full[-1], tuple(back_other[:1]))
    )
    acts.append(acts_last)
    back_other = [back_other[0], *stages.hold(*back_other[1:])]

    back_mine = wide_call(acts, feed_full, span, jnp.float32, ties=stages.ties)
    got, back_mine = settle(ring.swap_side(back_other[0]), back_mine)
    mine = add_low(back_mine[0], got)
    back_parts, low_parts, mixed_parts, grad_second = [], [], [], 0.0
    out_other, out_mine, out_sums, out_got = None, None, [], []

    def back_middle_call(i, mine, other):
        return row_call(
            back_middle_kernel,
            part,
            part,
            [
                (mine, "rows"),
                (other, "rows"),
                (middle_parts[i], "rows"),
                (upstream, i),
                (gain_two, "all"),
                (output_full, "all"),
            ],
            [
                (model_width, jnp.float32),
                (model_width, jnp.bfloat16),
                (query_columns, jnp.bfloat16),
            ],
            [model_width],
            stages.ties,
        )

    for i in range(PARTS):
        work = []
        if i + 1 < CHUNKS:
            last_grads = grad_call(
                *sides,
                (acts[i + 1], acts_other[i + 1]),
                (mine,) + stages.ties,
                i,
                CHUNKS - 1,
                last_grads,
            )
            work = [last_grads]
        if i == PARTS - 2:
            work = [
                wide_call(acts_other, feed_full, out_span, jnp.bfloat16, ties=(mine,), parts=2)
            ]
        if i == PARTS - 1:
            work = [wide_call(acts, feed_full, out_span, jnp.float32, ties=(mine,), parts=2)]
        done = back_middle_call(i - 1, *last) if i else []
        moves = [swap_tensor(mine)]
        if i + 1 < PARTS:
            moves.append(ring.swap_side(back_other[i + 1]))
        moves, work, done = settle(moves, work, done)
        back_other[i + 2 :] = stages.hold(*back_other[i + 2 :])
        last = (mine, moves[0])
        if i + 1 < PARTS:
            mine = add_low(back_mine[i + 1], moves[1])
        if i + 1 < CHUNKS:
            last_grads = work[0]
        if i == PARTS - 2:
            out_other = list(work[0])
        if i == PARTS - 1:
            out_mine = work[0]
        if i:
            back_parts.append(done[0])
            low_parts.append(done[1])
            mixed_parts.append(done[2])
            grad_second = grad_second + done[3]
    done = back_middle_call(PARTS - 1, *last)
    back_parts.append(done[0])
    low_parts.append(done[1])
    mixed_parts.append(done[2])
    grad_second = grad_second + done[3]
    feed_grads.append(last_grads)

    scattered = [
        lax.psum_scatter(
            grad, "dp", scatter_dimension=0, tiled=True, axis_index_groups=ring.groups
        )
        for grad in feed_grads
    ]

    core = ring.core
    far = scatter_call(
        ring, width, low_parts, mixture_low, 1 - core, ties=stages.ties, apart=False
    )
    (got,) = settle(ring.swap_side(out_other[0]))
    (held,) = stages.hold(out_other[1])
    out_sums = [add_low(out_mine[0], got)]

    def picked(total):
        return lax.dynamic_slice_in_dim(total, (1 - ring.side) * width, width)

    work, scattered[0], far, got, out_next = settle(
        attention_call(
            *attend_args,
            (0, key_heads),
            mixed_parts,
            jnp.concatenate(row_totals, axis=0),
            stages.ties + (far[0][0],),
        ),
        scattered[0],
        [ring.swap_core(f[0]) for f in far],
        ring.swap_side(held),
        swap_tensor(out_sums[0]),
    )
    raw_grad, grad_qgain, grad_kgain = work
    out_sums.append(add_low(out_mine[1], got))
    out_done = [out_next]
    far_one = scatter_call(
        ring, width, [input_one], raw_grad, 1 - core, ties=stages.ties, apart=False
    )
    (near,), across = scatter_call(
        ring,
        width,
        low_parts,
        mixture_low,
        core,
        far,
        stages.ties + (far_one[0][0],),
        apart=False,
    )
    far_one, near, pair = settle(
        [ring.swap_core(f[0]) for f in far_one],
        near,
        ring.swap_side(*stages.hold(picked(scattered[0]))),
    )
    pairs_got = [pair]
    ((mine, other),) = settle(
        scatter_call(ring, width, [input_one], raw_grad, core, far_one, stages.ties)
    )
    *back_one, grad_first = back_first_call(raw_grad, attention_full, token_rows, stages.ties)
    gains = jnp.concatenate(
        [
            arrange_vector(grad_first[0], steps),
            arrange_vector(grad_second[0], steps) * 0.5,
            grad_qgain[0],
            grad_kgain[0],
        ]
    )
    back_one_other = []
    distances = [1] + [4 * 2**k for k in range((steps - 1).bit_length())] + [2]

    def gains_sum(value, chosen):
        for distance in chosen:
            value = value + lax.ppermute(
                value, "dp", [(k, k ^ distance) for k in range(dp_size)]
            )
        return value

    def token_call(first, last, into, ties):
        ins = [
            (back_one[first:last], "parts"),
            (back_one_other[first:last], "parts"),
            (token_rows, first),
            (back_parts[first:last], "parts"),
            (gain_one, "all"),
        ]
        return row_call(
            functools.partial(token_kernel, turn),
            (last - first) * part,
            part,
            ins,
            [(model_width, jnp.float32)],
            ties=ties,
            into=(into, first, rows),
        )[0]

    token_grad = block_output = None
    sizes = (width, raw_grad.shape[1]), (width, query_columns)
    joined_columns = sizes[0][1] + sizes[1][1]
    sent = None
    for i in range(steps):
        moves = [ring.swap_side(*stages.hold(other[i]))]
        if i == 0:
            moves.append(ring.swap_side(across[0]))
        else:
            moves.append(ring.shift(sent, 1))
        others = []
        turns = [i] if i < PARTS else []
        others.append([swap_tensor(back_one[k]) for k in turns])
        k = i - (steps - CHUNKS + 1)
        if k >= 0:
            last_pair = picked(scattered[1])[:, k * 3 * chunk : (k + 1) * 3 * chunk]
            others.append(ring.swap_side(*stages.hold(last_pair)))
        if i == 1:
            (block_output,) = row_call(
                functools.partial(output_kernel, turn),
                rows,
                128,
                [(middle_parts, "parts"), (out_sums, "halves"), (out_done, "halves")],
                [(model_width, jnp.bfloat16)],
                ties=stages.ties,
            )
            others.append(block_output)
        if i == steps - 1:
            early = len(back_one_other)
            token_grad = token_call(0, early, None, stages.ties)
            others.append(token_grad)
            others.append(finish_call(ring, chunk, scattered, pairs_got))
        if i == 0:
            others.append(swap_tensor(out_sums[1]))
        if i < 2:
            others.append(gains_sum(gains, distances[:-1] if i == 0 else distances[-1:]))
        if i == steps - 1:
            others.append(gains + swap_tensor(gains))
        moves, others = settle(moves, others)
        others = list(others)
        side, hop = moves
        if i == 0:
            across, group, late = hop, [mine[0], side], [(near, (0, 0)), (hop, (0, 0), sizes[1])]
        else:
            group = [mine[i], (hop, (0, 0)), side]
            late = [
                (near, (i, 0)),
                (across, (i, 0)),
                (hop, (0, sizes[0][1] // sizes[1][1]), sizes[1]),
            ]
        if i < steps - 1:
            (sent,) = sums_call(
                (("open", joined_columns), group), (("close", sizes[0][1]), late)
            )
        else:
            grad_query, grad_key, grad_value, grad_output = sums_call(
                ((query_columns, key_columns, key_columns), group), ("turned", late)
            )
        if i < 2 or i == steps - 1:
            gains = others.pop()
        if i == 0:
            out_done.append(others.pop())
        if i == steps - 1:
            grads = others.pop()
            token_grad = others.pop()
        if i == 1:
            block_output = others.pop()
        if k >= 0:
            pairs_got.append(others.pop())
        back_one_other += others.pop()
    if early < PARTS:
        token_grad = token_call(early, PARTS, token_grad, stages.ties)
    grads = finish_call(ring, chunk, None, pairs_got[-1:], grads)
    if not tiled:
        token_grad, block_output = turned(token_grad), turned(block_output)
    grad_gate, grad_up, grad_down = grads

    index = lax.axis_index("dp")

    def own_part(start, size):
        return lax.dynamic_slice_in_dim(gains, start + index * (size // dp_size), size // dp_size)

    return (
        block_output,
        token_grad,
        own_part(0, model_width),
        grad_query,
        grad_key,
        grad_value,
        own_part(2 * model_width, HEAD_SIZE),
        own_part(2 * model_width + HEAD_SIZE, HEAD_SIZE),
        grad_output,
        own_part(model_width, model_width),
        grad_gate,
        grad_up,
        grad_down,
    )


def solution(mesh):
    return jax.shard_map(
        functools.partial(shards, mesh.shape["dp"]),
        mesh=mesh,
        in_specs=(
            P("dp", None),
            P("dp", None),
            P(),
            P("dp", "tensor"),
            P("dp", "tensor"),
            P("dp", "tensor"),
            P(),
            P(),
            P("tensor", "dp"),
            P(),
            P("dp", "tensor"),
            P("dp", "tensor"),
            P("tensor", "dp"),
            P("dp", None),
        ),
        out_specs=(
            P("dp", None),
            P("dp", None),
            P("dp"),
            P("dp", "tensor"),
            P("dp", "tensor"),
            P("dp", "tensor"),
            P("dp"),
            P("dp"),
            P("tensor", "dp"),
            P("dp"),
            P("dp", "tensor"),
            P("dp", "tensor"),
            P("tensor", "dp"),
        ),
        check_vma=False,
    )
```

```python
import functools

import jax
import jax.numpy as jnp
from jax import lax
from jax.experimental import pallas as pl
from jax.experimental.pallas import tpu as pltpu
from jax.sharding import PartitionSpec as P

HEAD_SIZE = 128
BLK = 64


epsilon = 1e-06
rope_base = 1000000.0


def matrix_product(left, right):
    return jnp.dot(left, right, preferred_element_type=jnp.float32)


def inner_left(left, right):
    return lax.dot_general(
        left, right, (((0,), (0,)), ((), ())), preferred_element_type=jnp.float32
    )


def inner_right(left, right):
    return lax.dot_general(
        left, right, (((1,), (1,)), ((), ())), preferred_element_type=jnp.float32
    )


def layout(lengths, count_of_rows):
    padded = (lengths + BLK - 1) // BLK * BLK
    starts = jnp.cumsum(padded) - padded
    row_index = jnp.arange(count_of_rows, dtype=jnp.int32)
    inside = (row_index[:, None] >= starts[None, :]) & (
        row_index[:, None] < (starts + lengths)[None, :]
    )
    live_rows = jnp.any(inside, axis=1)
    slot_index = jnp.arange(lengths.shape[0], dtype=jnp.int32)
    owning = jnp.sum(jnp.where(inside, slot_index[None, :], 0), axis=1)
    position = jnp.sum(jnp.where(inside, row_index[:, None] - starts[None, :], 0), axis=1)
    segment = jnp.where(live_rows, owning, -1 - row_index)
    return (live_rows, segment, position)


def rotation(position, width):
    half_width = width // 2
    frequency = jnp.power(rope_base, -(jnp.arange(half_width, dtype=jnp.float32) * 2.0) / width)
    angles = position.astype(jnp.float32)[:, None] * frequency[None, :]
    return (jnp.cos(angles)[:, None, :], jnp.sin(angles)[:, None, :])


CHUNKS = 3
PARTS = 4
LANES = 128
ROW_BLOCK = 256
VMEM_LIMIT = 56 * 1024 * 1024


def add_low(left, right):
    return (left.astype(jnp.float32) + right.astype(jnp.float32)).astype(jnp.bfloat16)


class Ring:
    def __init__(self, size):
        self.size = size
        self.steps = size // 4
        index = lax.axis_index("dp")
        self.place = index // 4
        self.side = (index // 2) % 2
        self.core = index % 2
        self.places = [(self.place - 1 - i) % self.steps for i in range(self.steps)]
        self.groups = [
            [place * 4 + side * 2 + core for place in range(self.steps) for core in range(2)]
            for side in range(2)
        ]

    def swap_core(self, value):
        return lax.ppermute(value, "dp", [(i, i ^ 1) for i in range(self.size)])

    def swap_side(self, value):
        return lax.ppermute(value, "dp", [(i, i ^ 2) for i in range(self.size)])

    def shift(self, value, places):
        return lax.ppermute(
            value, "dp", [(i, (i + 4 * places) % self.size) for i in range(self.size)]
        )

    def pick(self, value, axis):
        low, high = jnp.split(value, 2, axis=axis)
        return (
            jnp.where(self.side == 0, low, high),
            jnp.where(self.side == 0, high, low),
        )

    def ordered(self, mine, other, axis):
        return jnp.where(
            self.side == 0,
            jnp.concatenate([mine, other], axis=axis),
            jnp.concatenate([other, mine], axis=axis),
        )

    def block(self, back, core, side):
        return ((self.place - back) % self.steps) * 4 + core * 2 + side


class Gather:
    def __init__(self, ring, piece):
        self.ring = ring
        self.hops, self.across, self.index = [piece], [], 0
        self.pieces, self.order = [], []

    def put(self, back, core, side, value):
        self.pieces.append(value)
        self.order.append(self.ring.block(back, core, side))

    def start(self, stages, hop=True, swap=1):
        ring, moves = self.ring, {}
        self.hops = list(stages.hold(*self.hops))
        if hop and len(self.hops) < ring.steps:
            moves["hop"] = ring.shift(self.hops[-1], 1)
        if swap:
            pieces = self.hops[self.index : self.index + swap]
            moves["side"] = [ring.swap_side(p) for p in pieces]
            moves["core"] = [ring.swap_core(p) for p in pieces]
            moves["both"] = [ring.swap_core(p) for p in self.across]
        return moves

    def finish(self, moves):
        ring = self.ring
        core, side = ring.core, ring.side
        if "hop" in moves:
            self.hops.append(moves["hop"])
        if "side" not in moves:
            return
        first = self.index - len(self.across)
        for back, value in enumerate(moves["both"], first):
            self.put(back, 1 - core, 1 - side, value)
        self.across = moves["side"]
        for back, (aside, other) in enumerate(zip(moves["side"], moves["core"]), self.index):
            self.put(back, core, side, self.hops[back])
            self.put(back, core, 1 - side, aside)
            self.put(back, 1 - core, side, other)
        self.index += len(moves["side"])

    @property
    def done(self):
        return len(self.pieces) == self.ring.size


class Stages:
    def __init__(self, mark):
        self.mark = mark

    def settle(self, *values):
        values, self.mark = lax.optimization_barrier((values, self.mark))
        return values

    def step(self, movers, *others):
        movers = [mover if isinstance(mover, tuple) else (mover, {}) for mover in movers]
        moves = [mover.start(self, **kind) for mover, kind in movers]
        moves, others = self.settle(moves, others)
        for (mover, _), move in zip(movers, moves):
            mover.finish(move)
        return others

    def hold(self, *values):
        return lax.optimization_barrier((values, self.mark))[0]

    @property
    def ties(self):
        return (self.mark,)


def swap_tensor(value):
    return lax.ppermute(value, "tensor", [(0, 1), (1, 0)])


def arrange(value, steps, width):
    blocks = [value[:, i * width : (i + 1) * width] for i in range(4 * steps)]
    order = [4 * place + k for place in range(steps) for k in (0, 2, 1, 3)]
    return jnp.concatenate([blocks[i] for i in order], axis=1)


def arrange_vector(vector, steps):
    return vector.reshape(steps, 2, 2, -1).swapaxes(1, 2).reshape(-1)


def sums_kernel(kinds, counts, *refs):
    ins, outs = refs[: sum(counts)], list(refs[sum(counts) :])
    for kind, count in zip(kinds, counts):
        group, ins = ins[:count], ins[count:]
        total = group[0][...].astype(jnp.float32)
        for ref in group[1:]:
            total = total + ref[...].astype(jnp.float32)
        if kind == "low":
            outs.pop(0)[...] = total.astype(jnp.bfloat16)
        elif kind == "turned":
            outs.pop(0)[...] = total.T
        elif kind[0] == "open":
            joined = outs.pop(0)
            joined[:, : total.shape[1]] = total.astype(jnp.bfloat16)
        elif kind[0] == "close":
            joined[:, kind[1] : kind[1] + total.shape[1]] = total.astype(jnp.bfloat16)
        else:
            first = 0
            for width in kind:
                outs.pop(0)[...] = total[:, first : first + width]
                first += width


def sums_call(*groups):
    shapes = []
    for kind, arrays in groups:
        rows, columns = arrays[-1][-1] if isinstance(arrays[-1], tuple) else arrays[-1].shape
        if kind[0] == "open":
            shapes.append(jax.ShapeDtypeStruct((rows, kind[1]), jnp.bfloat16))
        elif kind[0] == "close":
            continue
        elif kind == "low":
            shapes.append(jax.ShapeDtypeStruct((rows, columns), jnp.bfloat16))
        elif kind == "turned":
            shapes.append(jax.ShapeDtypeStruct((columns, rows), jnp.float32))
        else:
            shapes += [jax.ShapeDtypeStruct((rows, w), jnp.float32) for w in kind]
    ins, specs = [], []
    for _, arrays in groups:
        shape = arrays[-1][-1] if isinstance(arrays[-1], tuple) else arrays[-1].shape
        for a in arrays:
            a, *block = a if isinstance(a, tuple) else (a, (0, 0))
            ins.append(a)
            specs.append(pl.BlockSpec(shape, lambda i, block=block[0]: block))
    return pl.pallas_call(
        functools.partial(sums_kernel, [k for k, _ in groups], [len(a) for _, a in groups]),
        grid=(1,),
        in_specs=specs,
        out_specs=[pl.BlockSpec(shape.shape, lambda i: (0, 0)) for shape in shapes],
        out_shape=shapes,
        compiler_params=pltpu.CompilerParams(vmem_limit_bytes=VMEM_LIMIT),
        cost_estimate=pl.CostEstimate(
            flops=0, bytes_accessed=4 * sum(a.size for a in ins), transcendentals=0
        ),
    )(*ins)


def loose(ties):
    return [pl.BlockSpec(memory_space=pl.ANY) for _ in ties]


def row_call(kernel, rows, block, ins, outs, sums=(), ties=(), into=None):
    arrays, specs, places, cuts = [], [], [], 1
    for value, kind in ins:
        places.append(len(arrays))
        if kind in ("parts", "halves"):
            if kind == "parts":
                cuts = len(value)
            span = rows // len(value) // block
            for k, piece in enumerate(value):
                arrays.append(piece)
                specs.append(
                    pl.BlockSpec(
                        (block, piece.shape[1]),
                        lambda i, k=k, span=span: (jnp.clip(i - k * span, 0, span - 1), 0),
                    )
                )
            continue
        arrays.append(value)
        if kind == "all":
            specs.append(pl.BlockSpec(value.shape, lambda i: (0, 0)))
        else:
            first = 0 if kind == "rows" else kind
            specs.append(
                pl.BlockSpec((block, value.shape[1]), lambda i, first=first: (first + i, 0))
            )
    base, all_rows, aliases = 0, rows, {}
    count = len(arrays)
    if into is not None:
        given, base, all_rows = into
        if given is not None:
            ties = (given, *ties)
            aliases = {count: 0}
    out_specs = [pl.BlockSpec((block, c), lambda i: (base + i, 0)) for c, _ in outs]
    out_specs += [pl.BlockSpec((1, c), lambda i: (0, 0)) for c in sums]
    out_shape = [jax.ShapeDtypeStruct((all_rows, c), d) for c, d in outs]
    out_shape += [jax.ShapeDtypeStruct((1, c), jnp.float32) for c in sums]
    moved = sum(a.size * a.dtype.itemsize for a in arrays)
    moved += sum(rows * c * jnp.dtype(d).itemsize for c, d in outs)

    def body(*refs):
        given = refs[count + len(ties) :]
        if cuts == 1:
            kernel(*refs[:count], *given)
            return
        turn = pl.program_id(0) // (rows // cuts // block)
        for k in range(cuts):
            chosen = [
                refs[place + k * len(value) // cuts]
                if kind in ("parts", "halves")
                else refs[place]
                for place, (value, kind) in zip(places, ins)
            ]
            pl.when(turn == k)(functools.partial(kernel, *chosen, *given))

    return pl.pallas_call(
        body,
        grid=(rows // block,),
        in_specs=specs + loose(ties),
        out_specs=out_specs,
        out_shape=out_shape,
        input_output_aliases=aliases,
        compiler_params=pltpu.CompilerParams(vmem_limit_bytes=VMEM_LIMIT),
        cost_estimate=pl.CostEstimate(flops=0, bytes_accessed=moved, transcendentals=0),
    )(*arrays, *ties)


def inverse_rms(value):
    return lax.rsqrt(jnp.mean(value * value, axis=-1, keepdims=True) + epsilon)


def first_kernel(turn, tokens, cotangent, live, gain, tokens_out, upstream_out, normed_out):
    value = turn(tokens[...])
    tokens_out[...] = value
    value = value.astype(jnp.float32)
    normed_out[...] = (value * inverse_rms(value) * gain[...]).astype(jnp.bfloat16)
    back = turn(cotangent[...]).astype(jnp.float32)
    upstream_out[...] = (back * live[...]).astype(jnp.bfloat16)


def middle_kernel(tokens, mine, other, gain, middle_out, normed_out):
    branch = mine[...].astype(jnp.float32) + other[...].astype(jnp.float32)
    value = tokens[...].astype(jnp.float32) + branch
    middle_out[...] = value
    normed_out[...] = (value * inverse_rms(value) * gain[...]).astype(jnp.bfloat16)


def back_rms(value, gain, back):
    scale = inverse_rms(value)
    normed = value * scale
    pulled = back * gain
    center = jnp.mean(pulled * normed, axis=-1, keepdims=True)
    return scale * (pulled - normed * center), back * normed


def add_sum(out_ref, value):
    @pl.when(pl.program_id(0) == 0)
    def _():
        out_ref[...] = jnp.zeros_like(out_ref)

    out_ref[...] += jnp.sum(value, axis=0, keepdims=True)


def back_middle_kernel(
    mine, other, middle, upstream, gain, full, back_out, low_out, mixed_out, gain_out
):
    back = mine[...].astype(jnp.float32) + other[...].astype(jnp.float32)
    value, gain_term = back_rms(middle[...], gain[...], back)
    value = value + upstream[...].astype(jnp.float32)
    back_out[...] = value
    low = value.astype(jnp.bfloat16)
    low_out[...] = low
    mixed_out[...] = matrix_product(low, full[...]).astype(jnp.bfloat16)
    add_sum(gain_out, gain_term)


def output_kernel(turn, middle, mine, other, out):
    value = middle[...] + mine[...].astype(jnp.float32) + other[...].astype(jnp.float32)
    out[...] = turn(value).astype(jnp.bfloat16)


def token_kernel(turn, mine, other, tokens, back_middle, gain, out):
    back = mine[...].astype(jnp.float32) + other[...].astype(jnp.float32)
    value, _ = back_rms(tokens[...].astype(jnp.float32), gain[...], back)
    out[...] = turn(value + back_middle[...])


def feed_kernel(chunk, count, many, *refs):
    full, out = refs[count], refs[-1]
    block = out.shape[0]

    def picked(group, step):
        refs_of = refs[group[0] : group[1]]
        if len(refs_of) == 1:
            return refs_of[0][...]
        each = block // refs_of[0].shape[0]
        return jnp.concatenate([r[...] for r in refs_of[step * each : (step + 1) * each]], axis=0)

    def run(step):
        normed, upstream = picked((0, many), step), picked((many, count), step)
        gate = matrix_product(normed, full[:, :chunk])
        up = matrix_product(normed, full[:, chunk : 2 * chunk])
        back = matrix_product(upstream, full[:, 2 * chunk :])
        share = jax.nn.sigmoid(gate)
        active = gate * share
        out[:, :chunk] = (back * up * (share * (1.0 + gate * (1.0 - share)))).astype(jnp.bfloat16)
        out[:, chunk : 2 * chunk] = (back * active).astype(jnp.bfloat16)
        out[:, 2 * chunk :] = (active * up).astype(jnp.bfloat16)

    for step in range(2):
        pl.when(pl.program_id(0) == step)(functools.partial(run, step))


def feed_call(normed, upstream, full, ties=()):
    groups = [g if isinstance(g, list) else [g] for g in (normed, upstream)]
    rows, model_width = sum(a.shape[0] for a in groups[0]), full.shape[0]
    columns = full.shape[1]
    block = rows // 2
    specs = []
    for group in groups:
        if len(group) == 1:
            specs.append(pl.BlockSpec((block, model_width), lambda i: (i, 0)))
        else:
            specs += [pl.BlockSpec(a.shape, lambda i: (0, 0)) for a in group]
    return pl.pallas_call(
        functools.partial(feed_kernel, columns // 3, len(specs), len(groups[0])),
        grid=(2,),
        in_specs=specs + [pl.BlockSpec(full.shape, lambda i: (0, 0))] + loose(ties),
        out_specs=pl.BlockSpec((block, columns), lambda i: (i, 0)),
        out_shape=jax.ShapeDtypeStruct((rows, columns), jnp.bfloat16),
        compiler_params=pltpu.CompilerParams(vmem_limit_bytes=VMEM_LIMIT),
        cost_estimate=pl.CostEstimate(
            flops=2 * rows * model_width * columns,
            bytes_accessed=2 * (2 * rows * model_width + full.size + rows * columns),
            transcendentals=rows * columns // 3,
        ),
    )(*groups[0], *groups[1], full, *ties)


def wide_kernel(count, started, parts, *refs):
    outs, total = refs[-parts:], None
    for act, full in zip(refs[:count], refs[count : 2 * count]):
        term = inner_right(act[...], full[...])
        total = term if total is None else total + term
    if started:
        total = total + refs[2 * count][...]
    part = outs[0].shape[0]
    for i, out in enumerate(outs):
        out[...] = total[i * part : (i + 1) * part].astype(out.dtype)


def wide_call(acts, fulls, span, out_dtype, start=None, ties=(), parts=PARTS):
    lo, hi = span
    size, index = hi - lo, lo // (hi - lo)
    rows, model_width, count = acts[0].shape[0], fulls[0].shape[0], len(acts)
    tile = 512
    ins = list(acts) + list(fulls)
    specs = [pl.BlockSpec((rows, size), lambda i: (0, index))] * count
    specs += [pl.BlockSpec((tile, size), lambda i: (i, index))] * count
    if start is not None:
        ins.append(start)
        specs.append(pl.BlockSpec((rows, tile), lambda i: (0, i)))
    ins += list(ties)
    specs += [pl.BlockSpec(memory_space=pl.ANY) for _ in ties]
    return pl.pallas_call(
        functools.partial(wide_kernel, count, start is not None, parts),
        grid=(model_width // tile,),
        in_specs=specs,
        out_specs=[pl.BlockSpec((rows // parts, tile), lambda i: (0, i))] * parts,
        out_shape=[jax.ShapeDtypeStruct((rows // parts, model_width), out_dtype)] * parts,
        compiler_params=pltpu.CompilerParams(vmem_limit_bytes=VMEM_LIMIT),
        cost_estimate=pl.CostEstimate(
            flops=2 * rows * model_width * size * count,
            bytes_accessed=2 * (rows + model_width) * size * count + rows * model_width * 6,
            transcendentals=0,
        ),
    )(*ins)


def grad_kernel(split, counts, *refs):
    out = refs[-1]
    acts = refs[sum(counts) : sum(counts) + 2]
    first = 0
    total = [0.0, 0.0]
    for group, count in enumerate(counts):
        rows, act = 0, acts[group % 2]
        columns = slice(0, split) if group < 2 else slice(split, None)
        parts = [r[...] for r in refs[first : first + count]]
        left = parts[0] if count == 1 else jnp.concatenate(parts, axis=0)
        total[group // 2] = total[group // 2] + inner_left(left, act[:, columns])
        first += count
    out[:, :split] = total[0].astype(jnp.bfloat16)
    out[:, split:] = total[1].astype(jnp.bfloat16)


def grad_call(normed, upstream, acts, ties=(), place=0, places=1, into=None):
    groups = [g if isinstance(g, list) else [g] for g in (*normed, *upstream)]
    lefts = [a for group in groups for a in group]
    rows, model_width = acts[0].shape[0], lefts[0].shape[1]
    columns = acts[0].shape[1]
    tall = 512
    ins = lefts + list(acts)
    specs = [pl.BlockSpec((a.shape[0], tall), lambda i: (0, i)) for a in lefts]
    specs += [pl.BlockSpec((rows, columns), lambda i: (0, 0))] * 2
    aliases = {}
    if into is not None:
        aliases = {len(ins): 0}
        ins.append(into)
        specs.append(pl.BlockSpec(memory_space=pl.ANY))
    return pl.pallas_call(
        functools.partial(grad_kernel, columns // 3 * 2, [len(g) for g in groups]),
        grid=(model_width // tall,),
        in_specs=specs + loose(ties),
        out_specs=pl.BlockSpec((tall, columns), lambda i: (i, place)),
        out_shape=jax.ShapeDtypeStruct((model_width, places * columns), jnp.bfloat16),
        input_output_aliases=aliases,
        compiler_params=pltpu.CompilerParams(vmem_limit_bytes=VMEM_LIMIT),
        cost_estimate=pl.CostEstimate(
            flops=4 * rows * model_width * columns,
            bytes_accessed=2 * (4 * rows * model_width + 2 * rows * columns + model_width * columns),
            transcendentals=0,
        ),
    )(*ins, *ties)


def norm_rope(raw, gain, cosine, sine):
    scale = inverse_rms(raw)
    normed = raw * scale
    scaled = normed * gain
    return scaled * cosine + pltpu.roll(scaled, HEAD_SIZE // 2, 1) * sine, normed, scale


def back_norm_rope(back, normed, scale, gain, cosine, sine):
    back = back * cosine - pltpu.roll(back, HEAD_SIZE // 2, 1) * sine
    pulled = back * gain
    center = jnp.mean(pulled * normed, axis=-1, keepdims=True)
    return scale * (pulled - normed * center), back * normed


def allowed_pairs(segment_column, segment_row, first, count):
    height = first + count
    key = lax.broadcasted_iota(jnp.int32, (height, count), 0)
    query = lax.broadcasted_iota(jnp.int32, (height, count), 1) + first
    same = segment_column[:height, :] == segment_row[:, first:height]
    return same & (key <= query)


def attend_kernel(
    start, queries, keys, values, query_gain, key_gain, cosine, sine, seg_column, seg_row, *rest
):
    out, total_out = rest[-2:]
    size, rows = queries.shape[0], keys.shape[0]
    key = norm_rope(keys[...], key_gain[...], cosine[:rows, :], sine[:rows, :])[0]
    key = key.astype(jnp.bfloat16)
    value = values[...].T.astype(jnp.bfloat16)
    spans = [slice(lo, lo + HEAD_SIZE) for lo in range(0, queries.shape[1], HEAD_SIZE)]
    turn = cosine[start : start + size, :], sine[start : start + size, :]
    heads = [
        norm_rope(queries[:, span], query_gain[...], *turn)[0].astype(jnp.bfloat16)
        for span in spans
    ]
    for first in range(0, size, ROW_BLOCK):
        here = slice(first, first + ROW_BLOCK)
        end = start + first + ROW_BLOCK
        allowed = allowed_pairs(seg_column, seg_row, start + first, ROW_BLOCK)
        for k, (span, query) in enumerate(zip(spans, heads)):
            scores = inner_right(key[:end], query[here]) * HEAD_SIZE ** (-0.5)
            scores = jnp.where(allowed, scores, -1e30)
            largest = jnp.max(scores, axis=0, keepdims=True)
            raised = jnp.exp(scores - largest)
            total = jnp.sum(raised, axis=0, keepdims=True)
            weights = (raised * (1.0 / total)).astype(jnp.bfloat16)
            mixed = matrix_product(value[:, :end], weights)
            out[here, span] = mixed.T.astype(jnp.bfloat16)
            total_out[k : k + 1, here] = largest + jnp.log(total)


def attend_back_kernel(
    query_columns,
    key_columns,
    queries,
    keys,
    values,
    query_gain,
    key_gain,
    cosine,
    sine,
    seg_column,
    seg_row,
    totals,
    *rest,
):
    out, query_gain_out, key_gain_out = rest[-3:]
    back_parts = rest[:2]
    head = pl.program_id(0)
    rows, wide = queries.shape
    scaling = HEAD_SIZE ** (-0.5)
    cosine, sine = cosine[...], sine[...]
    key, key_normed, key_scale = norm_rope(keys[...], key_gain[...], cosine, sine)
    turned = key.T.astype(jnp.bfloat16)
    key = key.astype(jnp.bfloat16)
    value = values[...].astype(jnp.bfloat16)
    back_mixture = jnp.concatenate([b[...] for b in back_parts], axis=0)
    spans = [slice(lo, lo + HEAD_SIZE) for lo in range(0, wide, HEAD_SIZE)]
    heads = [norm_rope(queries[:, span], query_gain[...], cosine, sine) for span in spans]
    back_queries = [[] for _ in spans]
    back_key, back_value = None, None
    for first in range(0, rows, ROW_BLOCK):
        end = first + ROW_BLOCK
        allowed = allowed_pairs(seg_column, seg_row, first, ROW_BLOCK)
        key_term, value_term = 0.0, 0.0
        for k, span in enumerate(spans):
            query = heads[k][0][first:end].astype(jnp.bfloat16)
            back = back_mixture[first:end, span]
            scores = inner_right(key[:end], query) * scaling
            weights = jnp.where(allowed, jnp.exp(scores - totals[k : k + 1, first:end]), 0.0)
            terms = inner_right(value[:end], back) * weights
            value_term = value_term + matrix_product(weights.astype(jnp.bfloat16), back)
            center = jnp.sum(terms, axis=0, keepdims=True)
            back_scores = (terms - weights * center).astype(jnp.bfloat16)
            back_queries[k].append(matrix_product(turned[:, :end], back_scores).T * scaling)
            key_term = key_term + matrix_product(back_scores, query) * scaling
        if back_key is None:
            back_key, back_value = key_term, value_term
        else:
            back_key = jnp.concatenate([back_key + key_term[:first], key_term[first:]], axis=0)
            back_value = jnp.concatenate(
                [back_value + value_term[:first], value_term[first:]], axis=0
            )
    query_term = 0.0
    for k, (lo, (_, normed, scale)) in enumerate(zip(range(0, wide, HEAD_SIZE), heads)):
        back_query, term = back_norm_rope(
            jnp.concatenate(back_queries[k], axis=0), normed, scale, query_gain[...], cosine, sine
        )
        query_term = query_term + term
        start = pl.multiple_of(head * wide + lo, HEAD_SIZE)
        out[:, pl.ds(start, HEAD_SIZE)] = back_query.astype(jnp.bfloat16)
    back_key, key_sum = back_norm_rope(
        back_key, key_normed, key_scale, key_gain[...], cosine, sine
    )
    start = pl.multiple_of(query_columns + head * HEAD_SIZE, HEAD_SIZE)
    out[:, pl.ds(start, HEAD_SIZE)] = back_key.astype(jnp.bfloat16)
    start = pl.multiple_of(query_columns + key_columns + head * HEAD_SIZE, HEAD_SIZE)
    out[:, pl.ds(start, HEAD_SIZE)] = back_value.astype(jnp.bfloat16)
    add_sum(query_gain_out, query_term)
    add_sum(key_gain_out, key_sum)


def attention_call(raw, query_columns, key_columns, gains, tables, segment, span, back=None, totals=None, ties=()):
    rows, columns = raw.shape
    start, end = span
    count = key_columns // HEAD_SIZE
    wide = query_columns * HEAD_SIZE // key_columns
    first_key = query_columns // HEAD_SIZE
    first_value = first_key + key_columns // HEAD_SIZE
    ins = [raw, raw, raw, *gains, *tables, segment[:, None], segment[None, :]]
    size = end - start
    specs = [
        pl.BlockSpec((size, wide), lambda h: (start // size, h)),
        pl.BlockSpec((end, HEAD_SIZE), lambda h: (0, first_key + h)),
        pl.BlockSpec((end, HEAD_SIZE), lambda h: (0, first_value + h)),
    ] + [pl.BlockSpec(a.shape, lambda h: (0, 0)) for a in ins[3:]]
    params = dict(
        grid=(count,),
        compiler_params=pltpu.CompilerParams(vmem_limit_bytes=VMEM_LIMIT),
    )
    pairs = count * wide // HEAD_SIZE * rows * rows
    if back is None:
        return pl.pallas_call(
            functools.partial(attend_kernel, start),
            in_specs=specs + loose(ties),
            out_specs=[
                pl.BlockSpec((size, wide), lambda h: (0, h)),
                pl.BlockSpec((8, size), lambda h: (h, 0)),
            ],
            out_shape=[
                jax.ShapeDtypeStruct((size, count * wide), jnp.bfloat16),
                jax.ShapeDtypeStruct((count * 8, size), jnp.float32),
            ],
            cost_estimate=pl.CostEstimate(
                flops=4 * pairs * HEAD_SIZE, bytes_accessed=5 * raw.size, transcendentals=pairs
            ),
            **params,
        )(*ins, *ties)
    gain_spec = pl.BlockSpec((1, HEAD_SIZE), lambda h: (0, 0))
    gain_shape = jax.ShapeDtypeStruct((1, HEAD_SIZE), jnp.float32)
    return pl.pallas_call(
        functools.partial(attend_back_kernel, query_columns, key_columns),
        in_specs=specs
        + [pl.BlockSpec((8, rows), lambda h: (h, 0))]
        + [pl.BlockSpec((b.shape[0], wide), lambda h: (0, h)) for b in back]
        + loose(ties),
        out_specs=[pl.BlockSpec((rows, columns), lambda h: (0, 0)), gain_spec, gain_spec],
        out_shape=[jax.ShapeDtypeStruct((rows, columns), jnp.bfloat16), gain_shape, gain_shape],
        cost_estimate=pl.CostEstimate(
            flops=12 * pairs * HEAD_SIZE, bytes_accessed=8 * raw.size, transcendentals=pairs
        ),
        **params,
    )(*ins, totals, *back, *ties)


def back_first_kernel(raw_grad, full, tokens, *rest):
    outs, gain_out, scale = rest[-2 - PARTS : -2], rest[-2], rest[-1]
    part, tile = outs[0].shape

    @pl.when(pl.program_id(0) == 0)
    def _():
        scale[...] = inverse_rms(tokens[...].astype(jnp.float32))

    back = inner_right(raw_grad[...], full[...])
    for i, out in enumerate(outs):
        out[...] = back[i * part : (i + 1) * part].astype(jnp.bfloat16)
    start = pl.multiple_of(pl.program_id(0) * tile, tile)
    normed = tokens[:, pl.ds(start, tile)].astype(jnp.float32) * scale[...]
    gain_out[...] = jnp.sum(back * normed, axis=0, keepdims=True)


def back_first_call(raw_grad, full, tokens, ties=()):
    rows, model_width = tokens.shape
    tile, part = 512, rows // PARTS
    return pl.pallas_call(
        back_first_kernel,
        grid=(model_width // tile,),
        in_specs=[
            pl.BlockSpec(raw_grad.shape, lambda i: (0, 0)),
            pl.BlockSpec((tile, full.shape[1]), lambda i: (i, 0)),
            pl.BlockSpec(tokens.shape, lambda i: (0, 0)),
        ]
        + [pl.BlockSpec(memory_space=pl.ANY) for _ in ties],
        out_specs=[pl.BlockSpec((part, tile), lambda i: (0, i))] * PARTS
        + [pl.BlockSpec((1, tile), lambda i: (0, i))],
        out_shape=[jax.ShapeDtypeStruct((part, model_width), jnp.bfloat16)] * PARTS
        + [jax.ShapeDtypeStruct((1, model_width), jnp.float32)],
        scratch_shapes=[pltpu.VMEM((rows, 1), jnp.float32)],
        compiler_params=pltpu.CompilerParams(vmem_limit_bytes=VMEM_LIMIT),
        cost_estimate=pl.CostEstimate(
            flops=2 * rows * full.size,
            bytes_accessed=2 * full.size + 8 * tokens.size,
            transcendentals=0,
        ),
    )(raw_grad, full, tokens, *ties)


def scatter_kernel(width, steps, lefts, rights, gots, ties, info, *refs):
    turned, outs = refs[-1], refs[lefts + rights + gots + ties : -1]
    left, right = refs[:lefts], refs[lefts : lefts + rights]
    got = refs[lefts + rights : lefts + rights + gots]
    size = steps * width

    @pl.when(pl.program_id(0) == 0)
    def _():
        for k in range(2):
            side = info[1] if k == 0 else 1 - info[1]
            for i in range(steps):
                start = pl.multiple_of((info[2 + i] * 4 + info[0] * 2 + side) * width, width)
                first = 0
                for part in left:
                    block = part[:, pl.ds(start, width)].T
                    row = k * size + i * width
                    turned[row : row + width, first : first + part.shape[0]] = block
                    first += part.shape[0]

    joined = right[0][...]
    if rights > 1:
        joined = jnp.concatenate([r[...] for r in right], axis=0)
    total = matrix_product(turned[...], joined)
    for k in range(2):
        value = total[k * size : (k + 1) * size]
        if gots:
            value = value + got[k][...].astype(jnp.float32)
        value = value.astype(jnp.bfloat16)
        each = len(outs) // 2
        rows = size // each
        for i in range(each):
            outs[k * each + i][...] = value[i * rows : (i + 1) * rows]


def scatter_call(ring, width, left, right, core, got=(), ties=(), apart=True):
    rows, columns = sum(r.shape[0] for r in right), right[0].shape[1]
    steps = ring.steps
    each = steps if apart else 1
    if 2 * width % LANES:
        blocks = jnp.concatenate(left, axis=0).reshape(rows, steps, 2, 2, width)
        right = jnp.concatenate(right, axis=0)
        outs = []
        for k, side in enumerate((ring.side, 1 - ring.side)):
            for i, place in enumerate(ring.places):
                picked = lax.dynamic_slice(
                    blocks, (0, place, core, side, 0), (rows, 1, 1, 1, width)
                )
                total = inner_left(picked.reshape(rows, width), right)
                if got:
                    total = total + got[k][i * width : (i + 1) * width].astype(jnp.float32)
                outs.append(total.astype(jnp.bfloat16))
        if apart:
            return outs[:steps], outs[steps:]
        return [jnp.concatenate(outs[:steps])], [jnp.concatenate(outs[steps:])]
    info = jnp.stack([core, ring.side] + ring.places).astype(jnp.int32)
    tile, tall = 512, steps * width // each
    outs = pl.pallas_call(
        functools.partial(
            scatter_kernel, width, steps, len(left), len(right), len(got), len(ties)
        ),
        grid_spec=pltpu.PrefetchScalarGridSpec(
            num_scalar_prefetch=1,
            grid=(columns // tile,),
            in_specs=[pl.BlockSpec(a.shape, lambda i, info: (0, 0)) for a in left]
            + [pl.BlockSpec((r.shape[0], tile), lambda i, info: (0, i)) for r in right]
            + [pl.BlockSpec((steps * width, tile), lambda i, info: (0, i)) for _ in got]
            + loose(ties),
            out_specs=[pl.BlockSpec((tall, tile), lambda i, info: (0, i))] * (2 * each),
            scratch_shapes=[pltpu.VMEM((2 * steps * width, rows), jnp.bfloat16)],
        ),
        out_shape=[jax.ShapeDtypeStruct((tall, columns), jnp.bfloat16)] * (2 * each),
        compiler_params=pltpu.CompilerParams(vmem_limit_bytes=VMEM_LIMIT),
        cost_estimate=pl.CostEstimate(
            flops=4 * rows * steps * width * columns,
            bytes_accessed=2 * rows * (columns + 16 * width) + 4 * steps * width * columns,
            transcendentals=0,
        ),
    )(info, *left, *right, *got, *ties)
    return outs[:each], outs[each:]


def finish_kernel(chunk, counts, info, *refs):
    count = len(counts)
    totals, others, (gate, up, down) = refs[:count], refs[count:-3], refs[-3:]
    side, width = info[0], gate.shape[0]
    half = gate.shape[1] // 2
    values = []
    for total, chunks in zip(totals, counts):
        mine = total[pl.ds(pl.multiple_of(side * width, width), width), :]
        values += [(mine[:, 3 * j * chunk : 3 * (j + 1) * chunk], side) for j in range(chunks)]
    values += [(other[...], 1 - side) for other in others]
    for j, (value, at) in enumerate(values):
        value = value.astype(jnp.float32)
        start = pl.multiple_of(at * half + j % CHUNKS * chunk, chunk)
        gate[:, pl.ds(start, chunk)] = value[:, :chunk]
        up[:, pl.ds(start, chunk)] = value[:, chunk : 2 * chunk]
        down[pl.ds(start, chunk), :] = value[:, 2 * chunk :].T


def finish_call(ring, chunk, totals, others):
    width, hidden = others[0].shape[0], 2 * CHUNKS * chunk
    counts = [a.shape[1] // (3 * chunk) for a in totals]
    shapes = [(width, hidden), (width, hidden), (hidden, width)]
    whole = [pl.BlockSpec(a.shape, lambda i, info: (0, 0)) for a in (*totals, *others)]
    return pl.pallas_call(
        functools.partial(finish_kernel, chunk, counts),
        grid_spec=pltpu.PrefetchScalarGridSpec(
            num_scalar_prefetch=1,
            grid=(1,),
            in_specs=whole,
            out_specs=[pl.BlockSpec(shape, lambda i, info: (0, 0)) for shape in shapes],
        ),
        out_shape=[jax.ShapeDtypeStruct(shape, jnp.float32) for shape in shapes],
        compiler_params=pltpu.CompilerParams(vmem_limit_bytes=VMEM_LIMIT),
        cost_estimate=pl.CostEstimate(
            flops=0, bytes_accessed=18 * hidden * width, transcendentals=0
        ),
    )(jnp.stack([ring.side]).astype(jnp.int32), *totals, *others)


def join_kernel(width, count, order, left, *rest):
    pieces, (product, whole) = rest[:count], rest[count:]
    for i, piece in enumerate(pieces):
        whole[pl.ds(pl.multiple_of(order[i] * width, width), width), :] = piece[...]
    product[...] = matrix_product(left[...], whole[...])


def join_call(gather, left):
    width, columns = gather.pieces[0].shape
    rows, model_width = left.shape
    tile = columns // 4
    count = len(gather.pieces)
    return pl.pallas_call(
        functools.partial(join_kernel, width, count),
        grid_spec=pltpu.PrefetchScalarGridSpec(
            num_scalar_prefetch=1,
            grid=(columns // tile,),
            in_specs=[pl.BlockSpec((rows, model_width), lambda i, order: (0, 0))]
            + [pl.BlockSpec((width, tile), lambda i, order: (0, i))] * count,
            out_specs=[
                pl.BlockSpec((rows, tile), lambda i, order: (0, i)),
                pl.BlockSpec((model_width, tile), lambda i, order: (0, i)),
            ],
        ),
        out_shape=[
            jax.ShapeDtypeStruct((rows, columns), jnp.float32),
            jax.ShapeDtypeStruct((model_width, columns), jnp.bfloat16),
        ],
        compiler_params=pltpu.CompilerParams(vmem_limit_bytes=VMEM_LIMIT),
        cost_estimate=pl.CostEstimate(
            flops=2 * rows * model_width * columns,
            bytes_accessed=4 * model_width * columns + 4 * rows * columns,
            transcendentals=0,
        ),
    )(jnp.stack(gather.order).astype(jnp.int32), left, *gather.pieces)


def join_wide_kernel(width, count, order, left, *rest):
    pieces, whole, total, outs = rest[:count], rest[count], rest[-1], rest[count + 1 : -1]
    for i, piece in enumerate(pieces):
        whole[pl.ds(pl.multiple_of(order[i] * width, width), width), :] = piece[...]
    term = inner_right(left[...], whole[...])

    @pl.when(pl.program_id(0) == 0)
    def _():
        total[...] = term

    @pl.when(pl.program_id(0) == 1)
    def _():
        part = outs[0].shape[0]
        for i, out in enumerate(outs):
            value = total[i * part : (i + 1) * part, :] + term[i * part : (i + 1) * part]
            out[...] = value.astype(jnp.bfloat16)


def join_wide_call(gather, left, part):
    width, columns = gather.pieces[0].shape
    rows, model_width = left.shape[0], width * len(gather.pieces)
    tile, parts = columns // 2, rows // part
    count = len(gather.pieces)
    return pl.pallas_call(
        functools.partial(join_wide_kernel, width, count),
        grid_spec=pltpu.PrefetchScalarGridSpec(
            num_scalar_prefetch=1,
            grid=(2,),
            in_specs=[pl.BlockSpec((rows, tile), lambda i, order: (0, i))]
            + [pl.BlockSpec((width, tile), lambda i, order: (0, i))] * count,
            out_specs=[pl.BlockSpec((model_width, tile), lambda i, order: (0, i))]
            + [pl.BlockSpec((part, model_width), lambda i, order: (0, 0))] * parts,
            scratch_shapes=[pltpu.VMEM((rows, model_width), jnp.float32)],
        ),
        out_shape=[jax.ShapeDtypeStruct((model_width, columns), jnp.bfloat16)]
        + [jax.ShapeDtypeStruct((part, model_width), jnp.bfloat16)] * parts,
        compiler_params=pltpu.CompilerParams(vmem_limit_bytes=VMEM_LIMIT),
        cost_estimate=pl.CostEstimate(
            flops=2 * rows * model_width * columns,
            bytes_accessed=4 * model_width * columns + 4 * rows * model_width,
            transcendentals=0,
        ),
    )(jnp.stack(gather.order).astype(jnp.int32), left, *gather.pieces)


def rows_product_kernel(left, right, *outs):
    outs = outs[-2:]
    total = inner_right(left[...], right[...])
    part = outs[0].shape[0]
    for i, out in enumerate(outs):
        out[...] = total[i * part : (i + 1) * part].astype(jnp.bfloat16)


def rows_product(left, right, part, ties=()):
    rows, columns = left.shape
    model_width = right.shape[0]
    tile = 512
    return pl.pallas_call(
        rows_product_kernel,
        grid=(model_width // tile,),
        in_specs=[
            pl.BlockSpec(left.shape, lambda i: (0, 0)),
            pl.BlockSpec((tile, columns), lambda i: (i, 0)),
        ]
        + loose(ties),
        out_specs=[pl.BlockSpec((part, tile), lambda i: (0, i))] * (rows // part),
        out_shape=[jax.ShapeDtypeStruct((part, model_width), jnp.bfloat16)] * (rows // part),
        compiler_params=pltpu.CompilerParams(vmem_limit_bytes=VMEM_LIMIT),
        cost_estimate=pl.CostEstimate(
            flops=2 * rows * right.size, bytes_accessed=2 * right.size, transcendentals=0
        ),
    )(left, right, *ties)


def shards(
    dp_size,
    tokens,
    seq_lengths,
    first_gain,
    query_weight,
    key_matrix,
    value_matrix,
    query_norm_gain,
    key_gain,
    output_weight,
    second_gain,
    gate_weight,
    up_weight,
    down_weight,
    cotangent,
):
    ring = Ring(dp_size)
    steps = ring.steps
    rows, model_width = tokens.shape
    width = query_weight.shape[0]
    key_heads = key_matrix.shape[1] // HEAD_SIZE
    query_columns, key_columns = query_weight.shape[1], key_matrix.shape[1]
    part = rows // PARTS
    tiled = width % LANES == 0
    turned = functools.partial(arrange, steps=steps, width=width)
    turn = turned if tiled else (lambda value: value)
    if not tiled:
        tokens, cotangent = turned(tokens), turned(cotangent)

    hidden_width = gate_weight.shape[1] // 2
    chunk = hidden_width // CHUNKS
    pieces = [ring.pick(w, 1) for w in (gate_weight, up_weight, down_weight.T)]
    feed_mine, feed_other = (
        [
            jnp.concatenate([p[k][:, j * chunk : (j + 1) * chunk] for p in pieces], axis=1)
            for j in range(CHUNKS)
        ]
        for k in range(2)
    )
    feed_full = [None] * CHUNKS

    def feed_gather(j, got):
        block = ring.ordered(feed_mine[j], got, 0)
        feed_full[j] = lax.all_gather(
            block, "dp", axis=0, tiled=True, axis_index_groups=ring.groups
        )

    attention = Gather(ring, jnp.concatenate([query_weight, key_matrix, value_matrix], axis=1))
    output = Gather(ring, output_weight.T)

    live_rows, segment, position = layout(seq_lengths[0], rows)
    cosine_table, sinusoid_table = rotation(position, HEAD_SIZE)
    gain_one = arrange_vector(first_gain.astype(jnp.float32), steps)[None]
    gain_two = arrange_vector(second_gain.astype(jnp.float32), steps)[None]
    tables = (
        jnp.concatenate([cosine_table[:, 0], cosine_table[:, 0]], axis=1),
        jnp.concatenate([-sinusoid_table[:, 0], sinusoid_table[:, 0]], axis=1),
    )
    head_gains = (
        query_norm_gain.astype(jnp.float32)[None],
        key_gain.astype(jnp.float32)[None],
    )
    stages = Stages(jnp.broadcast_to(gain_one[:, :LANES], (8, LANES)) + 0.0)
    settle, step = stages.settle, stages.step
    token_rows, upstream, input_one = row_call(
        functools.partial(first_kernel, turn),
        rows,
        128,
        [
            (tokens, "rows"),
            (cotangent, "rows"),
            (live_rows[:, None].astype(jnp.float32), "rows"),
            (gain_one, "all"),
        ],
        [(model_width, jnp.bfloat16)] * 3,
    )
    for i in range(steps):
        movers = [attention]
        if i != 2:
            movers.append((output, dict(swap=int(i > 2))))
        others = []
        if i in (1, 2):
            others.append(ring.swap_side(*stages.hold(feed_other[i - 1])))
        if i == 0:
            others = [token_rows, upstream, input_one, tables]
        others = step(movers, *others)
        if i == 0:
            token_rows, upstream, input_one, tables = others
        if i in (1, 2):
            feed_gather(i - 1, others[0])
    step([attention])
    place = lax.axis_index("tensor")
    sent = [
        lax.dynamic_slice_in_dim(upstream, place * (rows // 2) + k * part, part) for k in range(2)
    ]

    raw, attention_full = step([(output, dict(swap=2))], *join_call(attention, input_one))
    half = rows // 2
    attend_args = (raw, query_columns, key_columns, head_gains, tables, segment)
    mixed, row_total = attention_call(*attend_args, (0, half), ties=stages.ties)
    while not output.done:
        (mixed,) = step([output], mixed)
    mixture_low, row_totals = [mixed], [row_total]
    output_full, *branch_parts = join_wide_call(output, mixed, part)
    (late,) = stages.hold(feed_other[2:])

    middle_parts, normed_parts, normed_other = [], [], []
    got = None
    for i in range(PARTS + 1):
        work = []
        if i:
            work = row_call(
                middle_kernel,
                part,
                part,
                [
                    (token_rows, i - 1),
                    (branch_parts[i - 1], "rows"),
                    (got, "rows"),
                    (gain_two, "all"),
                ],
                [(model_width, jnp.float32), (model_width, jnp.bfloat16)],
            )
        if i < PARTS:
            moves = [swap_tensor(branch_parts[i])]
            if i < 2:
                moves.append(ring.swap_side(stages.hold(sent[i])[0]))
            else:
                moves.append(ring.swap_side(normed_parts[i - 2]))
            extra = []
            if i == 0:
                mixed, row_total = attention_call(*attend_args, (half, rows), ties=stages.ties)
                mixture_low.append(mixed)
                row_totals.append(row_total)
                extra = [mixed, [ring.swap_side(w) for w in late]]
            if i == 1:
                extra = rows_product(mixture_low[1], output_full, part, stages.ties)
            moves, work, extra = settle(moves, work, extra)
            got = moves[0]
            if i == 0:
                mixture_low[1], extra = extra
                for j, value in enumerate(extra):
                    feed_gather(2 + j, value)
            if i == 1:
                branch_parts += extra
            if i < 2:
                sent[i] = moves[1]
            else:
                normed_other.append(moves[1])
        if i:
            middle_parts.append(work[0])
            normed_parts.append(work[1])
    got = [swap_tensor(v) for v in stages.hold(*sent)]

    span, out_span = (0, 2 * chunk), (2 * chunk, 3 * chunk)
    rest = [ring.swap_side(p) for p in normed_parts[len(normed_other) :]]
    acts = []
    for j in range(CHUNKS - 1):
        act, rest[j : j + 1], there = settle(
            feed_call(normed_parts, upstream, feed_full[j], stages.ties),
            rest[j : j + 1],
            got if j == CHUNKS - 2 else [],
        )
        acts.append(act)
    got = there
    rest, upstream_other = settle(
        rest, [jnp.where(place == 0, a, b) for a, b in zip(sent + got, got + sent)]
    )
    normed_other += rest
    sides = (normed_parts, normed_other), (upstream, upstream_other)
    acts_other = [feed_call(normed_other, upstream_other, feed_full[0], stages.ties)]
    feed_grads = [grad_call(*sides, (acts[0], acts_other[0]))]
    last_grads = None
    for j in range(1, CHUNKS - 1):
        acts_other.append(
            feed_call(normed_other, upstream_other, feed_full[j], (feed_grads + acts_other[1:])[-1:])
        )
    (early,) = wide_call(acts_other, feed_full[:-1], span, jnp.float32, parts=1)
    acts_other.append(feed_call(normed_other, upstream_other, feed_full[-1], (early,)))
    back_other = wide_call(acts_other[-1:], feed_full[-1:], span, jnp.bfloat16, early)
    (acts_last,) = settle(
        feed_call(normed_parts, upstream, feed_full[-1], tuple(back_other[:1]))
    )
    acts.append(acts_last)
    back_other = [back_other[0], *stages.hold(*back_other[1:])]

    back_mine = wide_call(acts, feed_full, span, jnp.float32, ties=stages.ties)
    got, back_mine = settle(ring.swap_side(back_other[0]), back_mine)
    mine = add_low(back_mine[0], got)
    back_parts, low_parts, mixed_parts, grad_second = [], [], [], 0.0
    out_other, out_mine, out_sums, out_got = None, None, [], []

    def back_middle_call(k, mine, other):
        return row_call(
            back_middle_kernel,
            2 * part,
            part,
            [
                (mine, "parts"),
                (other, "parts"),
                (middle_parts[2 * k : 2 * k + 2], "parts"),
                (upstream, 2 * k),
                (gain_two, "all"),
                (output_full, "all"),
            ],
            [
                (model_width, jnp.float32),
                (model_width, jnp.bfloat16),
                (query_columns, jnp.bfloat16),
            ],
            [model_width],
            stages.ties,
        )

    sums, sums_got = [], []
    for i in range(PARTS):
        work = []
        if i + 1 < CHUNKS:
            last_grads = grad_call(
                *sides,
                (acts[i + 1], acts_other[i + 1]),
                (mine,) + stages.ties,
                i,
                CHUNKS - 1,
                last_grads,
            )
            work = [last_grads]
        if i == PARTS - 2:
            work = [
                wide_call(acts_other, feed_full, out_span, jnp.bfloat16, ties=(mine,), parts=2)
            ]
        if i == PARTS - 1:
            work = [wide_call(acts, feed_full, out_span, jnp.float32, ties=(mine,), parts=2)]
        done = back_middle_call(0, sums, sums_got) if i == 2 else []
        moves = [swap_tensor(mine)]
        if i + 1 < PARTS:
            moves.append(ring.swap_side(back_other[i + 1]))
        moves, work, done = settle(moves, work, done)
        back_other[i + 2 :] = stages.hold(*back_other[i + 2 :])
        sums.append(mine)
        sums_got.append(moves[0])
        if i + 1 < PARTS:
            mine = add_low(back_mine[i + 1], moves[1])
        if i + 1 < CHUNKS:
            last_grads = work[0]
        if i == PARTS - 2:
            out_other = list(work[0])
        if i == PARTS - 1:
            out_mine = work[0]
        if i == 2:
            back_parts.append(done[0])
            low_parts.append(done[1])
            mixed_parts.append(done[2])
            grad_second = grad_second + done[3]
    done = back_middle_call(1, sums[2:], sums_got[2:])
    back_parts.append(done[0])
    low_parts.append(done[1])
    mixed_parts.append(done[2])
    grad_second = grad_second + done[3]
    feed_grads.append(last_grads)

    scattered = [
        lax.psum_scatter(
            grad, "dp", scatter_dimension=0, tiled=True, axis_index_groups=ring.groups
        )
        for grad in feed_grads
    ]

    core = ring.core
    far = scatter_call(
        ring, width, low_parts, mixture_low, 1 - core, ties=stages.ties, apart=False
    )
    (got,) = settle(ring.swap_side(out_other[0]))
    (held,) = stages.hold(out_other[1])
    out_sums = [add_low(out_mine[0], got)]

    def picked(total):
        return lax.dynamic_slice_in_dim(total, (1 - ring.side) * width, width)

    work, scattered[0], far, got, out_next = settle(
        attention_call(
            *attend_args,
            (0, rows),
            mixed_parts,
            jnp.concatenate(row_totals, axis=1),
            stages.ties + (far[0][0],),
        ),
        scattered[0],
        [ring.swap_core(f[0]) for f in far],
        ring.swap_side(held),
        swap_tensor(out_sums[0]),
    )
    raw_grad, grad_qgain, grad_kgain = work
    out_sums.append(add_low(out_mine[1], got))
    out_done = [out_next]
    far_one = scatter_call(
        ring, width, [input_one], [raw_grad], 1 - core, ties=stages.ties, apart=False
    )
    (near,), across = scatter_call(
        ring,
        width,
        low_parts,
        mixture_low,
        core,
        far,
        stages.ties + (far_one[0][0],),
        apart=False,
    )
    far_one, near, pair = settle(
        [ring.swap_core(f[0]) for f in far_one],
        near,
        ring.swap_side(*stages.hold(picked(scattered[0]))),
    )
    pairs_got = [pair]
    ((mine, other),) = settle(
        scatter_call(ring, width, [input_one], [raw_grad], core, far_one, stages.ties)
    )
    *back_one, grad_first = back_first_call(raw_grad, attention_full, token_rows, stages.ties)
    gains = jnp.concatenate(
        [
            arrange_vector(grad_first[0], steps),
            arrange_vector(grad_second[0], steps) * 0.5,
            grad_qgain[0],
            grad_kgain[0],
        ]
    )
    back_one_other = []
    distances = [1] + [4 * 2**k for k in range((steps - 1).bit_length())] + [2]

    def gains_sum(value, chosen):
        for distance in chosen:
            value = value + lax.ppermute(
                value, "dp", [(k, k ^ distance) for k in range(dp_size)]
            )
        return value

    def token_call(first, last, into, ties):
        ins = [
            (back_one[first:last], "parts"),
            (back_one_other[first:last], "parts"),
            (token_rows, first),
            (back_parts, "halves"),
            (gain_one, "all"),
        ]
        return row_call(
            functools.partial(token_kernel, turn),
            (last - first) * part,
            part,
            ins,
            [(model_width, jnp.float32)],
            ties=ties,
            into=(into, first, rows),
        )[0]

    token_grad = block_output = None
    sizes = (width, raw_grad.shape[1]), (width, query_columns)
    joined_columns = sizes[0][1] + sizes[1][1]
    sent = None
    for i in range(steps):
        moves = [ring.swap_side(*stages.hold(other[i]))]
        if i == 0:
            moves.append(ring.swap_side(across[0]))
        else:
            moves.append(ring.shift(sent, 1))
        others = []
        turns = {0: [0], 1: [1], 2: [2, 3]}.get(i, [])
        others.append([swap_tensor(back_one[k]) for k in turns])
        k = i - (steps - CHUNKS)
        if 0 <= k < CHUNKS - 1:
            last_pair = picked(scattered[1])[:, k * 3 * chunk : (k + 1) * 3 * chunk]
            others.append(ring.swap_side(*stages.hold(last_pair)))
        if i == 1:
            (block_output,) = row_call(
                functools.partial(output_kernel, turn),
                rows,
                128,
                [(middle_parts, "parts"), (out_sums, "halves"), (out_done, "halves")],
                [(model_width, jnp.bfloat16)],
                ties=stages.ties,
            )
            others.append(block_output)
        if i == steps - 1:
            token_grad = token_call(0, PARTS, None, stages.ties)
            others.append(token_grad)
            others.append(finish_call(ring, chunk, scattered, pairs_got))
        if i == 0:
            others.append(swap_tensor(out_sums[1]))
        if i < 2:
            others.append(gains_sum(gains, distances[:-1] if i == 0 else distances[-1:]))
        if i == steps - 1:
            others.append(gains + swap_tensor(gains))
        moves, others = settle(moves, others)
        others = list(others)
        side, hop = moves
        if i == 0:
            across, group, late = hop, [mine[0], side], [(near, (0, 0)), (hop, (0, 0), sizes[1])]
        else:
            group = [mine[i], (hop, (0, 0)), side]
            late = [
                (near, (i, 0)),
                (across, (i, 0)),
                (hop, (0, sizes[0][1] // sizes[1][1]), sizes[1]),
            ]
        if i < steps - 1:
            (sent,) = sums_call(
                (("open", joined_columns), group), (("close", sizes[0][1]), late)
            )
        else:
            grad_query, grad_key, grad_value, grad_output = sums_call(
                ((query_columns, key_columns, key_columns), group), ("turned", late)
            )
        if i < 2 or i == steps - 1:
            gains = others.pop()
        if i == 0:
            out_done.append(others.pop())
        if i == steps - 1:
            grads = others.pop()
            token_grad = others.pop()
        if i == 1:
            block_output = others.pop()
        if 0 <= k < CHUNKS - 1:
            pairs_got.append(others.pop())
        back_one_other += others.pop()
    if not tiled:
        token_grad, block_output = turned(token_grad), turned(block_output)
    grad_gate, grad_up, grad_down = grads

    index = lax.axis_index("dp")

    def own_part(start, size):
        return lax.dynamic_slice_in_dim(gains, start + index * (size // dp_size), size // dp_size)

    return (
        block_output,
        token_grad,
        own_part(0, model_width),
        grad_query,
        grad_key,
        grad_value,
        own_part(2 * model_width, HEAD_SIZE),
        own_part(2 * model_width + HEAD_SIZE, HEAD_SIZE),
        grad_output,
        own_part(model_width, model_width),
        grad_gate,
        grad_up,
        grad_down,
    )


def solution(mesh):
    return jax.shard_map(
        functools.partial(shards, mesh.shape["dp"]),
        mesh=mesh,
        in_specs=(
            P("dp", None),
            P("dp", None),
            P(),
            P("dp", "tensor"),
            P("dp", "tensor"),
            P("dp", "tensor"),
            P(),
            P(),
            P("tensor", "dp"),
            P(),
            P("dp", "tensor"),
            P("dp", "tensor"),
            P("tensor", "dp"),
            P("dp", None),
        ),
        out_specs=(
            P("dp", None),
            P("dp", None),
            P("dp"),
            P("dp", "tensor"),
            P("dp", "tensor"),
            P("dp", "tensor"),
            P("dp"),
            P("dp"),
            P("tensor", "dp"),
            P("dp"),
            P("dp", "tensor"),
            P("dp", "tensor"),
            P("tensor", "dp"),
        ),
        check_vma=False,
    )
```

```python
import functools

import jax
import jax.numpy as jnp
from jax import lax
from jax.experimental import pallas as pl
from jax.experimental.pallas import tpu as pltpu
from jax.sharding import PartitionSpec as P

HEAD_SIZE = 128
BLK = 64


epsilon = 1e-06
rope_base = 1000000.0


def matrix_product(left, right):
    return jnp.dot(left, right, preferred_element_type=jnp.float32)


def inner_left(left, right):
    return lax.dot_general(
        left, right, (((0,), (0,)), ((), ())), preferred_element_type=jnp.float32
    )


def inner_right(left, right):
    return lax.dot_general(
        left, right, (((1,), (1,)), ((), ())), preferred_element_type=jnp.float32
    )


def layout(lengths, count_of_rows):
    padded = (lengths + BLK - 1) // BLK * BLK
    starts = jnp.cumsum(padded) - padded
    row_index = jnp.arange(count_of_rows, dtype=jnp.int32)
    inside = (row_index[:, None] >= starts[None, :]) & (
        row_index[:, None] < (starts + lengths)[None, :]
    )
    live_rows = jnp.any(inside, axis=1)
    slot_index = jnp.arange(lengths.shape[0], dtype=jnp.int32)
    owning = jnp.sum(jnp.where(inside, slot_index[None, :], 0), axis=1)
    position = jnp.sum(jnp.where(inside, row_index[:, None] - starts[None, :], 0), axis=1)
    segment = jnp.where(live_rows, owning, -1 - row_index)
    return (live_rows, segment, position)


def rotation(position, width):
    half_width = width // 2
    frequency = jnp.power(rope_base, -(jnp.arange(half_width, dtype=jnp.float32) * 2.0) / width)
    angles = position.astype(jnp.float32)[:, None] * frequency[None, :]
    return (jnp.cos(angles)[:, None, :], jnp.sin(angles)[:, None, :])


CHUNKS = 3
PARTS = 4
LANES = 128
ROW_BLOCK = 256
VMEM_LIMIT = 56 * 1024 * 1024


def add_low(left, right):
    return (left.astype(jnp.float32) + right.astype(jnp.float32)).astype(jnp.bfloat16)


class Ring:
    def __init__(self, size):
        self.size = size
        self.steps = size // 4
        index = lax.axis_index("dp")
        self.place = index // 4
        self.side = (index // 2) % 2
        self.core = index % 2
        self.places = [(self.place - 1 - i) % self.steps for i in range(self.steps)]
        self.groups = [
            [place * 4 + side * 2 + core for place in range(self.steps) for core in range(2)]
            for side in range(2)
        ]

    def swap_core(self, value):
        return lax.ppermute(value, "dp", [(i, i ^ 1) for i in range(self.size)])

    def swap_side(self, value):
        return lax.ppermute(value, "dp", [(i, i ^ 2) for i in range(self.size)])

    def shift(self, value, places):
        return lax.ppermute(
            value, "dp", [(i, (i + 4 * places) % self.size) for i in range(self.size)]
        )

    def pick(self, value, axis):
        low, high = jnp.split(value, 2, axis=axis)
        return (
            jnp.where(self.side == 0, low, high),
            jnp.where(self.side == 0, high, low),
        )

    def ordered(self, mine, other, axis):
        return jnp.where(
            self.side == 0,
            jnp.concatenate([mine, other], axis=axis),
            jnp.concatenate([other, mine], axis=axis),
        )

    def block(self, back, core, side):
        return ((self.place - back) % self.steps) * 4 + core * 2 + side


class Gather:
    def __init__(self, ring, piece):
        self.ring = ring
        self.hops, self.across, self.index = [piece], [], 0
        self.pieces, self.order = [], []

    def put(self, back, core, side, value):
        self.pieces.append(value)
        self.order.append(self.ring.block(back, core, side))

    def start(self, stages, hop=True, swap=1):
        ring, moves = self.ring, {}
        self.hops = list(stages.hold(*self.hops))
        if hop and len(self.hops) < ring.steps:
            moves["hop"] = ring.shift(self.hops[-1], 1)
        if swap:
            pieces = self.hops[self.index : self.index + swap]
            moves["side"] = [ring.swap_side(p) for p in pieces]
            moves["core"] = [ring.swap_core(p) for p in pieces]
            moves["both"] = [ring.swap_core(p) for p in self.across]
        return moves

    def finish(self, moves):
        ring = self.ring
        core, side = ring.core, ring.side
        if "hop" in moves:
            self.hops.append(moves["hop"])
        if "side" not in moves:
            return
        first = self.index - len(self.across)
        for back, value in enumerate(moves["both"], first):
            self.put(back, 1 - core, 1 - side, value)
        self.across = moves["side"]
        for back, (aside, other) in enumerate(zip(moves["side"], moves["core"]), self.index):
            self.put(back, core, side, self.hops[back])
            self.put(back, core, 1 - side, aside)
            self.put(back, 1 - core, side, other)
        self.index += len(moves["side"])

    @property
    def done(self):
        return len(self.pieces) == self.ring.size


class Stages:
    def __init__(self, mark):
        self.mark = mark

    def settle(self, *values):
        values, self.mark = lax.optimization_barrier((values, self.mark))
        return values

    def step(self, movers, *others):
        movers = [mover if isinstance(mover, tuple) else (mover, {}) for mover in movers]
        moves = [mover.start(self, **kind) for mover, kind in movers]
        moves, others = self.settle(moves, others)
        for (mover, _), move in zip(movers, moves):
            mover.finish(move)
        return others

    def hold(self, *values):
        return lax.optimization_barrier((values, self.mark))[0]

    @property
    def ties(self):
        return (self.mark,)


def swap_tensor(value):
    return lax.ppermute(value, "tensor", [(0, 1), (1, 0)])


def arrange(value, steps, width):
    blocks = [value[:, i * width : (i + 1) * width] for i in range(4 * steps)]
    order = [4 * place + k for place in range(steps) for k in (0, 2, 1, 3)]
    return jnp.concatenate([blocks[i] for i in order], axis=1)


def arrange_vector(vector, steps):
    return vector.reshape(steps, 2, 2, -1).swapaxes(1, 2).reshape(-1)


def sums_kernel(kinds, counts, *refs):
    ins, outs = refs[: sum(counts)], list(refs[sum(counts) :])
    for kind, count in zip(kinds, counts):
        group, ins = ins[:count], ins[count:]
        total = group[0][...].astype(jnp.float32)
        for ref in group[1:]:
            total = total + ref[...].astype(jnp.float32)
        if kind == "low":
            outs.pop(0)[...] = total.astype(jnp.bfloat16)
        elif kind == "turned":
            outs.pop(0)[...] = total.T
        elif kind[0] == "open":
            joined = outs.pop(0)
            joined[:, : total.shape[1]] = total.astype(jnp.bfloat16)
        elif kind[0] == "close":
            joined[:, kind[1] : kind[1] + total.shape[1]] = total.astype(jnp.bfloat16)
        else:
            first = 0
            for width in kind:
                outs.pop(0)[...] = total[:, first : first + width]
                first += width


def sums_call(*groups):
    shapes = []
    for kind, arrays in groups:
        rows, columns = arrays[-1][-1] if isinstance(arrays[-1], tuple) else arrays[-1].shape
        if kind[0] == "open":
            shapes.append(jax.ShapeDtypeStruct((rows, kind[1]), jnp.bfloat16))
        elif kind[0] == "close":
            continue
        elif kind == "low":
            shapes.append(jax.ShapeDtypeStruct((rows, columns), jnp.bfloat16))
        elif kind == "turned":
            shapes.append(jax.ShapeDtypeStruct((columns, rows), jnp.float32))
        else:
            shapes += [jax.ShapeDtypeStruct((rows, w), jnp.float32) for w in kind]
    ins, specs = [], []
    for _, arrays in groups:
        shape = arrays[-1][-1] if isinstance(arrays[-1], tuple) else arrays[-1].shape
        for a in arrays:
            a, *block = a if isinstance(a, tuple) else (a, (0, 0))
            ins.append(a)
            specs.append(pl.BlockSpec(shape, lambda i, block=block[0]: block))
    return pl.pallas_call(
        functools.partial(sums_kernel, [k for k, _ in groups], [len(a) for _, a in groups]),
        grid=(1,),
        in_specs=specs,
        out_specs=[pl.BlockSpec(shape.shape, lambda i: (0, 0)) for shape in shapes],
        out_shape=shapes,
        compiler_params=pltpu.CompilerParams(vmem_limit_bytes=VMEM_LIMIT),
        cost_estimate=pl.CostEstimate(
            flops=0, bytes_accessed=4 * sum(a.size for a in ins), transcendentals=0
        ),
    )(*ins)


def loose(ties):
    return [pl.BlockSpec(memory_space=pl.ANY) for _ in ties]


def row_call(kernel, rows, block, ins, outs, sums=(), ties=(), into=None):
    arrays, specs, places, cuts = [], [], [], 1
    for value, kind in ins:
        places.append(len(arrays))
        if kind in ("parts", "halves"):
            if kind == "parts":
                cuts = len(value)
            span = rows // len(value) // block
            for k, piece in enumerate(value):
                arrays.append(piece)
                specs.append(
                    pl.BlockSpec(
                        (block, piece.shape[1]),
                        lambda i, k=k, span=span: (jnp.clip(i - k * span, 0, span - 1), 0),
                    )
                )
            continue
        arrays.append(value)
        if kind == "all":
            specs.append(pl.BlockSpec(value.shape, lambda i: (0, 0)))
        else:
            first = 0 if kind == "rows" else kind
            specs.append(
                pl.BlockSpec((block, value.shape[1]), lambda i, first=first: (first + i, 0))
            )
    base, all_rows, aliases = 0, rows, {}
    count = len(arrays)
    if into is not None:
        given, base, all_rows = into
        if given is not None:
            ties = (given, *ties)
            aliases = {count: 0}
    out_specs = [pl.BlockSpec((block, c), lambda i: (base + i, 0)) for c, _ in outs]
    out_specs += [pl.BlockSpec((1, c), lambda i: (0, 0)) for c in sums]
    out_shape = [jax.ShapeDtypeStruct((all_rows, c), d) for c, d in outs]
    out_shape += [jax.ShapeDtypeStruct((1, c), jnp.float32) for c in sums]
    moved = sum(a.size * a.dtype.itemsize for a in arrays)
    moved += sum(rows * c * jnp.dtype(d).itemsize for c, d in outs)

    def body(*refs):
        given = refs[count + len(ties) :]
        if cuts == 1:
            kernel(*refs[:count], *given)
            return
        turn = pl.program_id(0) // (rows // cuts // block)
        for k in range(cuts):
            chosen = [
                refs[place + k * len(value) // cuts]
                if kind in ("parts", "halves")
                else refs[place]
                for place, (value, kind) in zip(places, ins)
            ]
            pl.when(turn == k)(functools.partial(kernel, *chosen, *given))

    return pl.pallas_call(
        body,
        grid=(rows // block,),
        in_specs=specs + loose(ties),
        out_specs=out_specs,
        out_shape=out_shape,
        input_output_aliases=aliases,
        compiler_params=pltpu.CompilerParams(vmem_limit_bytes=VMEM_LIMIT),
        cost_estimate=pl.CostEstimate(flops=0, bytes_accessed=moved, transcendentals=0),
    )(*arrays, *ties)


def inverse_rms(value):
    return lax.rsqrt(jnp.mean(value * value, axis=-1, keepdims=True) + epsilon)


def first_kernel(turn, tokens, cotangent, live, gain, tokens_out, upstream_out, normed_out):
    value = turn(tokens[...])
    tokens_out[...] = value
    value = value.astype(jnp.float32)
    normed_out[...] = (value * inverse_rms(value) * gain[...]).astype(jnp.bfloat16)
    back = turn(cotangent[...]).astype(jnp.float32)
    upstream_out[...] = (back * live[...]).astype(jnp.bfloat16)


def middle_kernel(tokens, mine, other, gain, middle_out, normed_out):
    branch = mine[...].astype(jnp.float32) + other[...].astype(jnp.float32)
    value = tokens[...].astype(jnp.float32) + branch
    middle_out[...] = value
    normed_out[...] = (value * inverse_rms(value) * gain[...]).astype(jnp.bfloat16)


def back_rms(value, gain, back):
    scale = inverse_rms(value)
    normed = value * scale
    pulled = back * gain
    center = jnp.mean(pulled * normed, axis=-1, keepdims=True)
    return scale * (pulled - normed * center), back * normed


def add_sum(out_ref, value):
    @pl.when(pl.program_id(0) == 0)
    def _():
        out_ref[...] = jnp.zeros_like(out_ref)

    out_ref[...] += jnp.sum(value, axis=0, keepdims=True)


def back_middle_kernel(
    mine, other, middle, upstream, gain, full, back_out, low_out, mixed_out, gain_out
):
    back = mine[...].astype(jnp.float32) + other[...].astype(jnp.float32)
    value, gain_term = back_rms(middle[...], gain[...], back)
    value = value + upstream[...].astype(jnp.float32)
    back_out[...] = value
    low = value.astype(jnp.bfloat16)
    low_out[...] = low
    mixed_out[...] = matrix_product(low, full[...]).astype(jnp.bfloat16)
    add_sum(gain_out, gain_term)


def output_kernel(turn, middle, mine, other, out):
    value = middle[...] + mine[...].astype(jnp.float32) + other[...].astype(jnp.float32)
    out[...] = turn(value).astype(jnp.bfloat16)


def token_kernel(turn, mine, other, tokens, back_middle, gain, out):
    back = mine[...].astype(jnp.float32) + other[...].astype(jnp.float32)
    value, _ = back_rms(tokens[...].astype(jnp.float32), gain[...], back)
    out[...] = turn(value + back_middle[...])


def feed_kernel(chunk, count, many, *refs):
    full, out = refs[count], refs[-1]
    block = out.shape[0]

    def picked(group, step):
        refs_of = refs[group[0] : group[1]]
        if len(refs_of) == 1:
            return refs_of[0][...]
        each = block // refs_of[0].shape[0]
        return jnp.concatenate([r[...] for r in refs_of[step * each : (step + 1) * each]], axis=0)

    def run(step):
        normed, upstream = picked((0, many), step), picked((many, count), step)
        gate = matrix_product(normed, full[:, :chunk])
        up = matrix_product(normed, full[:, chunk : 2 * chunk])
        back = matrix_product(upstream, full[:, 2 * chunk :])
        share = jax.nn.sigmoid(gate)
        active = gate * share
        out[:, :chunk] = (back * up * (share * (1.0 + gate * (1.0 - share)))).astype(jnp.bfloat16)
        out[:, chunk : 2 * chunk] = (back * active).astype(jnp.bfloat16)
        out[:, 2 * chunk :] = (active * up).astype(jnp.bfloat16)

    for step in range(2):
        pl.when(pl.program_id(0) == step)(functools.partial(run, step))


def feed_call(normed, upstream, full, ties=()):
    groups = [g if isinstance(g, list) else [g] for g in (normed, upstream)]
    rows, model_width = sum(a.shape[0] for a in groups[0]), full.shape[0]
    columns = full.shape[1]
    block = rows // 2
    specs = []
    for group in groups:
        if len(group) == 1:
            specs.append(pl.BlockSpec((block, model_width), lambda i: (i, 0)))
        else:
            specs += [pl.BlockSpec(a.shape, lambda i: (0, 0)) for a in group]
    return pl.pallas_call(
        functools.partial(feed_kernel, columns // 3, len(specs), len(groups[0])),
        grid=(2,),
        in_specs=specs + [pl.BlockSpec(full.shape, lambda i: (0, 0))] + loose(ties),
        out_specs=pl.BlockSpec((block, columns), lambda i: (i, 0)),
        out_shape=jax.ShapeDtypeStruct((rows, columns), jnp.bfloat16),
        compiler_params=pltpu.CompilerParams(vmem_limit_bytes=VMEM_LIMIT),
        cost_estimate=pl.CostEstimate(
            flops=2 * rows * model_width * columns,
            bytes_accessed=2 * (2 * rows * model_width + full.size + rows * columns),
            transcendentals=rows * columns // 3,
        ),
    )(*groups[0], *groups[1], full, *ties)


def wide_kernel(count, started, parts, *refs):
    outs, total = refs[-parts:], None
    for act, full in zip(refs[:count], refs[count : 2 * count]):
        term = inner_right(act[...], full[...])
        total = term if total is None else total + term
    if started:
        total = total + refs[2 * count][...]
    part = outs[0].shape[0]
    for i, out in enumerate(outs):
        out[...] = total[i * part : (i + 1) * part].astype(out.dtype)


def wide_call(acts, fulls, span, out_dtype, start=None, ties=(), parts=PARTS):
    lo, hi = span
    size, index = hi - lo, lo // (hi - lo)
    rows, model_width, count = acts[0].shape[0], fulls[0].shape[0], len(acts)
    tile = 512
    ins = list(acts) + list(fulls)
    specs = [pl.BlockSpec((rows, size), lambda i: (0, index))] * count
    specs += [pl.BlockSpec((tile, size), lambda i: (i, index))] * count
    if start is not None:
        ins.append(start)
        specs.append(pl.BlockSpec((rows, tile), lambda i: (0, i)))
    ins += list(ties)
    specs += [pl.BlockSpec(memory_space=pl.ANY) for _ in ties]
    return pl.pallas_call(
        functools.partial(wide_kernel, count, start is not None, parts),
        grid=(model_width // tile,),
        in_specs=specs,
        out_specs=[pl.BlockSpec((rows // parts, tile), lambda i: (0, i))] * parts,
        out_shape=[jax.ShapeDtypeStruct((rows // parts, model_width), out_dtype)] * parts,
        compiler_params=pltpu.CompilerParams(vmem_limit_bytes=VMEM_LIMIT),
        cost_estimate=pl.CostEstimate(
            flops=2 * rows * model_width * size * count,
            bytes_accessed=2 * (rows + model_width) * size * count + rows * model_width * 6,
            transcendentals=0,
        ),
    )(*ins)


def grad_kernel(split, counts, *refs):
    out = refs[-1]
    acts = refs[sum(counts) : sum(counts) + 2]
    first = 0
    total = [0.0, 0.0]
    for group, count in enumerate(counts):
        rows, act = 0, acts[group % 2]
        columns = slice(0, split) if group < 2 else slice(split, None)
        parts = [r[...] for r in refs[first : first + count]]
        left = parts[0] if count == 1 else jnp.concatenate(parts, axis=0)
        total[group // 2] = total[group // 2] + inner_left(left, act[:, columns])
        first += count
    out[:, :split] = total[0].astype(jnp.bfloat16)
    out[:, split:] = total[1].astype(jnp.bfloat16)


def grad_call(normed, upstream, acts, ties=(), place=0, places=1, into=None):
    groups = [g if isinstance(g, list) else [g] for g in (*normed, *upstream)]
    lefts = [a for group in groups for a in group]
    rows, model_width = acts[0].shape[0], lefts[0].shape[1]
    columns = acts[0].shape[1]
    tall = 512
    ins = lefts + list(acts)
    specs = [pl.BlockSpec((a.shape[0], tall), lambda i: (0, i)) for a in lefts]
    specs += [pl.BlockSpec((rows, columns), lambda i: (0, 0))] * 2
    aliases = {}
    if into is not None:
        aliases = {len(ins): 0}
        ins.append(into)
        specs.append(pl.BlockSpec(memory_space=pl.ANY))
    return pl.pallas_call(
        functools.partial(grad_kernel, columns // 3 * 2, [len(g) for g in groups]),
        grid=(model_width // tall,),
        in_specs=specs + loose(ties),
        out_specs=pl.BlockSpec((tall, columns), lambda i: (i, place)),
        out_shape=jax.ShapeDtypeStruct((model_width, places * columns), jnp.bfloat16),
        input_output_aliases=aliases,
        compiler_params=pltpu.CompilerParams(vmem_limit_bytes=VMEM_LIMIT),
        cost_estimate=pl.CostEstimate(
            flops=4 * rows * model_width * columns,
            bytes_accessed=2 * (4 * rows * model_width + 2 * rows * columns + model_width * columns),
            transcendentals=0,
        ),
    )(*ins, *ties)


def norm_rope(raw, gain, cosine, sine):
    scale = inverse_rms(raw)
    normed = raw * scale
    scaled = normed * gain
    return scaled * cosine + pltpu.roll(scaled, HEAD_SIZE // 2, 1) * sine, normed, scale


def back_norm_rope(back, normed, scale, gain, cosine, sine):
    back = back * cosine - pltpu.roll(back, HEAD_SIZE // 2, 1) * sine
    pulled = back * gain
    center = jnp.mean(pulled * normed, axis=-1, keepdims=True)
    return scale * (pulled - normed * center), back * normed


def allowed_pairs(segment_column, segment_row, first, count):
    height = first + count
    key = lax.broadcasted_iota(jnp.int32, (height, count), 0)
    query = lax.broadcasted_iota(jnp.int32, (height, count), 1) + first
    same = segment_column[:height, :] == segment_row[:, first:height]
    return same & (key <= query)


def attend_kernel(
    start, queries, keys, values, query_gain, key_gain, cosine, sine, seg_column, seg_row, *rest
):
    out, total_out = rest[-2:]
    size, rows = queries.shape[0], keys.shape[0]
    key = norm_rope(keys[...], key_gain[...], cosine[:rows, :], sine[:rows, :])[0]
    key = key.astype(jnp.bfloat16)
    value = values[...].T.astype(jnp.bfloat16)
    spans = [slice(lo, lo + HEAD_SIZE) for lo in range(0, queries.shape[1], HEAD_SIZE)]
    turn = cosine[start : start + size, :], sine[start : start + size, :]
    heads = [
        norm_rope(queries[:, span], query_gain[...], *turn)[0].astype(jnp.bfloat16)
        for span in spans
    ]
    for first in range(0, size, ROW_BLOCK):
        here = slice(first, first + ROW_BLOCK)
        end = start + first + ROW_BLOCK
        allowed = allowed_pairs(seg_column, seg_row, start + first, ROW_BLOCK)
        for k, (span, query) in enumerate(zip(spans, heads)):
            scores = inner_right(key[:end], query[here]) * HEAD_SIZE ** (-0.5)
            scores = jnp.where(allowed, scores, -1e30)
            largest = jnp.max(scores, axis=0, keepdims=True)
            raised = jnp.exp(scores - largest)
            total = jnp.sum(raised, axis=0, keepdims=True)
            weights = (raised * (1.0 / total)).astype(jnp.bfloat16)
            mixed = matrix_product(value[:, :end], weights)
            out[here, span] = mixed.T.astype(jnp.bfloat16)
            total_out[k : k + 1, here] = largest + jnp.log(total)


def attend_back_kernel(
    query_columns,
    key_columns,
    queries,
    keys,
    values,
    query_gain,
    key_gain,
    cosine,
    sine,
    seg_column,
    seg_row,
    totals,
    *rest,
):
    out, query_gain_out, key_gain_out = rest[-3:]
    back_parts = rest[:2]
    head = pl.program_id(0)
    rows, wide = queries.shape
    scaling = HEAD_SIZE ** (-0.5)
    cosine, sine = cosine[...], sine[...]
    key, key_normed, key_scale = norm_rope(keys[...], key_gain[...], cosine, sine)
    turned = key.T.astype(jnp.bfloat16)
    key = key.astype(jnp.bfloat16)
    value = values[...].astype(jnp.bfloat16)
    back_mixture = jnp.concatenate([b[...] for b in back_parts], axis=0)
    spans = [slice(lo, lo + HEAD_SIZE) for lo in range(0, wide, HEAD_SIZE)]
    heads = [norm_rope(queries[:, span], query_gain[...], cosine, sine) for span in spans]
    back_queries = [[] for _ in spans]
    back_key, back_value = None, None
    for first in range(0, rows, ROW_BLOCK):
        end = first + ROW_BLOCK
        allowed = allowed_pairs(seg_column, seg_row, first, ROW_BLOCK)
        key_term, value_term = 0.0, 0.0
        for k, span in enumerate(spans):
            query = heads[k][0][first:end].astype(jnp.bfloat16)
            back = back_mixture[first:end, span]
            scores = inner_right(key[:end], query) * scaling
            weights = jnp.where(allowed, jnp.exp(scores - totals[k : k + 1, first:end]), 0.0)
            terms = inner_right(value[:end], back) * weights
            value_term = value_term + matrix_product(weights.astype(jnp.bfloat16), back)
            center = jnp.sum(terms, axis=0, keepdims=True)
            back_scores = (terms - weights * center).astype(jnp.bfloat16)
            back_queries[k].append(matrix_product(turned[:, :end], back_scores).T * scaling)
            key_term = key_term + matrix_product(back_scores, query) * scaling
        if back_key is None:
            back_key, back_value = key_term, value_term
        else:
            back_key = jnp.concatenate([back_key + key_term[:first], key_term[first:]], axis=0)
            back_value = jnp.concatenate(
                [back_value + value_term[:first], value_term[first:]], axis=0
            )
    query_term = 0.0
    for k, (lo, (_, normed, scale)) in enumerate(zip(range(0, wide, HEAD_SIZE), heads)):
        back_query, term = back_norm_rope(
            jnp.concatenate(back_queries[k], axis=0), normed, scale, query_gain[...], cosine, sine
        )
        query_term = query_term + term
        start = pl.multiple_of(head * wide + lo, HEAD_SIZE)
        out[:, pl.ds(start, HEAD_SIZE)] = back_query.astype(jnp.bfloat16)
    back_key, key_sum = back_norm_rope(
        back_key, key_normed, key_scale, key_gain[...], cosine, sine
    )
    start = pl.multiple_of(query_columns + head * HEAD_SIZE, HEAD_SIZE)
    out[:, pl.ds(start, HEAD_SIZE)] = back_key.astype(jnp.bfloat16)
    start = pl.multiple_of(query_columns + key_columns + head * HEAD_SIZE, HEAD_SIZE)
    out[:, pl.ds(start, HEAD_SIZE)] = back_value.astype(jnp.bfloat16)
    add_sum(query_gain_out, query_term)
    add_sum(key_gain_out, key_sum)


def attention_call(raw, query_columns, key_columns, gains, tables, segment, span, back=None, totals=None, ties=()):
    rows, columns = raw.shape
    start, end = span
    count = key_columns // HEAD_SIZE
    wide = query_columns * HEAD_SIZE // key_columns
    first_key = query_columns // HEAD_SIZE
    first_value = first_key + key_columns // HEAD_SIZE
    ins = [raw, raw, raw, *gains, *tables, segment[:, None], segment[None, :]]
    size = end - start
    specs = [
        pl.BlockSpec((size, wide), lambda h: (start // size, h)),
        pl.BlockSpec((end, HEAD_SIZE), lambda h: (0, first_key + h)),
        pl.BlockSpec((end, HEAD_SIZE), lambda h: (0, first_value + h)),
    ] + [pl.BlockSpec(a.shape, lambda h: (0, 0)) for a in ins[3:]]
    params = dict(
        grid=(count,),
        compiler_params=pltpu.CompilerParams(vmem_limit_bytes=VMEM_LIMIT),
    )
    pairs = count * wide // HEAD_SIZE * rows * rows
    if back is None:
        return pl.pallas_call(
            functools.partial(attend_kernel, start),
            in_specs=specs + loose(ties),
            out_specs=[
                pl.BlockSpec((size, wide), lambda h: (0, h)),
                pl.BlockSpec((8, size), lambda h: (h, 0)),
            ],
            out_shape=[
                jax.ShapeDtypeStruct((size, count * wide), jnp.bfloat16),
                jax.ShapeDtypeStruct((count * 8, size), jnp.float32),
            ],
            cost_estimate=pl.CostEstimate(
                flops=4 * pairs * HEAD_SIZE, bytes_accessed=5 * raw.size, transcendentals=pairs
            ),
            **params,
        )(*ins, *ties)
    gain_spec = pl.BlockSpec((1, HEAD_SIZE), lambda h: (0, 0))
    gain_shape = jax.ShapeDtypeStruct((1, HEAD_SIZE), jnp.float32)
    return pl.pallas_call(
        functools.partial(attend_back_kernel, query_columns, key_columns),
        in_specs=specs
        + [pl.BlockSpec((8, rows), lambda h: (h, 0))]
        + [pl.BlockSpec((b.shape[0], wide), lambda h: (0, h)) for b in back]
        + loose(ties),
        out_specs=[pl.BlockSpec((rows, columns), lambda h: (0, 0)), gain_spec, gain_spec],
        out_shape=[jax.ShapeDtypeStruct((rows, columns), jnp.bfloat16), gain_shape, gain_shape],
        cost_estimate=pl.CostEstimate(
            flops=12 * pairs * HEAD_SIZE, bytes_accessed=8 * raw.size, transcendentals=pairs
        ),
        **params,
    )(*ins, totals, *back, *ties)


def back_first_kernel(raw_grad, full, tokens, *rest):
    outs, gain_out, scale = rest[-2 - PARTS : -2], rest[-2], rest[-1]
    part, tile = outs[0].shape

    @pl.when(pl.program_id(0) == 0)
    def _():
        scale[...] = inverse_rms(tokens[...].astype(jnp.float32))

    back = inner_right(raw_grad[...], full[...])
    for i, out in enumerate(outs):
        out[...] = back[i * part : (i + 1) * part].astype(jnp.bfloat16)
    start = pl.multiple_of(pl.program_id(0) * tile, tile)
    normed = tokens[:, pl.ds(start, tile)].astype(jnp.float32) * scale[...]
    gain_out[...] = jnp.sum(back * normed, axis=0, keepdims=True)


def back_first_call(raw_grad, full, tokens, ties=()):
    rows, model_width = tokens.shape
    tile, part = 512, rows // PARTS
    return pl.pallas_call(
        back_first_kernel,
        grid=(model_width // tile,),
        in_specs=[
            pl.BlockSpec(raw_grad.shape, lambda i: (0, 0)),
            pl.BlockSpec((tile, full.shape[1]), lambda i: (i, 0)),
            pl.BlockSpec(tokens.shape, lambda i: (0, 0)),
        ]
        + [pl.BlockSpec(memory_space=pl.ANY) for _ in ties],
        out_specs=[pl.BlockSpec((part, tile), lambda i: (0, i))] * PARTS
        + [pl.BlockSpec((1, tile), lambda i: (0, i))],
        out_shape=[jax.ShapeDtypeStruct((part, model_width), jnp.bfloat16)] * PARTS
        + [jax.ShapeDtypeStruct((1, model_width), jnp.float32)],
        scratch_shapes=[pltpu.VMEM((rows, 1), jnp.float32)],
        compiler_params=pltpu.CompilerParams(vmem_limit_bytes=VMEM_LIMIT),
        cost_estimate=pl.CostEstimate(
            flops=2 * rows * full.size,
            bytes_accessed=2 * full.size + 8 * tokens.size,
            transcendentals=0,
        ),
    )(raw_grad, full, tokens, *ties)


def scatter_kernel(width, steps, lefts, rights, gots, ties, flipped, info, *refs):
    turned, outs = refs[-1], refs[lefts + rights + gots + ties : -1]
    left, right = refs[:lefts], refs[lefts : lefts + rights]
    got = refs[lefts + rights : lefts + rights + gots]
    size = steps * width

    @pl.when(pl.program_id(0) == 0)
    def _():
        for k in range(2):
            side = info[1] if k == 0 else 1 - info[1]
            for i in range(steps):
                start = pl.multiple_of((info[2 + i] * 4 + info[0] * 2 + side) * width, width)
                first, row = 0, k * size + i * width
                if flipped:
                    turned[row : row + width, :] = left[0][pl.ds(start, width), :]
                    continue
                for part in left:
                    block = part[:, pl.ds(start, width)].T
                    turned[row : row + width, first : first + part.shape[0]] = block
                    first += part.shape[0]

    joined = right[0][...]
    if rights > 1:
        joined = jnp.concatenate([r[...] for r in right], axis=0)
    total = matrix_product(turned[...], joined)
    for k in range(2):
        value = total[k * size : (k + 1) * size]
        if gots:
            value = value + got[k][...].astype(jnp.float32)
        value = value.astype(jnp.bfloat16)
        each = len(outs) // 2
        rows = size // each
        for i in range(each):
            outs[k * each + i][...] = value[i * rows : (i + 1) * rows]


def scatter_call(ring, width, left, right, core, got=(), ties=(), apart=True, flipped=False):
    rows, columns = sum(r.shape[0] for r in right), right[0].shape[1]
    steps = ring.steps
    each = steps if apart else 1
    if 2 * width % LANES:
        left = left[0].T if flipped else jnp.concatenate(left, axis=0)
        blocks = left.reshape(rows, steps, 2, 2, width)
        right = jnp.concatenate(right, axis=0)
        outs = []
        for k, side in enumerate((ring.side, 1 - ring.side)):
            for i, place in enumerate(ring.places):
                picked = lax.dynamic_slice(
                    blocks, (0, place, core, side, 0), (rows, 1, 1, 1, width)
                )
                total = inner_left(picked.reshape(rows, width), right)
                if got:
                    total = total + got[k][i * width : (i + 1) * width].astype(jnp.float32)
                outs.append(total.astype(jnp.bfloat16))
        if apart:
            return outs[:steps], outs[steps:]
        return [jnp.concatenate(outs[:steps])], [jnp.concatenate(outs[steps:])]
    info = jnp.stack([core, ring.side] + ring.places).astype(jnp.int32)
    tile, tall = 512, steps * width // each
    outs = pl.pallas_call(
        functools.partial(
            scatter_kernel, width, steps, len(left), len(right), len(got), len(ties), flipped
        ),
        grid_spec=pltpu.PrefetchScalarGridSpec(
            num_scalar_prefetch=1,
            grid=(columns // tile,),
            in_specs=[pl.BlockSpec(a.shape, lambda i, info: (0, 0)) for a in left]
            + [pl.BlockSpec((r.shape[0], tile), lambda i, info: (0, i)) for r in right]
            + [pl.BlockSpec((steps * width, tile), lambda i, info: (0, i)) for _ in got]
            + loose(ties),
            out_specs=[pl.BlockSpec((tall, tile), lambda i, info: (0, i))] * (2 * each),
            scratch_shapes=[pltpu.VMEM((2 * steps * width, rows), jnp.bfloat16)],
        ),
        out_shape=[jax.ShapeDtypeStruct((tall, columns), jnp.bfloat16)] * (2 * each),
        compiler_params=pltpu.CompilerParams(vmem_limit_bytes=VMEM_LIMIT),
        cost_estimate=pl.CostEstimate(
            flops=4 * rows * steps * width * columns,
            bytes_accessed=2 * rows * (columns + 16 * width) + 4 * steps * width * columns,
            transcendentals=0,
        ),
    )(info, *left, *right, *got, *ties)
    return outs[:each], outs[each:]


def finish_kernel(chunk, counts, info, *refs):
    count = len(counts)
    totals, others, (gate, up, down) = refs[:count], refs[count:-3], refs[-3:]
    side, width = info[0], gate.shape[0]
    half = gate.shape[1] // 2
    values = []
    for total, chunks in zip(totals, counts):
        mine = total[pl.ds(pl.multiple_of(side * width, width), width), :]
        values += [(mine[:, 3 * j * chunk : 3 * (j + 1) * chunk], side) for j in range(chunks)]
    values += [(other[...], 1 - side) for other in others]
    for j, (value, at) in enumerate(values):
        value = value.astype(jnp.float32)
        start = pl.multiple_of(at * half + j % CHUNKS * chunk, chunk)
        gate[:, pl.ds(start, chunk)] = value[:, :chunk]
        up[:, pl.ds(start, chunk)] = value[:, chunk : 2 * chunk]
        down[pl.ds(start, chunk), :] = value[:, 2 * chunk :].T


def finish_call(ring, chunk, totals, others):
    width, hidden = others[0].shape[0], 2 * CHUNKS * chunk
    counts = [a.shape[1] // (3 * chunk) for a in totals]
    shapes = [(width, hidden), (width, hidden), (hidden, width)]
    whole = [pl.BlockSpec(a.shape, lambda i, info: (0, 0)) for a in (*totals, *others)]
    return pl.pallas_call(
        functools.partial(finish_kernel, chunk, counts),
        grid_spec=pltpu.PrefetchScalarGridSpec(
            num_scalar_prefetch=1,
            grid=(1,),
            in_specs=whole,
            out_specs=[pl.BlockSpec(shape, lambda i, info: (0, 0)) for shape in shapes],
        ),
        out_shape=[jax.ShapeDtypeStruct(shape, jnp.float32) for shape in shapes],
        compiler_params=pltpu.CompilerParams(vmem_limit_bytes=VMEM_LIMIT),
        cost_estimate=pl.CostEstimate(
            flops=0, bytes_accessed=18 * hidden * width, transcendentals=0
        ),
    )(jnp.stack([ring.side]).astype(jnp.int32), *totals, *others)


def join_kernel(width, count, order, left, *rest):
    pieces, (product, whole) = rest[:count], rest[count:]
    for i, piece in enumerate(pieces):
        whole[pl.ds(pl.multiple_of(order[i] * width, width), width), :] = piece[...]
    product[...] = matrix_product(left[...], whole[...])


def join_call(gather, left):
    width, columns = gather.pieces[0].shape
    rows, model_width = left.shape
    tile = columns // 2
    count = len(gather.pieces)
    return pl.pallas_call(
        functools.partial(join_kernel, width, count),
        grid_spec=pltpu.PrefetchScalarGridSpec(
            num_scalar_prefetch=1,
            grid=(columns // tile,),
            in_specs=[pl.BlockSpec((rows, model_width), lambda i, order: (0, 0))]
            + [pl.BlockSpec((width, tile), lambda i, order: (0, i))] * count,
            out_specs=[
                pl.BlockSpec((rows, tile), lambda i, order: (0, i)),
                pl.BlockSpec((model_width, tile), lambda i, order: (0, i)),
            ],
        ),
        out_shape=[
            jax.ShapeDtypeStruct((rows, columns), jnp.float32),
            jax.ShapeDtypeStruct((model_width, columns), jnp.bfloat16),
        ],
        compiler_params=pltpu.CompilerParams(vmem_limit_bytes=VMEM_LIMIT),
        cost_estimate=pl.CostEstimate(
            flops=2 * rows * model_width * columns,
            bytes_accessed=4 * model_width * columns + 4 * rows * columns,
            transcendentals=0,
        ),
    )(jnp.stack(gather.order).astype(jnp.int32), left, *gather.pieces)


def join_wide_kernel(width, count, order, left, *rest):
    pieces, whole, total, outs = rest[:count], rest[count], rest[-1], rest[count + 1 : -1]
    for i, piece in enumerate(pieces):
        whole[pl.ds(pl.multiple_of(order[i] * width, width), width), :] = piece[...]
    term = inner_right(left[...], whole[...])

    @pl.when(pl.program_id(0) == 0)
    def _():
        total[...] = term

    @pl.when(pl.program_id(0) == 1)
    def _():
        part = outs[0].shape[0]
        for i, out in enumerate(outs):
            value = total[i * part : (i + 1) * part, :] + term[i * part : (i + 1) * part]
            out[...] = value.astype(jnp.bfloat16)


def join_wide_call(gather, left, part):
    width, columns = gather.pieces[0].shape
    rows, model_width = left.shape[0], width * len(gather.pieces)
    tile, parts = columns // 2, rows // part
    count = len(gather.pieces)
    return pl.pallas_call(
        functools.partial(join_wide_kernel, width, count),
        grid_spec=pltpu.PrefetchScalarGridSpec(
            num_scalar_prefetch=1,
            grid=(2,),
            in_specs=[pl.BlockSpec((rows, tile), lambda i, order: (0, i))]
            + [pl.BlockSpec((width, tile), lambda i, order: (0, i))] * count,
            out_specs=[pl.BlockSpec((model_width, tile), lambda i, order: (0, i))]
            + [pl.BlockSpec((part, model_width), lambda i, order: (0, 0))] * parts,
            scratch_shapes=[pltpu.VMEM((rows, model_width), jnp.float32)],
        ),
        out_shape=[jax.ShapeDtypeStruct((model_width, columns), jnp.bfloat16)]
        + [jax.ShapeDtypeStruct((part, model_width), jnp.bfloat16)] * parts,
        compiler_params=pltpu.CompilerParams(vmem_limit_bytes=VMEM_LIMIT),
        cost_estimate=pl.CostEstimate(
            flops=2 * rows * model_width * columns,
            bytes_accessed=4 * model_width * columns + 4 * rows * model_width,
            transcendentals=0,
        ),
    )(jnp.stack(gather.order).astype(jnp.int32), left, *gather.pieces)


def rows_product_kernel(left, right, *outs):
    outs = outs[-2:]
    total = inner_right(left[...], right[...])
    part = outs[0].shape[0]
    for i, out in enumerate(outs):
        out[...] = total[i * part : (i + 1) * part].astype(jnp.bfloat16)


def rows_product(left, right, part, ties=()):
    rows, columns = left.shape
    model_width = right.shape[0]
    tile = 512
    return pl.pallas_call(
        rows_product_kernel,
        grid=(model_width // tile,),
        in_specs=[
            pl.BlockSpec(left.shape, lambda i: (0, 0)),
            pl.BlockSpec((tile, columns), lambda i: (i, 0)),
        ]
        + loose(ties),
        out_specs=[pl.BlockSpec((part, tile), lambda i: (0, i))] * (rows // part),
        out_shape=[jax.ShapeDtypeStruct((part, model_width), jnp.bfloat16)] * (rows // part),
        compiler_params=pltpu.CompilerParams(vmem_limit_bytes=VMEM_LIMIT),
        cost_estimate=pl.CostEstimate(
            flops=2 * rows * right.size, bytes_accessed=2 * right.size, transcendentals=0
        ),
    )(left, right, *ties)


def shards(
    dp_size,
    tokens,
    seq_lengths,
    first_gain,
    query_weight,
    key_matrix,
    value_matrix,
    query_norm_gain,
    key_gain,
    output_weight,
    second_gain,
    gate_weight,
    up_weight,
    down_weight,
    cotangent,
):
    ring = Ring(dp_size)
    steps = ring.steps
    rows, model_width = tokens.shape
    width = query_weight.shape[0]
    key_heads = key_matrix.shape[1] // HEAD_SIZE
    query_columns, key_columns = query_weight.shape[1], key_matrix.shape[1]
    part = rows // PARTS
    tiled = width % LANES == 0
    turned = functools.partial(arrange, steps=steps, width=width)
    turn = turned if tiled else (lambda value: value)
    if not tiled:
        tokens, cotangent = turned(tokens), turned(cotangent)

    hidden_width = gate_weight.shape[1] // 2
    chunk = hidden_width // CHUNKS
    pieces = [ring.pick(w, 1) for w in (gate_weight, up_weight, down_weight.T)]
    feed_mine, feed_other = (
        [
            jnp.concatenate([p[k][:, j * chunk : (j + 1) * chunk] for p in pieces], axis=1)
            for j in range(CHUNKS)
        ]
        for k in range(2)
    )
    feed_full = [None] * CHUNKS

    def feed_gather(j, got):
        block = ring.ordered(feed_mine[j], got, 0)
        feed_full[j] = lax.all_gather(
            block, "dp", axis=0, tiled=True, axis_index_groups=ring.groups
        )

    attention = Gather(ring, jnp.concatenate([query_weight, key_matrix, value_matrix], axis=1))
    output = Gather(ring, output_weight.T)

    live_rows, segment, position = layout(seq_lengths[0], rows)
    cosine_table, sinusoid_table = rotation(position, HEAD_SIZE)
    gain_one = arrange_vector(first_gain.astype(jnp.float32), steps)[None]
    gain_two = arrange_vector(second_gain.astype(jnp.float32), steps)[None]
    tables = (
        jnp.concatenate([cosine_table[:, 0], cosine_table[:, 0]], axis=1),
        jnp.concatenate([-sinusoid_table[:, 0], sinusoid_table[:, 0]], axis=1),
    )
    head_gains = (
        query_norm_gain.astype(jnp.float32)[None],
        key_gain.astype(jnp.float32)[None],
    )
    stages = Stages(jnp.broadcast_to(gain_one[:, :LANES], (8, LANES)) + 0.0)
    settle, step = stages.settle, stages.step
    token_rows, upstream, input_one = row_call(
        functools.partial(first_kernel, turn),
        rows,
        128,
        [
            (tokens, "rows"),
            (cotangent, "rows"),
            (live_rows[:, None].astype(jnp.float32), "rows"),
            (gain_one, "all"),
        ],
        [(model_width, jnp.bfloat16)] * 3,
    )
    for i in range(steps):
        movers = [attention]
        if i != 2:
            movers.append((output, dict(swap=int(i > 2))))
        others = []
        if i in (1, 2):
            others.append(ring.swap_side(*stages.hold(feed_other[i - 1])))
        if i == 0:
            others = [token_rows, upstream, input_one, tables]
        others = step(movers, *others)
        if i == 0:
            token_rows, upstream, input_one, tables = others
        if i in (1, 2):
            feed_gather(i - 1, others[0])
    step([attention])
    place = lax.axis_index("tensor")
    sent = [
        lax.dynamic_slice_in_dim(upstream, place * (rows // 2) + k * part, part) for k in range(2)
    ]

    raw, attention_full = step([(output, dict(swap=2))], *join_call(attention, input_one))
    half = rows // 2
    attend_args = (raw, query_columns, key_columns, head_gains, tables, segment)
    mixed, row_total = attention_call(*attend_args, (0, half), ties=stages.ties)
    while not output.done:
        (mixed,) = step([output], mixed)
    mixture_low, row_totals = [mixed], [row_total]
    output_full, *branch_parts = join_wide_call(output, mixed, part)
    (late,) = stages.hold(feed_other[2:])

    middle_parts, normed_parts, normed_other = [], [], []
    got = None
    for i in range(PARTS + 1):
        work = []
        if i:
            work = row_call(
                middle_kernel,
                part,
                part,
                [
                    (token_rows, i - 1),
                    (branch_parts[i - 1], "rows"),
                    (got, "rows"),
                    (gain_two, "all"),
                ],
                [(model_width, jnp.float32), (model_width, jnp.bfloat16)],
            )
        if i < PARTS:
            moves = [swap_tensor(branch_parts[i])]
            if i < 2:
                moves.append(ring.swap_side(stages.hold(sent[i])[0]))
            else:
                moves.append(ring.swap_side(normed_parts[i - 2]))
            extra = []
            if i == 0:
                mixed, row_total = attention_call(*attend_args, (half, rows), ties=stages.ties)
                mixture_low.append(mixed)
                row_totals.append(row_total)
                extra = [mixed, [ring.swap_side(w) for w in late]]
            if i == 2:
                extra = [input_one.T]
            if i == 1:
                extra = rows_product(mixture_low[1], output_full, part, stages.ties)
            moves, work, extra = settle(moves, work, extra)
            got = moves[0]
            if i == 0:
                mixture_low[1], extra = extra
                for j, value in enumerate(extra):
                    feed_gather(2 + j, value)
            if i == 1:
                branch_parts += extra
            if i == 2:
                (flipped,) = extra
            if i < 2:
                sent[i] = moves[1]
            else:
                normed_other.append(moves[1])
        if i:
            middle_parts.append(work[0])
            normed_parts.append(work[1])
    got = [swap_tensor(v) for v in stages.hold(*sent)]

    span, out_span = (0, 2 * chunk), (2 * chunk, 3 * chunk)
    rest = [ring.swap_side(p) for p in normed_parts[len(normed_other) :]]
    acts = []
    for j in range(CHUNKS - 1):
        act, rest[j : j + 1], there = settle(
            feed_call(normed_parts, upstream, feed_full[j], stages.ties),
            rest[j : j + 1],
            got if j == CHUNKS - 2 else [],
        )
        acts.append(act)
    got = there
    rest, upstream_other = settle(
        rest, [jnp.where(place == 0, a, b) for a, b in zip(sent + got, got + sent)]
    )
    normed_other += rest
    sides = (normed_parts, normed_other), (upstream, upstream_other)
    acts_other = [feed_call(normed_other, upstream_other, feed_full[0], stages.ties)]
    feed_grads = [grad_call(*sides, (acts[0], acts_other[0]))]
    last_grads = None
    for j in range(1, CHUNKS - 1):
        acts_other.append(
            feed_call(normed_other, upstream_other, feed_full[j], (feed_grads + acts_other[1:])[-1:])
        )
    (early,) = wide_call(acts_other, feed_full[:-1], span, jnp.float32, parts=1)
    acts_other.append(feed_call(normed_other, upstream_other, feed_full[-1], (early,)))
    back_other = wide_call(acts_other[-1:], feed_full[-1:], span, jnp.bfloat16, early)
    (acts_last,) = settle(
        feed_call(normed_parts, upstream, feed_full[-1], tuple(back_other[:1]))
    )
    acts.append(acts_last)
    back_other = [back_other[0], *stages.hold(*back_other[1:])]

    back_mine = wide_call(acts, feed_full, span, jnp.float32, ties=stages.ties)
    got, back_mine = settle(ring.swap_side(back_other[0]), back_mine)
    mine = add_low(back_mine[0], got)
    back_parts, low_parts, mixed_parts, grad_second = [], [], [], 0.0
    out_other, out_mine, out_sums, out_got = None, None, [], []

    def back_middle_call(k, mine, other):
        return row_call(
            back_middle_kernel,
            2 * part,
            part,
            [
                (mine, "parts"),
                (other, "parts"),
                (middle_parts[2 * k : 2 * k + 2], "parts"),
                (upstream, 2 * k),
                (gain_two, "all"),
                (output_full, "all"),
            ],
            [
                (model_width, jnp.float32),
                (model_width, jnp.bfloat16),
                (query_columns, jnp.bfloat16),
            ],
            [model_width],
            stages.ties,
        )

    sums, sums_got = [], []
    for i in range(PARTS):
        work = []
        if i + 1 < CHUNKS:
            last_grads = grad_call(
                *sides,
                (acts[i + 1], acts_other[i + 1]),
                (mine,) + stages.ties,
                i,
                CHUNKS - 1,
                last_grads,
            )
            work = [last_grads]
        if i == PARTS - 2:
            work = [
                wide_call(acts_other, feed_full, out_span, jnp.bfloat16, ties=(mine,), parts=2)
            ]
        if i == PARTS - 1:
            work = [wide_call(acts, feed_full, out_span, jnp.float32, ties=(mine,), parts=2)]
        done = back_middle_call(0, sums, sums_got) if i == 2 else []
        moves = [swap_tensor(mine)]
        if i + 1 < PARTS:
            moves.append(ring.swap_side(back_other[i + 1]))
        moves, work, done = settle(moves, work, done)
        back_other[i + 2 :] = stages.hold(*back_other[i + 2 :])
        sums.append(mine)
        sums_got.append(moves[0])
        if i + 1 < PARTS:
            mine = add_low(back_mine[i + 1], moves[1])
        if i + 1 < CHUNKS:
            last_grads = work[0]
        if i == PARTS - 2:
            out_other = list(work[0])
        if i == PARTS - 1:
            out_mine = work[0]
        if i == 2:
            back_parts.append(done[0])
            low_parts.append(done[1])
            mixed_parts.append(done[2])
            grad_second = grad_second + done[3]
    done = back_middle_call(1, sums[2:], sums_got[2:])
    back_parts.append(done[0])
    low_parts.append(done[1])
    mixed_parts.append(done[2])
    grad_second = grad_second + done[3]
    feed_grads.append(last_grads)

    scattered = [
        lax.psum_scatter(
            grad, "dp", scatter_dimension=0, tiled=True, axis_index_groups=ring.groups
        )
        for grad in feed_grads
    ]

    core = ring.core
    far = scatter_call(
        ring, width, low_parts, mixture_low, 1 - core, ties=stages.ties, apart=False
    )
    (got,) = settle(ring.swap_side(out_other[0]))
    (held,) = stages.hold(out_other[1])
    out_sums = [add_low(out_mine[0], got)]

    def picked(total):
        return lax.dynamic_slice_in_dim(total, (1 - ring.side) * width, width)

    work, scattered[0], far, got, out_next = settle(
        attention_call(
            *attend_args,
            (0, rows),
            mixed_parts,
            jnp.concatenate(row_totals, axis=1),
            stages.ties + (far[0][0],),
        ),
        scattered[0],
        [ring.swap_core(f[0]) for f in far],
        ring.swap_side(held),
        swap_tensor(out_sums[0]),
    )
    raw_grad, grad_qgain, grad_kgain = work
    out_sums.append(add_low(out_mine[1], got))
    out_done = [out_next]
    far_one = scatter_call(
        ring, width, [flipped], [raw_grad], 1 - core, ties=stages.ties, apart=False, flipped=True
    )
    (near,), across = scatter_call(
        ring,
        width,
        low_parts,
        mixture_low,
        core,
        far,
        stages.ties + (far_one[0][0],),
        apart=False,
    )
    far_one, near, pair = settle(
        [ring.swap_core(f[0]) for f in far_one],
        near,
        ring.swap_side(*stages.hold(picked(scattered[0]))),
    )
    pairs_got = [pair]
    ((mine, other),) = settle(
        scatter_call(
            ring, width, [flipped], [raw_grad], core, far_one, stages.ties, flipped=True
        )
    )
    *back_one, grad_first = back_first_call(raw_grad, attention_full, token_rows, stages.ties)
    gains = jnp.concatenate(
        [
            arrange_vector(grad_first[0], steps),
            arrange_vector(grad_second[0], steps) * 0.5,
            grad_qgain[0],
            grad_kgain[0],
        ]
    )
    back_one_other = []
    distances = [1] + [4 * 2**k for k in range((steps - 1).bit_length())] + [2]

    def gains_sum(value, chosen):
        for distance in chosen:
            value = value + lax.ppermute(
                value, "dp", [(k, k ^ distance) for k in range(dp_size)]
            )
        return value

    def token_call(first, last, into, ties):
        ins = [
            (back_one[first:last], "parts"),
            (back_one_other[first:last], "parts"),
            (token_rows, first),
            (back_parts, "halves"),
            (gain_one, "all"),
        ]
        return row_call(
            functools.partial(token_kernel, turn),
            (last - first) * part,
            part,
            ins,
            [(model_width, jnp.float32)],
            ties=ties,
            into=(into, first, rows),
        )[0]

    token_grad = block_output = None
    sizes = (width, raw_grad.shape[1]), (width, query_columns)
    joined_columns = sizes[0][1] + sizes[1][1]
    sent = None
    for i in range(steps):
        moves = [ring.swap_side(*stages.hold(other[i]))]
        if i == 0:
            moves.append(ring.swap_side(across[0]))
        else:
            moves.append(ring.shift(sent, 1))
        others = []
        turns = {0: [0], 1: [1, 2], 2: [3]}.get(i, [])
        others.append([swap_tensor(back_one[k]) for k in turns])
        k = i - (steps - CHUNKS)
        if 0 <= k < CHUNKS - 1:
            last_pair = picked(scattered[1])[:, k * 3 * chunk : (k + 1) * 3 * chunk]
            others.append(ring.swap_side(*stages.hold(last_pair)))
        if i == 1:
            (block_output,) = row_call(
                functools.partial(output_kernel, turn),
                rows,
                128,
                [(middle_parts, "parts"), (out_sums, "halves"), (out_done, "halves")],
                [(model_width, jnp.bfloat16)],
                ties=stages.ties,
            )
            others.append(block_output)
        if i == steps - 1:
            token_grad = token_call(0, PARTS, None, stages.ties)
            others.append(token_grad)
            others.append(finish_call(ring, chunk, scattered, pairs_got))
        if i == 0:
            others.append(swap_tensor(out_sums[1]))
        if i in (0, 2):
            others.append(gains_sum(gains, distances[:-1] if i == 0 else distances[-1:]))
        if i == steps - 1:
            others.append(gains + swap_tensor(gains))
        moves, others = settle(moves, others)
        others = list(others)
        side, hop = moves
        if i == 0:
            across, group, late = hop, [mine[0], side], [(near, (0, 0)), (hop, (0, 0), sizes[1])]
        else:
            group = [mine[i], (hop, (0, 0)), side]
            late = [
                (near, (i, 0)),
                (across, (i, 0)),
                (hop, (0, sizes[0][1] // sizes[1][1]), sizes[1]),
            ]
        if i < steps - 1:
            (sent,) = sums_call(
                (("open", joined_columns), group), (("close", sizes[0][1]), late)
            )
        else:
            grad_query, grad_key, grad_value, grad_output = sums_call(
                ((query_columns, key_columns, key_columns), group), ("turned", late)
            )
        if i in (0, 2, steps - 1):
            gains = others.pop()
        if i == 0:
            out_done.append(others.pop())
        if i == steps - 1:
            grads = others.pop()
            token_grad = others.pop()
        if i == 1:
            block_output = others.pop()
        if 0 <= k < CHUNKS - 1:
            pairs_got.append(others.pop())
        back_one_other += others.pop()
    if not tiled:
        token_grad, block_output = turned(token_grad), turned(block_output)
    grad_gate, grad_up, grad_down = grads

    index = lax.axis_index("dp")

    def own_part(start, size):
        return lax.dynamic_slice_in_dim(gains, start + index * (size // dp_size), size // dp_size)

    return (
        block_output,
        token_grad,
        own_part(0, model_width),
        grad_query,
        grad_key,
        grad_value,
        own_part(2 * model_width, HEAD_SIZE),
        own_part(2 * model_width + HEAD_SIZE, HEAD_SIZE),
        grad_output,
        own_part(model_width, model_width),
        grad_gate,
        grad_up,
        grad_down,
    )


def solution(mesh):
    return jax.shard_map(
        functools.partial(shards, mesh.shape["dp"]),
        mesh=mesh,
        in_specs=(
            P("dp", None),
            P("dp", None),
            P(),
            P("dp", "tensor"),
            P("dp", "tensor"),
            P("dp", "tensor"),
            P(),
            P(),
            P("tensor", "dp"),
            P(),
            P("dp", "tensor"),
            P("dp", "tensor"),
            P("tensor", "dp"),
            P("dp", None),
        ),
        out_specs=(
            P("dp", None),
            P("dp", None),
            P("dp"),
            P("dp", "tensor"),
            P("dp", "tensor"),
            P("dp", "tensor"),
            P("dp"),
            P("dp"),
            P("tensor", "dp"),
            P("dp"),
            P("dp", "tensor"),
            P("dp", "tensor"),
            P("tensor", "dp"),
        ),
        check_vma=False,
    )
```
